32 devices in a mesh: silo: 16 (over z, y, core), shard: 2 (over x).
Axes of the slice: x: 2, y: 2, z: 4, core: 2. Of those that a mesh axis runs over, the one named last changes fastest.
Arguments:
- activ: bfloat16 [32768, 1280], P(('silo', 'shard')), may hold values from -6 to 6
- cotangent: bfloat16 [32768, 640], P(('silo', 'shard')), may hold values from -6 to 6
- error_memory: float32 [16, 2, 3200, 256], P('silo', 'shard'), may hold values from -5 to 5
- params: float32 [16, 640, 1280], P('silo', 'shard'), may hold values from -6 to 6
- estimate: float32 [16, 640, 1280], P('silo', 'shard'), may hold values from -6 to 6
- mixed: float32 [16, 640, 1280], P('silo', 'shard'), may hold values from -6 to 6
- kept_blocks: int32 [16, 2, 2, 64], P('silo'), may hold values from 0 to 1599, as said below
- kept_counts: int32 [16, 2, 2], P('silo'), may hold values from 1 to 64, as said below
- gossip_blocks: int32 [16, 2, 128], P(None, 'shard'), may hold values from 0 to 1599, as said below
- gossip_counts: int32 [16, 2], P(None, 'shard'), may hold values from 1 to 128, as said below
Outputs:
- params_out: float32 [16, 640, 1280], P('silo', 'shard')
- estimate_out: float32 [16, 640, 1280], P('silo', 'shard')
- mixed_out: float32 [16, 640, 1280], P('silo', 'shard')
- error_out: float32 [16, 2, 3200, 256], P('silo', 'shard')
The draws below stay inside these ranges and needn't reach their ends.
Inputs may be any that keep to these rules, and one draw needn't show every extreme that they name: `kept_blocks`: for each silo, sender and owner the 64 entries are distinct. In every silo some owner has kept_counts equal to 64 from every sender. `kept_counts`: in every silo one owner receives 64 from every device of the silo. `gossip_blocks`: for each silo and owner the 128 entries are distinct. `gossip_counts`: for every owner some silo gossips 128 blocks.
All inputs are finite; a program needn't handle non-finite values.
Results may differ from the reference program's by a relative error of at most 0.0003.
Values sent between devices are 32-bit elements; how exact they have to be, the bound alone decides.
No kernel may reach another device: no remote copies, remote signals or barrier semaphores. Data moves between devices by JAX's collectives and lax.ppermute only.
A program may use at most 64 MiB of HBM per device.

```python
import jax
import jax.numpy as jnp
from jax import lax

C_IN = 1280
C_OUT = 640
BLK = 256
TOK_DEV = 1024
CAP = 64
GK = 128
SILOS = 16
SHARDS = 2
NB = 3200
BLK_OWN = 1600
ROWS = 32768


def distinct_lists(key, groups, length):
    keys = jax.random.split(key, groups)
    rows = jax.vmap(lambda one_key: jax.random.permutation(one_key, BLK_OWN)[:length])(keys)
    return rows.astype(jnp.int32)


def draw_kept_blocks(key, part):
    rows = distinct_lists(jax.random.fold_in(key, 11), SILOS * SHARDS * SHARDS, CAP)
    return rows.reshape(SILOS, SHARDS, SHARDS, CAP)


def draw_kept_counts(key, part):
    key_heat, key_base, key_full = jax.random.split(jax.random.fold_in(key, 23), 3)
    heat = jax.random.randint(key_heat, (SILOS, 1, SHARDS), 1, 5)
    base = jax.random.randint(key_base, (SILOS, SHARDS, SHARDS), 0, CAP)
    counts = jnp.clip(base * heat // 2 + 1, 1, CAP)
    hottest = jax.random.randint(key_full, (SILOS,), 0, SHARDS)
    full_owner = jnp.arange(SHARDS)[None, None, :] == hottest[:, None, None]
    return jnp.where(full_owner, CAP, counts).astype(jnp.int32)


def draw_gossip_blocks(key, part):
    rows = distinct_lists(jax.random.fold_in(key, 37), SILOS * SHARDS, GK)
    return rows.reshape(SILOS, SHARDS, GK)


def draw_gossip_counts(key, part):
    key_base, key_full = jax.random.split(jax.random.fold_in(key, 41), 2)
    counts = jax.random.randint(key_base, (SILOS, SHARDS), 1, GK + 1)
    fullest = jax.random.randint(key_full, (SHARDS,), 0, SILOS)
    full_silo = jnp.arange(SILOS)[:, None] == fullest[None, :]
    return jnp.where(full_silo, GK, counts).astype(jnp.int32)


def levels(own_key, dims, cuts, low, largest):
    level = 1.0
    for position, shards_of in cuts:
        draws = jax.random.uniform(jax.random.fold_in(jax.random.fold_in(own_key, 6), position), (shards_of,), jnp.float32, low / len(cuts), largest / len(cuts))
        level = level * jnp.repeat(jnp.exp(draws), dims[position] // shards_of).reshape((-1,) + (1,) * (len(dims) - 1 - position))
    return level


def scatter_about(key, extent, scale, reach, shards=(), held_as=jnp.bfloat16):
    loudness = levels(key, extent, shards, -0.22, 0.18) if shards else 1.0
    values = jax.random.normal(key, extent, jnp.float32) * scale * loudness
    return jnp.minimum(jnp.maximum(values, -reach), reach).astype(held_as)


def setup_inputs(seed: int = 0) -> dict:
    splits = jax.random.split(jax.random.key(seed), 11)
    activ = scatter_about(splits[0], (ROWS, C_IN), 1.0, 6.0, ((0, 32),))
    cotangent = scatter_about(splits[1], (ROWS, C_OUT), 1.0, 6.0, ((0, 32),))
    error_memory = scatter_about(splits[2], (SILOS, SHARDS, NB, BLK), 0.7, 5.0, ((0, 16), (1, 2)), jnp.float32)
    params = scatter_about(splits[3], (SILOS, C_OUT, C_IN), 1.0, 6.0, ((0, 16), (1, 2)), jnp.float32)
    estimate = scatter_about(splits[4], (SILOS, C_OUT, C_IN), 1.0, 6.0, ((0, 16), (1, 2)), jnp.float32)
    mixed = scatter_about(splits[5], (SILOS, C_OUT, C_IN), 1.0, 6.0, ((0, 16), (1, 2)), jnp.float32)
    kept_blocks = draw_kept_blocks(jax.random.fold_in(splits[10], 71), 0)
    kept_counts = draw_kept_counts(jax.random.fold_in(splits[10], 71), 0)
    gossip_blocks = draw_gossip_blocks(jax.random.fold_in(splits[10], 71), 0)
    gossip_counts = draw_gossip_counts(jax.random.fold_in(splits[10], 71), 0)
    return {"activ": activ, "cotangent": cotangent, "error_memory": error_memory, "params": params, "estimate": estimate, "mixed": mixed, "kept_blocks": kept_blocks, "kept_counts": kept_counts, "gossip_blocks": gossip_blocks, "gossip_counts": gossip_counts}


LEARN_RATE = 0.25
CONSENSUS = 0.5
MIX_WEIGHT = 1.0 / 3.0


def reference(activ, cotangent, error_memory, params, estimate, mixed, kept_blocks, kept_counts, gossip_blocks, gossip_counts):
    scale_in = C_IN ** -0.5
    acts = activ.reshape(SILOS, SHARDS, TOK_DEV, C_IN)
    cots = cotangent.reshape(SILOS, SHARDS, TOK_DEV, C_OUT)
    offsets = (jnp.arange(SHARDS, dtype=jnp.int32) * BLK_OWN)[:, None]
    slot_ids = jnp.arange(CAP, dtype=jnp.int32)[None, :]
    gossip_slot_ids = jnp.arange(GK, dtype=jnp.int32)[None, :]

    def one_device(inputs):
        act_rows, cot_rows, memory, my_lists, my_counts = inputs
        grad_local = jnp.dot(cot_rows.T, act_rows, preferred_element_type=jnp.float32) * scale_in
        pending = memory + grad_local.reshape(NB, BLK)
        global_ids = (my_lists + offsets).reshape(-1)
        filled = (slot_ids < my_counts[:, None]).astype(jnp.int32).reshape(-1)
        chosen = jnp.zeros((NB,), jnp.int32).at[global_ids].max(filled)
        keep_mask = chosen[:, None] > 0
        return jnp.where(keep_mask, jnp.float32(0.0), pending), jnp.where(keep_mask, pending, jnp.float32(0.0))

    def one_silo(inputs):
        act_silo, cot_silo, memory_silo, lists_silo, counts_silo, weights_silo, estimate_silo, gossip_silo, gcounts_silo = inputs
        error_part, kept_terms = lax.map(one_device, (act_silo, cot_silo, memory_silo, lists_silo, counts_silo))
        summed = jnp.sum(kept_terms, axis=0)
        half_step = weights_silo.reshape(NB, BLK) - LEARN_RATE * summed
        drift = half_step - estimate_silo.reshape(NB, BLK)
        gossip_ids = (gossip_silo + offsets).reshape(-1)
        gossip_filled = (gossip_slot_ids < gcounts_silo[:, None]).astype(jnp.int32).reshape(-1)
        gossip_chosen = jnp.zeros((NB,), jnp.int32).at[gossip_ids].max(gossip_filled)
        delta = jnp.where(gossip_chosen[:, None] > 0, drift, jnp.float32(0.0))
        return error_part, half_step, delta

    error_out, half_step, delta = lax.map(one_silo, (acts, cots, error_memory, kept_blocks, kept_counts, params, estimate, gossip_blocks, gossip_counts))
    estimate_out = estimate + delta.reshape(estimate.shape)
    spread = delta + jnp.roll(delta, 1, axis=0) + jnp.roll(delta, -1, axis=0)
    mixed_out = mixed + MIX_WEIGHT * spread.reshape(mixed.shape)
    params_out = half_step.reshape(params.shape) + CONSENSUS * (mixed_out - estimate_out)
    return params_out, estimate_out, mixed_out, error_out
```

```python
import functools

import jax
import jax.numpy as jnp
from jax import lax
from jax.experimental import pallas as pl
from jax.experimental.pallas import tpu as pltpu
from jax.sharding import PartitionSpec as P

LEARN_RATE = 0.25
CONSENSUS = 0.5
MIX_WEIGHT = 1.0 / 3.0

F32, BF16, I32 = jnp.float32, jnp.bfloat16, jnp.int32
ANY = pl.BlockSpec(memory_space=pl.ANY)
IN_VMEM = pl.BlockSpec(memory_space=pltpu.VMEM)
MIB = 1 << 20


def dot(a, b, dims=((1,), (0,))):
    return lax.dot_general(a, b, (dims, ((), ())), preferred_element_type=F32)


def as_column(row):
    n = row.shape[1]
    eye = lax.broadcasted_iota(I32, (n, n), 0) == lax.broadcasted_iota(I32, (n, n), 1)
    spread = jnp.where(eye, jnp.broadcast_to(row.astype(F32), (n, n)), 0.0)
    return jnp.sum(spread, axis=1, keepdims=True).astype(I32)


def thirds(rows):
    high = rows.astype(BF16)
    rest = rows - high.astype(F32)
    middle = rest.astype(BF16)
    low = (rest - middle.astype(F32)).astype(BF16)
    return high, middle, low


def pick(choice, parts):
    high, middle, low = parts
    return dot(choice, high) + (dot(choice, middle) + dot(choice, low))


def onehot(mask):
    return jnp.where(mask, 1.0, 0.0).astype(BF16)


def divide(value, by):
    return (value * ((1 << 16) // by + 1)) >> 16


def select_kernel(shards, own_blocks, per_row, scale, lists, counts, act, cot, err, *refs):
    outs, (list_s, count_s, list_v, count_v, act_v, cot_v, err_v, sems) = refs[:shards], refs[shards:]
    me = lax.axis_index("shard")
    slots = list_v.shape[1]
    tokens = act_v.shape[0]
    parts = 4
    step = tokens // parts
    small = [
        pltpu.make_async_copy(lists.at[0, me], list_s, sems.at[0]),
        pltpu.make_async_copy(lists.at[0, me], list_v, sems.at[1]),
        pltpu.make_async_copy(counts.at[0], count_s, sems.at[2]),
    ]
    for copy in small:
        copy.start()
    big = []
    for part in range(parts):
        rows = pl.ds(part * step, step)
        pair = [
            pltpu.make_async_copy(cot.at[rows], cot_v.at[rows], sems.at[4 + 2 * part]),
            pltpu.make_async_copy(act.at[rows], act_v.at[rows], sems.at[5 + 2 * part]),
        ]
        for copy in pair:
            copy.start()
        big.append(pair)
    for copy in small:
        copy.wait()

    for shift in range(shards):
        owner = lax.rem(me + shift, shards)

        def fetch(slot, carry, owner=owner, shift=shift):
            block = owner * own_blocks + list_s[owner, slot]
            pltpu.make_async_copy(
                err.at[0, 0, pl.ds(block, 1)], err_v.at[pl.ds(shift * slots + slot, 1)], sems.at[3]
            ).start()
            return carry

        lax.fori_loop(0, slots, fetch, 0, unroll=8)

    columns, fills = [], []
    width_out = cot_v.shape[1]
    for shift in range(shards):
        owner = lax.rem(me + shift, shards)
        row = list_v[pl.ds(owner, 1), :] + owner * own_blocks
        columns.append(as_column(row))
        slot_ids = lax.broadcasted_iota(I32, (slots, 1), 0)
        fills.append(slot_ids < count_s[me, owner])
    blocks = jnp.concatenate(columns, axis=0)
    filled = jnp.concatenate(fills, axis=0)
    out_row = divide(blocks, per_row)
    segment = blocks - out_row * per_row
    total = blocks.shape[0]
    chosen = onehot(lax.broadcasted_iota(I32, (total, width_out), 1) == out_row)
    acc = jnp.zeros((total, act_v.shape[1]), F32)
    for part in range(parts):
        for copy in big[part]:
            copy.wait()
        rows = pl.ds(part * step, step)
        picked = dot(chosen, cot_v[rows, :], ((1,), (1,))).astype(BF16)
        acc = acc + dot(picked, act_v[rows, :])
    width = act_v.shape[1] // per_row
    grad = jnp.zeros((total, width), F32)
    for part in range(per_row):
        grad = jnp.where(segment == part, acc[:, part * width : (part + 1) * width], grad)
    pltpu.make_async_copy(err.at[0, 0, pl.ds(0, total)], err_v, sems.at[3]).wait()
    pending = jnp.where(filled, err_v[...] + grad * scale, 0.0)
    for shift in range(shards):
        outs[shift][...] = pending[shift * slots : (shift + 1) * slots]


def select(shards, own_blocks, per_row, scale, lists, counts, act, cot, err):
    slots = lists.shape[3]
    width = err.shape[3]
    return pl.pallas_call(
        functools.partial(select_kernel, shards, own_blocks, per_row, scale),
        name="kept_rows",
        in_specs=[ANY] * 5,
        out_specs=[IN_VMEM] * shards,
        out_shape=[jax.ShapeDtypeStruct((slots, width), F32)] * shards,
        scratch_shapes=[
            pltpu.SMEM((shards, slots), I32),
            pltpu.SMEM((shards, shards), I32),
            pltpu.VMEM((shards, slots), I32),
            pltpu.VMEM((8, 128), I32),
            pltpu.VMEM(act.shape, BF16),
            pltpu.VMEM(cot.shape, BF16),
            pltpu.VMEM((shards * slots, width), F32),
            pltpu.SemaphoreType.DMA((12,)),
        ],
        compiler_params=pltpu.CompilerParams(vmem_limit_bytes=16 * MIB),
    )(lists, counts, act, cot, err)


def base_kernel(
    shards, silos, per_row, lists, g_lists, g_counts, params, estimate, mine, base, match, *scratch
):
    list_v, g_s, g_v, gc_s, p_v, e_v, sems = scratch
    me = lax.axis_index("shard")
    silo = lax.axis_index("silo")
    slots = list_v.shape[2]
    g_slots = g_v.shape[1]
    width = p_v.shape[1]
    small = [
        pltpu.make_async_copy(g_lists.at[silo], g_s, sems.at[0]),
        pltpu.make_async_copy(g_lists.at[silo], g_v, sems.at[1]),
        pltpu.make_async_copy(g_counts, gc_s, sems.at[2]),
        pltpu.make_async_copy(lists.at[0], list_v, sems.at[3]),
    ]
    for copy in small:
        copy.start()
    for copy in small:
        copy.wait()

    def fetch(slot, carry):
        block = g_s[0, slot]
        row = divide(block, per_row)
        column = pl.multiple_of((block - row * per_row) * width, width)
        where = (0, pl.ds(row, 1), pl.ds(column, width))
        into = pl.ds(slot, 1)
        pltpu.make_async_copy(params.at[where], p_v.at[into], sems.at[4]).start()
        pltpu.make_async_copy(estimate.at[where], e_v.at[into], sems.at[5]).start()
        return carry

    lax.fori_loop(0, g_slots, fetch, 0, unroll=8)
    blocks = as_column(g_v[...])
    slot_ids = lax.broadcasted_iota(I32, (g_slots, 1), 0)
    filled = slot_ids < gc_s[silo, 0]
    for shift in range(shards):
        sender = lax.rem(me - shift + shards, shards)
        kept = list_v[sender, pl.ds(me, 1), :]
        same = onehot((blocks == kept) & filled)
        if shift == 0:
            own = pick(same, thirds(mine[...]))
        else:
            match[:, (shift - 1) * slots : shift * slots] = same
    pltpu.make_async_copy(p_v, p_v, sems.at[4]).wait()
    pltpu.make_async_copy(e_v, e_v, sems.at[5]).wait()
    base[...] = jnp.where(filled, p_v[...] - e_v[...], 0.0) - LEARN_RATE * own


def base_rows(shards, silos, per_row, lists, g_lists, g_counts, params, estimate, mine):
    slots, width = mine.shape
    g_slots = g_lists.shape[2]
    return pl.pallas_call(
        functools.partial(base_kernel, shards, silos, per_row),
        name="gossip_base",
        in_specs=[ANY] * 5 + [IN_VMEM],
        out_specs=[IN_VMEM] * 2,
        out_shape=[
            jax.ShapeDtypeStruct((g_slots, width), F32),
            jax.ShapeDtypeStruct((g_slots, (shards - 1) * slots), BF16),
        ],
        scratch_shapes=[
            pltpu.VMEM((shards, shards, slots), I32),
            pltpu.SMEM((1, g_slots), I32),
            pltpu.VMEM((1, g_slots), I32),
            pltpu.SMEM(g_counts.shape, I32),
            pltpu.VMEM((g_slots, width), F32),
            pltpu.VMEM((g_slots, width), F32),
            pltpu.SemaphoreType.DMA((6,)),
        ],
        compiler_params=pltpu.CompilerParams(vmem_limit_bytes=8 * MIB),
    )(lists, g_lists, g_counts, params, estimate, mine)


def delta_kernel(base, match, *refs):
    *arrived, out = refs
    slots = arrived[0].shape[0]
    total = base[...]
    for place, rows in enumerate(arrived):
        same = match[:, place * slots : (place + 1) * slots]
        total = total - LEARN_RATE * pick(same, thirds(rows[...]))
    out[...] = total


def delta_rows(base, match, arrived):
    return pl.pallas_call(
        delta_kernel,
        name="delta_rows",
        in_specs=[IN_VMEM] * (2 + len(arrived)),
        out_specs=IN_VMEM,
        out_shape=jax.ShapeDtypeStruct(base.shape, F32),
        compiler_params=pltpu.CompilerParams(vmem_limit_bytes=8 * MIB),
    )(base, match, *arrived)


def dense_kernel(
    shards, silos, own_blocks, per_row, scale,
    lists, counts, g_lists, g_counts, act, cot, err, params, estimate, mixed, delta, *refs
):
    kept = refs[:shards]
    (err_out, est_out, mixed_pre, params_pre, spread,
     list_s, count_s, list_v, g_v, act_v, cot_v, err_v, p_v, e_v, m_v, sems) = refs[shards:]
    me = lax.axis_index("shard")
    silo = lax.axis_index("silo")
    slots = list_v.shape[2]
    g_slots = g_v.shape[2]
    width = delta.shape[1]
    width_out = cot_v.shape[1]
    out_rows = p_v.shape[0]
    small = [
        pltpu.make_async_copy(lists.at[0, me], list_s, sems.at[0]),
        pltpu.make_async_copy(lists.at[0], list_v, sems.at[1]),
        pltpu.make_async_copy(counts.at[0], count_s, sems.at[2]),
        pltpu.make_async_copy(g_lists, g_v, sems.at[3]),
    ]
    owned = [
        pltpu.make_async_copy(params.at[0], p_v, sems.at[4]),
        pltpu.make_async_copy(estimate.at[0], e_v, sems.at[5]),
        pltpu.make_async_copy(mixed.at[0], m_v, sems.at[6]),
    ]
    big = [
        pltpu.make_async_copy(cot, cot_v, sems.at[7]),
        pltpu.make_async_copy(act, act_v, sems.at[8]),
    ]
    halves = range(width // 128)
    for half in halves:
        lanes = pl.ds(half * 128, 128)
        big.append(
            pltpu.make_async_copy(
                err.at[0, 0, :, lanes], err_v.at[half, pl.ds(0, shards * own_blocks)], sems.at[9 + half]
            )
        )
    for copy in small + owned + big:
        copy.start()
    for copy in small + owned:
        copy.wait()

    first, second = neighbours(silo, silos)
    kept_parts = thirds(jnp.concatenate([rows[...] for rows in kept], axis=0))
    kept_ids = jnp.concatenate(
        [list_v[lax.rem(me - shift + shards, shards), pl.ds(me, 1), :] for shift in range(shards)], axis=1
    )
    delta_parts = thirds(delta[...])
    own_ids = g_v[silo]
    next_ids = jnp.concatenate([g_v[first], g_v[second]], axis=1)
    for part in range(per_row):
        lanes = slice(part * width, (part + 1) * width)

        def places(ids):
            here = lax.broadcasted_iota(I32, (out_rows, ids.shape[1]), 0) * per_row + part
            return onehot(here == ids)

        grad = pick(places(kept_ids), kept_parts)
        change = pick(places(own_ids), delta_parts)
        spread[part * out_rows : (part + 1) * out_rows, :] = places(next_ids)
        half = p_v[:, lanes] - LEARN_RATE * grad
        est = e_v[:, lanes] + change
        mix = m_v[:, lanes] + MIX_WEIGHT * change
        e_v[:, lanes] = est
        mixed_pre[:, lanes] = mix
        params_pre[:, lanes] = half + CONSENSUS * (mix - est)
    est_copy = pltpu.make_async_copy(e_v, est_out.at[0], sems.at[4])
    est_copy.start()

    for copy in big:
        copy.wait()
    tile = 128
    for part in range(width_out // tile):
        grad = dot(cot_v[:, part * tile : (part + 1) * tile], act_v[...], ((0,), (0,))) * scale
        for seg in range(per_row):
            where = pl.ds(part * tile * per_row + seg, tile, stride=per_row)
            for half in halves:
                lane = seg * width + half * 128
                err_v[half, where, :] = err_v[half, where, :] + grad[:, lane : lane + 128]

    spare = shards * own_blocks
    for owner in range(shards):
        limit = count_s[me, owner]

        def clear(slot, carry, owner=owner, limit=limit):
            block = jnp.where(slot < limit, owner * own_blocks + list_s[owner, slot], spare)
            for half in halves:
                err_v[half, pl.ds(block, 1), :] = jnp.zeros((1, 128), F32)
            return carry

        lax.fori_loop(0, slots, clear, 0, unroll=8)
    stores = [
        pltpu.make_async_copy(
            err_v.at[half, pl.ds(0, spare)], err_out.at[0, 0, :, pl.ds(half * 128, 128)], sems.at[9 + half]
        )
        for half in halves
    ]
    for copy in stores:
        copy.start()
    for copy in stores:
        copy.wait()
    est_copy.wait()


def dense(shards, silos, own_blocks, per_row, scale, lists, counts, g_lists, g_counts, act, cot, err, params, estimate, mixed, delta, kept):
    slots = lists.shape[3]
    g_slots = g_lists.shape[2]
    width = err.shape[3]
    owned = params.shape[1:]
    return pl.pallas_call(
        functools.partial(dense_kernel, shards, silos, own_blocks, per_row, scale),
        name="dense",
        in_specs=[ANY] * 10 + [IN_VMEM] * (1 + shards),
        out_specs=[ANY, ANY, IN_VMEM, IN_VMEM, IN_VMEM],
        out_shape=[
            jax.ShapeDtypeStruct(err.shape, F32),
            jax.ShapeDtypeStruct(estimate.shape, F32),
            jax.ShapeDtypeStruct(owned, F32),
            jax.ShapeDtypeStruct(owned, F32),
            jax.ShapeDtypeStruct((own_blocks, 2 * g_slots), BF16),
        ],
        scratch_shapes=[
            pltpu.SMEM((shards, slots), I32),
            pltpu.SMEM((shards, shards), I32),
            pltpu.VMEM((shards, shards, slots), I32),
            pltpu.VMEM(g_lists.shape, I32),
            pltpu.VMEM(act.shape, BF16),
            pltpu.VMEM(cot.shape, BF16),
            pltpu.VMEM((width // 128, shards * own_blocks + 8, 128), F32),
            pltpu.VMEM(owned, F32),
            pltpu.VMEM(owned, F32),
            pltpu.VMEM(owned, F32),
            pltpu.SemaphoreType.DMA((9 + width // 128,)),
        ],
        compiler_params=pltpu.CompilerParams(vmem_limit_bytes=32 * MIB),
    )(lists, counts, g_lists, g_counts, act, cot, err, params, estimate, mixed, delta, *kept)


def final_kernel(per_row, mixed_pre, params_pre, spread, first, second, mixed_out, params_out, m_v, p_v, sems):
    out_rows = m_v.shape[0]
    width = m_v.shape[1] // per_row
    parts = thirds(jnp.concatenate([first[...], second[...]], axis=0))
    copies = []
    for part in range(per_row):
        lanes = slice(part * width, (part + 1) * width)
        change = pick(spread[part * out_rows : (part + 1) * out_rows, :], parts)
        m_v[:, lanes] = mixed_pre[:, lanes] + MIX_WEIGHT * change
        p_v[:, lanes] = params_pre[:, lanes] + (CONSENSUS * MIX_WEIGHT) * change
        pair = [
            pltpu.make_async_copy(m_v.at[:, lanes], mixed_out.at[0, :, lanes], sems.at[2 * part]),
            pltpu.make_async_copy(p_v.at[:, lanes], params_out.at[0, :, lanes], sems.at[2 * part + 1]),
        ]
        for copy in pair:
            copy.start()
        copies += pair
    for copy in copies:
        copy.wait()


def final(per_row, shape, mixed_pre, params_pre, spread, first, second):
    return pl.pallas_call(
        functools.partial(final_kernel, per_row),
        name="neighbours",
        in_specs=[IN_VMEM] * 5,
        out_specs=[ANY] * 2,
        out_shape=[jax.ShapeDtypeStruct(shape, F32)] * 2,
        scratch_shapes=[
            pltpu.VMEM(mixed_pre.shape, F32),
            pltpu.VMEM(mixed_pre.shape, F32),
            pltpu.SemaphoreType.DMA((2 * per_row,)),
        ],
        compiler_params=pltpu.CompilerParams(vmem_limit_bytes=20 * MIB),
    )(mixed_pre, params_pre, spread, first, second)


def neighbours(silo, silos):
    lower, upper = lax.rem(silo + silos - 1, silos), lax.rem(silo + 1, silos)
    if silos % 2:
        return lower, upper
    even = lax.rem(silo, 2) == 0
    return jnp.where(even, upper, lower), jnp.where(even, lower, upper)


def exchange(rows, silos):
    if silos % 2:
        routes = [[(a, (a + 1) % silos) for a in range(silos)], [(a, (a - 1) % silos) for a in range(silos)]]
    else:
        routes = [
            [(a, a ^ 1) for a in range(silos)],
            [(a, (a + 1 if a % 2 else a - 1) % silos) for a in range(silos)],
        ]
    far = lax.ppermute(rows, "silo", routes[1])
    near = lax.ppermute(rows, "silo", routes[0])
    return near, far


def body(
    activ, cotangent, error_memory, params, estimate, mixed,
    kept_blocks, kept_counts, gossip_blocks, gossip_counts,
):
    shards = lax.axis_size("shard")
    silos = lax.axis_size("silo")
    nblocks, block_len = error_memory.shape[2:]
    own_blocks = nblocks // shards
    per_row = activ.shape[1] // block_len
    scale = activ.shape[1] ** (-0.5)
    mine, *outgoing = select(
        shards, own_blocks, per_row, scale, kept_blocks, kept_counts, activ, cotangent, error_memory
    )
    arrived = [
        lax.ppermute(rows, "shard", [(r, (r + shift) % shards) for r in range(shards)])
        for shift, rows in enumerate(outgoing, 1)
    ]
    base, match = base_rows(
        shards, silos, per_row, kept_blocks, gossip_blocks, gossip_counts, params, estimate, mine
    )
    delta = delta_rows(base, match, arrived)
    first, second = exchange(delta, silos)
    error_out, estimate_out, mixed_pre, params_pre, spread = dense(
        shards, silos, own_blocks, per_row, scale, kept_blocks, kept_counts, gossip_blocks, gossip_counts,
        activ, cotangent, error_memory, params, estimate, mixed, delta, [mine, *arrived],
    )
    mixed_out, params_out = final(per_row, mixed.shape, mixed_pre, params_pre, spread, first, second)
    return params_out, estimate_out, mixed_out, error_out


def solution(mesh):
    in_specs = (
        P(("silo", "shard"), None),
        P(("silo", "shard"), None),
        P("silo", "shard", None, None),
        P("silo", "shard", None),
        P("silo", "shard", None),
        P("silo", "shard", None),
        P("silo", None, None, None),
        P("silo", None, None),
        P(None, "shard", None),
        P(None, "shard"),
    )
    out_specs = (
        P("silo", "shard", None),
        P("silo", "shard", None),
        P("silo", "shard", None),
        P("silo", "shard", None, None),
    )
    return jax.shard_map(body, mesh=mesh, in_specs=in_specs, out_specs=out_specs, check_vma=False)
```

```python
import functools

import jax
import jax.numpy as jnp
from jax import lax
from jax.experimental import pallas as pl
from jax.experimental.pallas import tpu as pltpu
from jax.sharding import PartitionSpec as P

LEARN_RATE = 0.25
CONSENSUS = 0.5
MIX_WEIGHT = 1.0 / 3.0

F32, BF16, I32 = jnp.float32, jnp.bfloat16, jnp.int32
ANY = pl.BlockSpec(memory_space=pl.ANY)
IN_VMEM = pl.BlockSpec(memory_space=pltpu.VMEM)
MIB = 1 << 20


def dot(a, b, dims=((1,), (0,))):
    return lax.dot_general(a, b, (dims, ((), ())), preferred_element_type=F32)


def as_column(row):
    n = row.shape[1]
    eye = lax.broadcasted_iota(I32, (n, n), 0) == lax.broadcasted_iota(I32, (n, n), 1)
    spread = jnp.where(eye, jnp.broadcast_to(row.astype(F32), (n, n)), 0.0)
    return jnp.sum(spread, axis=1, keepdims=True).astype(I32)


def thirds(rows):
    high = rows.astype(BF16)
    rest = rows - high.astype(F32)
    middle = rest.astype(BF16)
    low = (rest - middle.astype(F32)).astype(BF16)
    return high, middle, low


def pick(choice, parts):
    high, middle, low = parts
    return dot(choice, high) + (dot(choice, middle) + dot(choice, low))


def onehot(mask):
    return jnp.where(mask, 1.0, 0.0).astype(BF16)


def divide(value, by):
    return (value * ((1 << 16) // by + 1)) >> 16


def select_kernel(shards, own_blocks, per_row, scale, lists, counts, act, cot, err, *refs):
    mine, *outs = refs[:shards]
    act_v, cot_v, list_s, count_s, list_v, err_v, sems = refs[shards:]
    me = lax.axis_index("shard")
    slots = list_v.shape[1]
    tokens = act_v.shape[0]
    parts = 2
    step = tokens // parts
    small = [
        pltpu.make_async_copy(lists.at[0, me], list_s, sems.at[0]),
        pltpu.make_async_copy(lists.at[0, me], list_v, sems.at[1]),
        pltpu.make_async_copy(counts.at[0], count_s, sems.at[2]),
    ]
    for copy in small:
        copy.start()
    big = []
    for part in range(parts):
        rows = pl.ds(part * step, step)
        pair = [
            pltpu.make_async_copy(cot.at[rows], cot_v.at[rows], sems.at[4 + 2 * part]),
            pltpu.make_async_copy(act.at[rows], act_v.at[rows], sems.at[5 + 2 * part]),
        ]
        for copy in pair:
            copy.start()
        big.append(pair)
    for copy in small:
        copy.wait()

    for shift in range(1, shards):
        owner = lax.rem(me + shift, shards)

        def fetch(slot, carry, owner=owner, shift=shift):
            block = owner * own_blocks + list_s[owner, slot]
            pltpu.make_async_copy(
                err.at[0, 0, pl.ds(block, 1)], err_v.at[pl.ds((shift - 1) * slots + slot, 1)], sems.at[3]
            ).start()
            return carry

        lax.fori_loop(0, slots, fetch, 0, unroll=slots)

    columns, fills = [], []
    width_out = cot_v.shape[1]
    for shift in range(shards):
        owner = lax.rem(me + shift, shards)
        row = list_v[pl.ds(owner, 1), :] + owner * own_blocks
        columns.append(as_column(row))
        slot_ids = lax.broadcasted_iota(I32, (slots, 1), 0)
        fills.append(slot_ids < count_s[me, owner])
    blocks = jnp.concatenate(columns, axis=0)
    out_row = divide(blocks, per_row)
    segment = blocks - out_row * per_row
    total = blocks.shape[0]
    chosen = onehot(lax.broadcasted_iota(I32, (total, width_out), 1) == out_row)
    acc = jnp.zeros((total, act_v.shape[1]), F32)
    for part in range(parts):
        for copy in big[part]:
            copy.wait()
        rows = pl.ds(part * step, step)
        picked = dot(chosen, cot_v[rows, :], ((1,), (1,))).astype(BF16)
        acc = acc + dot(picked, act_v[rows, :])
    width = act_v.shape[1] // per_row
    grad = jnp.zeros((total, width), F32)
    for part in range(per_row):
        grad = jnp.where(segment == part, acc[:, part * width : (part + 1) * width], grad)
    grad = grad * scale
    mine[...] = grad[:slots]
    pltpu.make_async_copy(err.at[0, 0, pl.ds(0, total - slots)], err_v, sems.at[3]).wait()
    for shift in range(1, shards):
        here = slice((shift - 1) * slots, shift * slots)
        pending = err_v[here, :] + grad[shift * slots : (shift + 1) * slots]
        outs[shift - 1][...] = jnp.where(fills[shift], pending, 0.0)


def select(shards, own_blocks, per_row, scale, lists, counts, act, cot, err):
    slots = lists.shape[3]
    width = err.shape[3]
    return pl.pallas_call(
        functools.partial(select_kernel, shards, own_blocks, per_row, scale),
        name="kept_rows",
        in_specs=[ANY] * 5,
        out_specs=[IN_VMEM] * (shards + 2),
        out_shape=[pltpu.VMEM((slots, width), F32)] * shards
        + [pltpu.VMEM(act.shape, BF16), pltpu.VMEM(cot.shape, BF16)],
        scratch_shapes=[
            pltpu.SMEM((shards, slots), I32),
            pltpu.SMEM((shards, shards), I32),
            pltpu.VMEM((shards, slots), I32),
            pltpu.VMEM(((shards - 1) * slots, width), F32),
            pltpu.SemaphoreType.DMA((8,)),
        ],
        compiler_params=pltpu.CompilerParams(vmem_limit_bytes=16 * MIB),
    )(lists, counts, act, cot, err)


def add_gradient(cot_v, act_v, err_v, columns, per_row, scale):
    tile = 128
    halves = err_v.shape[0]
    for part in range(columns.start, columns.stop, tile):
        grad = dot(cot_v[:, part : part + tile], act_v[...], ((0,), (0,))) * scale
        for seg in range(per_row):
            where = pl.ds((part - columns.start) * per_row + seg, tile, stride=per_row)
            for half in range(halves):
                lane = (seg * halves + half) * 128
                err_v[half, where, :] = err_v[half, where, :] + grad[:, lane : lane + 128]


def clear_kept(err_v, list_s, count_s, me, own_blocks, first, spare):
    shards, slots = list_s.shape
    for owner in range(shards):
        if first >= (owner + 1) * own_blocks or first + spare <= owner * own_blocks:
            continue
        limit = count_s[me, owner]

        def clear(slot, carry, owner=owner, limit=limit):
            block = owner * own_blocks + list_s[owner, slot] - first
            kept = (slot < limit) & (block >= 0) & (block < spare)
            block = jnp.where(kept, block, spare)
            for half in range(err_v.shape[0]):
                err_v[half, pl.ds(block, 1), :] = jnp.zeros((1, 128), F32)
            return carry

        lax.fori_loop(0, slots, clear, 0, unroll=16)


def memory_copies(err, err_v, first, spare, sems):
    return [
        pltpu.make_async_copy(
            err.at[0, 0, pl.ds(first, spare), pl.ds(half * 128, 128)], err_v.at[half, pl.ds(0, spare)], sems[half]
        )
        for half in range(err_v.shape[0])
    ]


def base_kernel(
    shards, own_blocks, per_row, scale, split,
    lists, counts, g_lists, g_counts, params, estimate, err, grad, act_v, cot_v,
    base, match, mine, p_v, e_v, err_a,
    list_s, count_s, list_v, g_s, g_v, gc_s, pr_v, er_v, mr_v, sems,
):
    me = lax.axis_index("shard")
    silo = lax.axis_index("silo")
    slots = list_v.shape[2]
    g_slots = g_v.shape[1]
    width = pr_v.shape[1]
    spare = split * per_row
    small = [
        pltpu.make_async_copy(g_lists.at[silo], g_s, sems.at[0]),
        pltpu.make_async_copy(lists.at[0, me], list_s, sems.at[1]),
        pltpu.make_async_copy(counts.at[0], count_s, sems.at[2]),
        pltpu.make_async_copy(g_lists.at[silo], g_v, sems.at[3]),
        pltpu.make_async_copy(g_counts, gc_s, sems.at[4]),
        pltpu.make_async_copy(lists.at[0], list_v, sems.at[5]),
    ]
    for copy in small:
        copy.start()
    memory = memory_copies(err, err_a, 0, spare, [sems.at[6 + half] for half in range(err_a.shape[0])])
    for copy in memory:
        copy.start()
    for copy in small:
        copy.wait()

    def fetch(slot, carry):
        block = g_s[0, slot]
        row = divide(block, per_row)
        column = pl.multiple_of((block - row * per_row) * width, width)
        where = (0, pl.ds(row, 1), pl.ds(column, width))
        into = pl.ds(slot, 1)
        pltpu.make_async_copy(params.at[where], pr_v.at[into], sems.at[0]).start()
        pltpu.make_async_copy(estimate.at[where], er_v.at[into], sems.at[1]).start()
        return carry

    lax.fori_loop(0, g_slots, fetch, 0, unroll=32)

    def fetch_own(slot, carry):
        block = me * own_blocks + list_s[me, slot]
        pltpu.make_async_copy(err.at[0, 0, pl.ds(block, 1)], mr_v.at[pl.ds(slot, 1)], sems.at[2]).start()
        return carry

    lax.fori_loop(0, slots, fetch_own, 0, unroll=32)
    owned = [
        pltpu.make_async_copy(params.at[0], p_v, sems.at[3]),
        pltpu.make_async_copy(estimate.at[0], e_v, sems.at[4]),
    ]
    for copy in owned:
        copy.start()

    for copy in memory:
        copy.wait()
    add_gradient(cot_v, act_v, err_a, slice(0, split), per_row, scale)
    clear_kept(err_a, list_s, count_s, me, own_blocks, 0, spare)

    blocks = as_column(g_v[...])
    filled = lax.broadcasted_iota(I32, (g_slots, 1), 0) < gc_s[silo]
    kept_here = lax.broadcasted_iota(I32, (slots, 1), 0) < count_s[me, me]
    for shift in range(shards):
        sender = lax.rem(me - shift + shards, shards)
        same = onehot((blocks == list_v[sender, pl.ds(me, 1), :]) & filled)
        if shift == 0:
            own = same
        else:
            match[:, (shift - 1) * slots : shift * slots] = same
    pltpu.make_async_copy(pr_v, pr_v, sems.at[0]).wait()
    pltpu.make_async_copy(er_v, er_v, sems.at[1]).wait()
    pltpu.make_async_copy(mr_v, mr_v, sems.at[2]).wait()
    rows = jnp.where(kept_here, mr_v[...] + grad[...], 0.0)
    mine[...] = rows
    base[...] = jnp.where(filled, pr_v[...] - er_v[...], 0.0) - LEARN_RATE * pick(own, thirds(rows))
    for copy in owned:
        copy.wait()


def base_rows(
    shards, own_blocks, per_row, scale, split,
    lists, counts, g_lists, g_counts, params, estimate, err, grad, act_v, cot_v,
):
    slots, width = grad.shape
    g_slots = g_lists.shape[2]
    owned = params.shape[1:]
    return pl.pallas_call(
        functools.partial(base_kernel, shards, own_blocks, per_row, scale, split),
        name="gossip_base",
        in_specs=[ANY] * 7 + [IN_VMEM] * 3,
        out_specs=[IN_VMEM] * 6,
        out_shape=[
            pltpu.VMEM((g_slots, width), F32),
            pltpu.VMEM((g_slots, (shards - 1) * slots), BF16),
            pltpu.VMEM((slots, width), F32),
            pltpu.VMEM(owned, F32),
            pltpu.VMEM(owned, F32),
            pltpu.VMEM((width // 128, split * per_row + 8, 128), F32),
        ],
        scratch_shapes=[
            pltpu.SMEM((shards, slots), I32),
            pltpu.SMEM((shards, shards), I32),
            pltpu.VMEM((shards, shards, slots), I32),
            pltpu.SMEM((1, g_slots), I32),
            pltpu.VMEM((1, g_slots), I32),
            pltpu.SMEM(g_counts.shape, I32),
            pltpu.VMEM((g_slots, width), F32),
            pltpu.VMEM((g_slots, width), F32),
            pltpu.VMEM((slots, width), F32),
            pltpu.SemaphoreType.DMA((6 + width // 128,)),
        ],
        compiler_params=pltpu.CompilerParams(vmem_limit_bytes=16 * MIB),
    )(lists, counts, g_lists, g_counts, params, estimate, err, grad, act_v, cot_v)


def delta_kernel(base, match, *refs):
    *arrived, out = refs
    slots = arrived[0].shape[0]
    total = base[...]
    for place, rows in enumerate(arrived):
        same = match[:, place * slots : (place + 1) * slots]
        total = total - LEARN_RATE * pick(same, thirds(rows[...]))
    out[...] = total


def delta_rows(base, match, arrived):
    return pl.pallas_call(
        delta_kernel,
        name="delta_rows",
        in_specs=[IN_VMEM] * (2 + len(arrived)),
        out_specs=IN_VMEM,
        out_shape=pltpu.VMEM(base.shape, F32),
        compiler_params=pltpu.CompilerParams(vmem_limit_bytes=8 * MIB),
    )(base, match, *arrived)


def dense_kernel(
    shards, silos, own_blocks, per_row, scale, split,
    lists, counts, g_lists, err, mixed, p_v, e_v, act_v, cot_v, err_a, delta, *refs
):
    kept = refs[:shards]
    (err_out, est_out, mixed_pre, params_pre, spread,
     list_s, count_s, list_v, g_v, err_b, m_v, est_v, sems) = refs[shards:]
    me = lax.axis_index("shard")
    silo = lax.axis_index("silo")
    width = delta.shape[1]
    width_out = cot_v.shape[1]
    out_rows = p_v.shape[0]
    halves = width // 128
    done, rest = split * per_row, (width_out - split) * per_row
    small = [
        pltpu.make_async_copy(lists.at[0, me], list_s, sems.at[0]),
        pltpu.make_async_copy(lists.at[0], list_v, sems.at[1]),
        pltpu.make_async_copy(counts.at[0], count_s, sems.at[2]),
        pltpu.make_async_copy(g_lists, g_v, sems.at[3]),
    ]
    memory = memory_copies(err, err_b, done, rest, [sems.at[5 + half] for half in range(halves)])
    mixed_copy = pltpu.make_async_copy(mixed.at[0], m_v, sems.at[4])
    stores = [
        pltpu.make_async_copy(
            err_a.at[half, pl.ds(0, done)],
            err_out.at[0, 0, pl.ds(0, done), pl.ds(half * 128, 128)],
            sems.at[5 + halves + half],
        )
        for half in range(halves)
    ]
    for copy in small + memory + [mixed_copy] + stores:
        copy.start()
    for copy in memory:
        copy.wait()
    add_gradient(cot_v, act_v, err_b, slice(split, width_out), per_row, scale)
    for copy in small:
        copy.wait()
    clear_kept(err_b, list_s, count_s, me, own_blocks, done, rest)
    for half in range(halves):
        copy = pltpu.make_async_copy(
            err_b.at[half, pl.ds(0, rest)],
            err_out.at[0, 0, pl.ds(done, rest), pl.ds(half * 128, 128)],
            sems.at[5 + half],
        )
        copy.start()
        stores.append(copy)

    first, second = neighbours(silo, silos)
    kept_parts = thirds(jnp.concatenate([rows[...] for rows in kept], axis=0))
    kept_ids = jnp.concatenate(
        [list_v[lax.rem(me - shift + shards, shards), pl.ds(me, 1), :] for shift in range(shards)], axis=1
    )
    delta_parts = thirds(delta[...])
    own_ids = g_v[silo]
    next_ids = jnp.concatenate([g_v[first], g_v[second]], axis=1)
    mixed_copy.wait()
    for part in range(per_row):
        lanes = slice(part * width, (part + 1) * width)

        def places(ids):
            here = lax.broadcasted_iota(I32, (out_rows, ids.shape[1]), 0) * per_row + part
            return onehot(here == ids)

        grad = pick(places(kept_ids), kept_parts)
        change = pick(places(own_ids), delta_parts)
        spread[part * out_rows : (part + 1) * out_rows, :] = places(next_ids)
        half_step = p_v[:, lanes] - LEARN_RATE * grad
        est = e_v[:, lanes] + change
        mix = m_v[:, lanes] + MIX_WEIGHT * change
        est_v[:, lanes] = est
        mixed_pre[:, lanes] = mix
        params_pre[:, lanes] = half_step + CONSENSUS * (mix - est)
    est_copy = pltpu.make_async_copy(est_v, est_out.at[0], sems.at[4])
    est_copy.start()
    for copy in stores:
        copy.wait()
    est_copy.wait()


def dense(
    shards, silos, own_blocks, per_row, scale, split,
    lists, counts, g_lists, err, mixed, p_v, e_v, act_v, cot_v, err_a, delta, kept,
):
    slots = lists.shape[3]
    g_slots = g_lists.shape[2]
    width = err.shape[3]
    owned = p_v.shape
    rest = (cot_v.shape[1] - split) * per_row
    return pl.pallas_call(
        functools.partial(dense_kernel, shards, silos, own_blocks, per_row, scale, split),
        name="dense",
        in_specs=[ANY] * 5 + [IN_VMEM] * (6 + shards),
        out_specs=[ANY, ANY, IN_VMEM, IN_VMEM, IN_VMEM],
        out_shape=[
            pltpu.HBM(err.shape, F32),
            pltpu.HBM(mixed.shape, F32),
            pltpu.VMEM(owned, F32),
            pltpu.VMEM(owned, F32),
            pltpu.VMEM((own_blocks, 2 * g_slots), BF16),
        ],
        scratch_shapes=[
            pltpu.SMEM((shards, slots), I32),
            pltpu.SMEM((shards, shards), I32),
            pltpu.VMEM((shards, shards, slots), I32),
            pltpu.VMEM(g_lists.shape, I32),
            pltpu.VMEM((width // 128, rest + 8, 128), F32),
            pltpu.VMEM(owned, F32),
            pltpu.VMEM(owned, F32),
            pltpu.SemaphoreType.DMA((5 + 2 * (width // 128),)),
        ],
        compiler_params=pltpu.CompilerParams(vmem_limit_bytes=24 * MIB),
    )(lists, counts, g_lists, err, mixed, p_v, e_v, act_v, cot_v, err_a, delta, *kept)


def final_kernel(per_row, mixed_pre, params_pre, spread, first, second, mixed_out, params_out, m_v, p_v, sems):
    out_rows = m_v.shape[0]
    width = m_v.shape[1] // per_row
    parts = thirds(jnp.concatenate([first[...], second[...]], axis=0))
    copies = []
    for part in range(per_row):
        lanes = slice(part * width, (part + 1) * width)
        change = pick(spread[part * out_rows : (part + 1) * out_rows, :], parts)
        m_v[:, lanes] = mixed_pre[:, lanes] + MIX_WEIGHT * change
        p_v[:, lanes] = params_pre[:, lanes] + (CONSENSUS * MIX_WEIGHT) * change
        pair = [
            pltpu.make_async_copy(m_v.at[:, lanes], mixed_out.at[0, :, lanes], sems.at[2 * part]),
            pltpu.make_async_copy(p_v.at[:, lanes], params_out.at[0, :, lanes], sems.at[2 * part + 1]),
        ]
        for copy in pair:
            copy.start()
        copies += pair
    for copy in copies:
        copy.wait()


def final(per_row, shape, mixed_pre, params_pre, spread, first, second):
    return pl.pallas_call(
        functools.partial(final_kernel, per_row),
        name="neighbours",
        in_specs=[IN_VMEM] * 5,
        out_specs=[ANY] * 2,
        out_shape=[pltpu.HBM(shape, F32)] * 2,
        scratch_shapes=[
            pltpu.VMEM(mixed_pre.shape, F32),
            pltpu.VMEM(mixed_pre.shape, F32),
            pltpu.SemaphoreType.DMA((2 * per_row,)),
        ],
        compiler_params=pltpu.CompilerParams(vmem_limit_bytes=20 * MIB),
    )(mixed_pre, params_pre, spread, first, second)


def neighbours(silo, silos):
    lower, upper = lax.rem(silo + silos - 1, silos), lax.rem(silo + 1, silos)
    if silos % 2:
        return lower, upper
    even = lax.rem(silo, 2) == 0
    return jnp.where(even, upper, lower), jnp.where(even, lower, upper)


def exchange(rows, silos):
    if silos % 2:
        routes = [[(a, (a + 1) % silos) for a in range(silos)], [(a, (a - 1) % silos) for a in range(silos)]]
    else:
        routes = [
            [(a, a ^ 1) for a in range(silos)],
            [(a, (a + 1 if a % 2 else a - 1) % silos) for a in range(silos)],
        ]
    far = lax.ppermute(rows, "silo", routes[1])
    near = lax.ppermute(rows, "silo", routes[0])
    return near, far


def body(
    activ, cotangent, error_memory, params, estimate, mixed,
    kept_blocks, kept_counts, gossip_blocks, gossip_counts,
):
    shards = lax.axis_size("shard")
    silos = lax.axis_size("silo")
    nblocks, block_len = error_memory.shape[2:]
    own_blocks = nblocks // shards
    per_row = activ.shape[1] // block_len
    scale = activ.shape[1] ** (-0.5)
    split = cotangent.shape[1] // 2 // 128 * 128
    activ, cotangent, error_memory, params, estimate, mixed, kept_blocks, kept_counts, gossip_blocks, gossip_counts = (
        pltpu.with_memory_space_constraint(array, pltpu.HBM)
        for array in (
            activ, cotangent, error_memory, params, estimate, mixed,
            kept_blocks, kept_counts, gossip_blocks, gossip_counts.reshape(silos),
        )
    )
    grad, *outgoing, act_v, cot_v = select(
        shards, own_blocks, per_row, scale, kept_blocks, kept_counts, activ, cotangent, error_memory
    )
    arrived = [
        lax.ppermute(rows, "shard", [(r, (r + shift) % shards) for r in range(shards)])
        for shift, rows in enumerate(outgoing, 1)
    ]
    base, match, mine, p_v, e_v, err_a = base_rows(
        shards, own_blocks, per_row, scale, split, kept_blocks, kept_counts, gossip_blocks, gossip_counts,
        params, estimate, error_memory, grad, act_v, cot_v,
    )
    delta = delta_rows(base, match, arrived)
    first, second = exchange(delta, silos)
    error_out, estimate_out, mixed_pre, params_pre, spread = dense(
        shards, silos, own_blocks, per_row, scale, split, kept_blocks, kept_counts, gossip_blocks,
        error_memory, mixed, p_v, e_v, act_v, cot_v, err_a, delta, [mine, *arrived],
    )
    mixed_out, params_out = final(per_row, mixed.shape, mixed_pre, params_pre, spread, first, second)
    return params_out, estimate_out, mixed_out, error_out


def solution(mesh):
    in_specs = (
        P(("silo", "shard"), None),
        P(("silo", "shard"), None),
        P("silo", "shard", None, None),
        P("silo", "shard", None),
        P("silo", "shard", None),
        P("silo", "shard", None),
        P("silo", None, None, None),
        P("silo", None, None),
        P(None, "shard", None),
        P(None, "shard"),
    )
    out_specs = (
        P("silo", "shard", None),
        P("silo", "shard", None),
        P("silo", "shard", None),
        P("silo", "shard", None, None),
    )
    return jax.shard_map(body, mesh=mesh, in_specs=in_specs, out_specs=out_specs, check_vma=False)
```

```python
import functools

import jax
import jax.numpy as jnp
from jax import lax
from jax.experimental import pallas as pl
from jax.experimental.pallas import tpu as pltpu
from jax.sharding import PartitionSpec as P

LEARN_RATE = 0.25
CONSENSUS = 0.5
MIX_WEIGHT = 1.0 / 3.0

F32, BF16, I32 = jnp.float32, jnp.bfloat16, jnp.int32
ANY = pl.BlockSpec(memory_space=pl.ANY)
IN_VMEM = pl.BlockSpec(memory_space=pltpu.VMEM)
MIB = 1 << 20


def dot(a, b, dims=((1,), (0,))):
    return lax.dot_general(a, b, (dims, ((), ())), preferred_element_type=F32)


def as_column(row):
    n = row.shape[1]
    eye = lax.broadcasted_iota(I32, (n, n), 0) == lax.broadcasted_iota(I32, (n, n), 1)
    spread = jnp.where(eye, jnp.broadcast_to(row.astype(F32), (n, n)), 0.0)
    return jnp.sum(spread, axis=1, keepdims=True).astype(I32)


def split(rows):
    high = rows.astype(BF16)
    return jnp.concatenate([high, (rows - high.astype(F32)).astype(BF16)], axis=0)


def pick(choice, rows):
    return dot(jnp.concatenate([choice, choice], axis=1), rows)


def onehot(mask):
    return jnp.where(mask, 1.0, 0.0).astype(BF16)


def divide(value, by):
    return (value * ((1 << 16) // by + 1)) >> 16


def rows_kernel(shards, own_blocks, per_row, scale, lists, counts, g_lists, act, cot, err, *refs):
    outs = refs[: shards - 1]
    act_v, cot_v, lists_v, g_v, list_s, count_s, err_v, sems = refs[shards - 1 :]
    me = lax.axis_index("shard")
    slots = lists_v.shape[2]
    width = err_v.shape[1]
    parts = 4
    step = act_v.shape[0] // parts
    small = [
        pltpu.make_async_copy(lists.at[0, me], list_s, sems.at[0]),
        pltpu.make_async_copy(lists.at[0], lists_v, sems.at[1]),
        pltpu.make_async_copy(counts.at[0], count_s, sems.at[2]),
        pltpu.make_async_copy(g_lists, g_v, sems.at[3]),
    ]
    for copy in small:
        copy.start()
    big = []
    for part in range(parts):
        rows = pl.ds(part * step, step)
        pair = [
            pltpu.make_async_copy(cot.at[rows], cot_v.at[rows], sems.at[4 + 2 * part]),
            pltpu.make_async_copy(act.at[rows], act_v.at[rows], sems.at[5 + 2 * part]),
        ]
        for copy in pair:
            copy.start()
        big.append(pair)
    for copy in small:
        copy.wait()

    columns, fills = [], []
    for shift in range(1, shards):
        owner = lax.rem(me + shift, shards)

        def fetch(slot, carry, owner=owner, shift=shift):
            block = owner * own_blocks + list_s[owner, slot]
            into = err_v.at[pl.ds((shift - 1) * slots + slot, 1)]
            pltpu.make_async_copy(err.at[0, 0, pl.ds(block, 1)], into, sems.at[0]).start()
            return carry

        lax.fori_loop(0, slots, fetch, 0, unroll=slots)
        row = lists_v[me, pl.ds(owner, 1), :] + owner * own_blocks
        columns.append(as_column(row))
        slot_ids = lax.broadcasted_iota(I32, (slots, 1), 0)
        fills.append(slot_ids < count_s[me, owner])
    blocks = jnp.concatenate(columns, axis=0)
    filled = jnp.concatenate(fills, axis=0)
    out_row = divide(blocks, per_row)
    segment = blocks - out_row * per_row
    total = blocks.shape[0]
    chosen = onehot(lax.broadcasted_iota(I32, (total, cot_v.shape[1]), 1) == out_row)
    acc = jnp.zeros((total, act_v.shape[1]), F32)
    for part in range(parts):
        for copy in big[part]:
            copy.wait()
        rows = pl.ds(part * step, step)
        picked = dot(chosen, cot_v[rows, :], ((1,), (1,))).astype(BF16)
        acc = acc + dot(picked, act_v[rows, :])
    grad = jnp.zeros((total, width), F32)
    for part in range(per_row):
        grad = jnp.where(segment == part, acc[:, part * width : (part + 1) * width], grad)
    pltpu.make_async_copy(err_v, err_v, sems.at[0]).wait()
    pending = jnp.where(filled, err_v[...] + grad * scale, 0.0)
    for place, out in enumerate(outs):
        out[...] = pending[place * slots : (place + 1) * slots]


def moving_rows(shards, own_blocks, per_row, scale, lists, counts, g_lists, act, cot, err):
    slots = lists.shape[3]
    width = err.shape[3]
    return pl.pallas_call(
        functools.partial(rows_kernel, shards, own_blocks, per_row, scale),
        name="moving_rows",
        in_specs=[ANY] * 6,
        out_specs=[IN_VMEM] * (shards + 3),
        out_shape=[pltpu.VMEM((slots, width), F32)] * (shards - 1)
        + [
            pltpu.VMEM(act.shape, BF16),
            pltpu.VMEM(cot.shape, BF16),
            pltpu.VMEM(lists.shape[1:], I32),
            pltpu.VMEM(g_lists.shape, I32),
        ],
        scratch_shapes=[
            pltpu.SMEM((shards, slots), I32),
            pltpu.SMEM((shards, shards), I32),
            pltpu.VMEM(((shards - 1) * slots, width), F32),
            pltpu.SemaphoreType.DMA((12,)),
        ],
        compiler_params=pltpu.CompilerParams(vmem_limit_bytes=16 * MIB),
    )(lists, counts, g_lists, act, cot, err)


def take_kept(err_v, rows_v, list_s, count_s, me, own_blocks):
    shards, slots = list_s.shape
    halves = range(err_v.shape[0])

    def take(slot, carry):
        block = me * own_blocks + list_s[me, slot]
        for half in halves:
            rows_v[half, pl.ds(slot, 1), :] = err_v[half, pl.ds(block, 1), :]
        return carry

    lax.fori_loop(0, slots, take, 0, unroll=slots)
    for owner in range(shards):
        limit = count_s[me, owner]

        def clear(slot, carry, owner=owner, limit=limit):
            block = jnp.where(slot < limit, owner * own_blocks + list_s[owner, slot], shards * own_blocks)
            for half in halves:
                err_v[half, pl.ds(block, 1), :] = jnp.zeros((1, 128), F32)
            return carry

        lax.fori_loop(0, slots, clear, 0, unroll=slots)


def gradient_kernel(
    shards, own_blocks, per_row, scale,
    lists, counts, g_lists, g_counts, err, params, estimate, mixed, lists_v, g_v, act_v, cot_v,
    mine, base, match, err_v, p_v, e_v, m_v,
    list_s, count_s, g_s, gc_s, rows_v, grad_v, sems,
):
    me = lax.axis_index("shard")
    silo = lax.axis_index("silo")
    slots, width = mine.shape
    g_slots = g_v.shape[2]
    tile = 128
    tiles = cot_v.shape[1] // tile
    step = tile * per_row
    halves = err_v.shape[0]
    small = [
        pltpu.make_async_copy(g_counts, gc_s, sems.at[0]),
        pltpu.make_async_copy(counts.at[0], count_s, sems.at[1]),
        pltpu.make_async_copy(lists.at[0, me], list_s, sems.at[2]),
        pltpu.make_async_copy(g_lists.at[silo], g_s, sems.at[6]),
    ]
    for copy in small:
        copy.start()
    memory = []
    for part in range(tiles):
        rows = pl.ds(part * step, step)
        memory.append(
            [
                pltpu.make_async_copy(
                    err.at[0, 0, rows, pl.ds(half * 128, 128)],
                    err_v.at[half, rows],
                    sems.at[7 + part * halves + half],
                )
                for half in range(halves)
            ]
        )
    for copy in sum(memory, []):
        copy.start()
    out_rows = params.shape[1]
    owned = [
        pltpu.make_async_copy(
            array.at[0, :, pl.ds(chunk * 128, 128)], array_v.at[pl.ds(chunk * out_rows, out_rows)], sems.at[3 + place]
        )
        for place, (array, array_v) in enumerate([(params, p_v), (estimate, e_v), (mixed, m_v)])
        for chunk in range(per_row * halves)
    ]

    for copy in owned:
        copy.start()
    ahead = tiles - 1

    def tile_gradient(part):
        columns = pl.ds(pl.multiple_of(part * tile, tile), tile)
        return dot(cot_v[:, columns], act_v[...], ((0,), (0,))) * scale

    def pieces(grad, part):
        for seg in range(per_row):
            for half in range(halves):
                lane = (seg * halves + half) * 128
                yield (half, pl.ds(part * step + seg, tile, stride=per_row)), grad[:, lane : lane + 128]

    def store(part, carry):
        for where, piece in pieces(tile_gradient(part), part):
            grad_v[where] = piece
        return carry

    lax.fori_loop(0, ahead, store, 0)
    for copy in sum(memory, []):
        copy.wait()
    for where, piece in pieces(tile_gradient(ahead), ahead):
        err_v[where] = err_v[where] + piece
    for half in range(halves):
        err_v[half, : ahead * step, :] = err_v[half, : ahead * step, :] + grad_v[half]
    for copy in small:
        copy.wait()
    take_kept(err_v, rows_v, list_s, count_s, me, own_blocks)
    kept = lax.broadcasted_iota(I32, (slots, 1), 0) < count_s[me, me]
    mine[...] = jnp.where(kept, jnp.concatenate([rows_v[half, :slots] for half in range(halves)], axis=1), 0.0)
    blocks = as_column(g_v[silo])
    filled = lax.broadcasted_iota(I32, (g_slots, 1), 0) < gc_s[silo]
    for shift in range(shards):
        sender = lax.rem(me - shift + shards, shards)
        ids = lists_v[sender, pl.ds(me, 1), :]
        same = onehot((blocks == jnp.concatenate([ids, ids], axis=1)) & filled)
        if shift == 0:
            own = dot(same, split(mine[...]))
        else:
            match[:, 2 * (shift - 1) * slots : 2 * shift * slots] = same
    for copy in owned:
        copy.wait()

    def gather(slot, carry):
        block = g_s[0, slot]
        row = divide(block, per_row)
        start = (block - row * per_row) * (halves * out_rows) + row
        for half in range(halves):
            where = pl.ds(start + half * out_rows, 1)
            rows_v[half, pl.ds(slot, 1), :] = p_v[where, :] - e_v[where, :]
        return carry

    lax.fori_loop(0, g_slots, gather, 0, unroll=g_slots)
    rows = jnp.concatenate([rows_v[half, :g_slots] for half in range(halves)], axis=1)
    base[...] = jnp.where(filled, rows, 0.0) - LEARN_RATE * own


def gradient(
    shards, own_blocks, per_row, scale,
    lists, counts, g_lists, g_counts, err, params, estimate, mixed, lists_v, g_v, act_v, cot_v,
):
    slots = lists.shape[3]
    width = err.shape[3]
    g_slots = g_v.shape[2]
    owned = (params.shape[1] * params.shape[2] // 128, 128)
    halves = width // 128
    return pl.pallas_call(
        functools.partial(gradient_kernel, shards, own_blocks, per_row, scale),
        name="gradient",
        in_specs=[ANY] * 8 + [IN_VMEM] * 4,
        out_specs=[IN_VMEM] * 7,
        out_shape=[
            pltpu.VMEM((slots, width), F32),
            pltpu.VMEM((g_slots, width), F32),
            pltpu.VMEM((g_slots, 2 * (shards - 1) * slots), BF16),
            pltpu.VMEM((halves, shards * own_blocks + 8, 128), F32),
            pltpu.VMEM(owned, F32),
            pltpu.VMEM(owned, F32),
            pltpu.VMEM(owned, F32),
        ],
        scratch_shapes=[
            pltpu.SMEM((shards, slots), I32),
            pltpu.SMEM((shards, shards), I32),
            pltpu.SMEM((1, g_slots), I32),
            pltpu.SMEM(g_counts.shape, I32),
            pltpu.VMEM((halves, max(slots, g_slots), 128), F32),
            pltpu.VMEM((halves, (cot_v.shape[1] - 128) * per_row, 128), F32),
            pltpu.SemaphoreType.DMA((7 + cot_v.shape[1] // 128 * halves,)),
        ],
        compiler_params=pltpu.CompilerParams(vmem_limit_bytes=16 * MIB),
    )(lists, counts, g_lists, g_counts, err, params, estimate, mixed, lists_v, g_v, act_v, cot_v)


def delta_kernel(base, match, *refs):
    *arrived, out = refs
    rows = jnp.concatenate([split(each[...]) for each in arrived], axis=0)
    out[...] = base[...] - LEARN_RATE * dot(match[...], rows)


def delta_rows(base, match, arrived):
    return pl.pallas_call(
        delta_kernel,
        name="delta_rows",
        in_specs=[IN_VMEM] * (2 + len(arrived)),
        out_specs=IN_VMEM,
        out_shape=pltpu.VMEM(base.shape, F32),
        compiler_params=pltpu.CompilerParams(vmem_limit_bytes=8 * MIB),
    )(base, match, *arrived)


def own_kernel(shards, silos, per_row, lists_v, g_v, err_v, p_v, e_v, m_v, delta, *refs):
    kept = refs[:shards]
    err_out, est_out, mixed_pre, params_pre, spread, est_v, sems = refs[shards:]
    me = lax.axis_index("shard")
    silo = lax.axis_index("silo")
    width = delta.shape[1]
    halves = err_v.shape[0]
    out_rows = p_v.shape[0] // (per_row * halves)
    nblocks = err_out.shape[2]
    copies = [
        pltpu.make_async_copy(
            err_v.at[half, pl.ds(0, nblocks)], err_out.at[0, 0, :, pl.ds(half * 128, 128)], sems.at[half]
        )
        for half in range(err_v.shape[0])
    ]
    for copy in copies:
        copy.start()
    first, second = neighbours(silo, silos)
    kept_parts = split(jnp.concatenate([rows[...] for rows in kept], axis=0))
    kept_ids = jnp.concatenate(
        [lists_v[lax.rem(me - shift + shards, shards), pl.ds(me, 1), :] for shift in range(shards)], axis=1
    )
    delta_parts = split(delta[...])
    own_ids = g_v[silo]
    next_ids = jnp.concatenate([g_v[first], g_v[second]], axis=1)
    for part in range(per_row):
        lanes = slice(part * width, (part + 1) * width)

        def places(ids):
            here = lax.broadcasted_iota(I32, (out_rows, ids.shape[1]), 0) * per_row + part
            return onehot(here == ids)

        grad = pick(places(kept_ids), kept_parts)
        change = pick(places(own_ids), delta_parts)
        p, e, m = (
            jnp.concatenate(
                [
                    array[(part * halves + half) * out_rows : (part * halves + half + 1) * out_rows, :]
                    for half in range(halves)
                ],
                axis=1,
            )
            for array in (p_v, e_v, m_v)
        )
        half_step = p - LEARN_RATE * grad
        est = e + change
        mix = m + MIX_WEIGHT * change
        est_v[:, lanes] = est
        copy = pltpu.make_async_copy(est_v.at[:, lanes], est_out.at[0, :, lanes], sems.at[err_v.shape[0] + part])
        copy.start()
        copies.append(copy)
        mixed_pre[:, lanes] = mix
        params_pre[:, lanes] = half_step + CONSENSUS * (mix - est)
        spread[part * out_rows : (part + 1) * out_rows, :] = places(next_ids)
    for copy in copies:
        copy.wait()


def own_updates(shards, silos, per_row, err_shape, est_shape, lists_v, g_v, err_v, p_v, e_v, m_v, delta, kept):
    g_slots = g_v.shape[2]
    owned = est_shape[1:]
    return pl.pallas_call(
        functools.partial(own_kernel, shards, silos, per_row),
        name="own_updates",
        in_specs=[IN_VMEM] * (7 + shards),
        out_specs=[ANY, ANY, IN_VMEM, IN_VMEM, IN_VMEM],
        out_shape=[
            pltpu.HBM(err_shape, F32),
            pltpu.HBM(est_shape, F32),
            pltpu.VMEM(owned, F32),
            pltpu.VMEM(owned, F32),
            pltpu.VMEM((owned[0] * per_row, 2 * g_slots), BF16),
        ],
        scratch_shapes=[
            pltpu.VMEM(owned, F32),
            pltpu.SemaphoreType.DMA((err_v.shape[0] + per_row,)),
        ],
        compiler_params=pltpu.CompilerParams(vmem_limit_bytes=16 * MIB),
    )(lists_v, g_v, err_v, p_v, e_v, m_v, delta, *kept)


def final_kernel(per_row, mixed_pre, params_pre, spread, first, second, mixed_out, params_out, m_v, p_v, sems):
    out_rows = m_v.shape[0]
    width = m_v.shape[1] // per_row
    rows = split(jnp.concatenate([first[...], second[...]], axis=0))
    depth = spread.shape[1]
    copies = []
    for part in range(per_row):
        lanes = slice(part * width, (part + 1) * width)
        choice = spread[part * out_rows : (part + 1) * out_rows, :]
        change = dot(choice, rows[:depth]) + dot(choice, rows[depth:])
        m_v[:, lanes] = mixed_pre[:, lanes] + MIX_WEIGHT * change
        p_v[:, lanes] = params_pre[:, lanes] + (CONSENSUS * MIX_WEIGHT) * change
        pair = [
            pltpu.make_async_copy(m_v.at[:, lanes], mixed_out.at[0, :, lanes], sems.at[2 * part]),
            pltpu.make_async_copy(p_v.at[:, lanes], params_out.at[0, :, lanes], sems.at[2 * part + 1]),
        ]
        for copy in pair:
            copy.start()
        copies += pair
    for copy in copies:
        copy.wait()


def final(per_row, shape, mixed_pre, params_pre, spread, first, second):
    return pl.pallas_call(
        functools.partial(final_kernel, per_row),
        name="neighbours",
        in_specs=[IN_VMEM] * 5,
        out_specs=[ANY] * 2,
        out_shape=[pltpu.HBM(shape, F32)] * 2,
        scratch_shapes=[
            pltpu.VMEM(mixed_pre.shape, F32),
            pltpu.VMEM(mixed_pre.shape, F32),
            pltpu.SemaphoreType.DMA((2 * per_row,)),
        ],
        compiler_params=pltpu.CompilerParams(vmem_limit_bytes=20 * MIB),
    )(mixed_pre, params_pre, spread, first, second)


def neighbours(silo, silos):
    lower, upper = lax.rem(silo + silos - 1, silos), lax.rem(silo + 1, silos)
    if silos % 2:
        return lower, upper
    even = lax.rem(silo, 2) == 0
    return jnp.where(even, lower, upper), jnp.where(even, upper, lower)


def exchange(rows, silos):
    if silos % 2:
        routes = [[(a, (a + 1) % silos) for a in range(silos)], [(a, (a - 1) % silos) for a in range(silos)]]
    else:
        routes = [
            [(a, (a + 1 if a % 2 else a - 1) % silos) for a in range(silos)],
            [(a, a ^ 1) for a in range(silos)],
        ]
    far = lax.ppermute(rows, "silo", routes[0])
    near = lax.ppermute(rows, "silo", routes[1])
    return far, near


def body(
    activ, cotangent, error_memory, params, estimate, mixed,
    kept_blocks, kept_counts, gossip_blocks, gossip_counts,
):
    shards = lax.axis_size("shard")
    silos = lax.axis_size("silo")
    nblocks, block_len = error_memory.shape[2:]
    own_blocks = nblocks // shards
    per_row = activ.shape[1] // block_len
    scale = activ.shape[1] ** (-0.5)
    activ, cotangent, error_memory, params, estimate, mixed, kept_blocks, kept_counts, gossip_blocks, gossip_counts = (
        pltpu.with_memory_space_constraint(array, pltpu.HBM)
        for array in (
            activ, cotangent, error_memory, params, estimate, mixed,
            kept_blocks, kept_counts, gossip_blocks, gossip_counts.reshape(silos),
        )
    )
    *outgoing, act_v, cot_v, lists_v, g_v = moving_rows(
        shards, own_blocks, per_row, scale,
        kept_blocks, kept_counts, gossip_blocks, activ, cotangent, error_memory,
    )
    arrived = [
        lax.ppermute(rows, "shard", [(r, (r + shift) % shards) for r in range(shards)])
        for shift, rows in enumerate(outgoing, 1)
    ]
    mine, base, match, err_v, p_v, e_v, m_v = gradient(
        shards, own_blocks, per_row, scale, kept_blocks, kept_counts, gossip_blocks, gossip_counts,
        error_memory, params, estimate, mixed, lists_v, g_v, act_v, cot_v,
    )
    delta = delta_rows(base, match, arrived)
    first, second = exchange(delta, silos)
    error_out, estimate_out, mixed_pre, params_pre, spread = own_updates(
        shards, silos, per_row, error_memory.shape, estimate.shape,
        lists_v, g_v, err_v, p_v, e_v, m_v, delta, [mine, *arrived],
    )
    mixed_out, params_out = final(per_row, mixed.shape, mixed_pre, params_pre, spread, first, second)
    return params_out, estimate_out, mixed_out, error_out


def solution(mesh):
    in_specs = (
        P(("silo", "shard"), None),
        P(("silo", "shard"), None),
        P("silo", "shard", None, None),
        P("silo", "shard", None),
        P("silo", "shard", None),
        P("silo", "shard", None),
        P("silo", None, None, None),
        P("silo", None, None),
        P(None, "shard", None),
        P(None, "shard"),
    )
    out_specs = (
        P("silo", "shard", None),
        P("silo", "shard", None),
        P("silo", "shard", None),
        P("silo", "shard", None, None),
    )
    return jax.shard_map(body, mesh=mesh, in_specs=in_specs, out_specs=out_specs, check_vma=False)
```

```python
import functools

import jax
import jax.numpy as jnp
from jax import lax
from jax.experimental import pallas as pl
from jax.experimental.pallas import tpu as pltpu
from jax.sharding import PartitionSpec as P

LEARN_RATE = 0.25
CONSENSUS = 0.5
MIX_WEIGHT = 1.0 / 3.0

F32, BF16, I32 = jnp.float32, jnp.bfloat16, jnp.int32
ANY = pl.BlockSpec(memory_space=pl.ANY)
IN_VMEM = pl.BlockSpec(memory_space=pltpu.VMEM)
MIB = 1 << 20


def dot(a, b, dims=((1,), (0,))):
    return lax.dot_general(a, b, (dims, ((), ())), preferred_element_type=F32)


def as_column(row):
    n = row.shape[1]
    eye = lax.broadcasted_iota(I32, (n, n), 0) == lax.broadcasted_iota(I32, (n, n), 1)
    spread = jnp.where(eye, jnp.broadcast_to(row.astype(F32), (n, n)), 0.0)
    return jnp.sum(spread, axis=1, keepdims=True).astype(I32)


def split(rows):
    high = rows.astype(BF16)
    return jnp.concatenate([high, (rows - high.astype(F32)).astype(BF16)], axis=0)


def pick(choice, rows):
    return dot(jnp.concatenate([choice, choice], axis=1), rows)


def onehot(mask):
    return jnp.where(mask, 1.0, 0.0).astype(BF16)


def divide(value, by):
    return (value * ((1 << 16) // by + 1)) >> 16


TILE = 128


def owner_tiles(shards, width_out):
    rows = width_out // shards
    return max(-(-(owner + 1) * rows // TILE) - owner * rows // TILE for owner in range(shards))


def first_tile(me, shards, width_out):
    last = width_out // TILE - owner_tiles(shards, width_out)
    return jnp.minimum(lax.div(me * (width_out // shards), TILE), last)


def rows_kernel(shards, silos, own_blocks, per_row, scale, lists, counts, g_lists, g_counts, act, cot, err, *refs):
    grad_rows, err_rows = refs[:2]
    (act_v, cot_v, own_match, match, kept_hot, own_hot, spread, row_table, g_table,
     list_s, count_s, gc_s, lists_v, g_v, sems) = refs[2:]
    me = lax.axis_index("shard")
    silo = lax.axis_index("silo")
    slots = lists_v.shape[2]
    g_slots = g_v.shape[2]
    width = err_rows.shape[1]
    parts = 4
    depth = act_v.shape[0] // parts
    small = [
        pltpu.make_async_copy(lists.at[0, me], list_s, sems.at[0]),
        pltpu.make_async_copy(lists.at[0], lists_v, sems.at[1]),
        pltpu.make_async_copy(counts.at[0], count_s, sems.at[2]),
        pltpu.make_async_copy(g_lists, g_v, sems.at[3]),
        pltpu.make_async_copy(g_counts, gc_s, sems.at[4]),
    ]
    cot_copy = pltpu.make_async_copy(cot, cot_v, sems.at[5])
    act_copies = [
        pltpu.make_async_copy(act.at[rows], act_v.at[rows], sems.at[6 + part])
        for part, rows in enumerate(pl.ds(part * depth, depth) for part in range(parts))
    ]
    for copy in [*small, cot_copy, *act_copies]:
        copy.start()
    for copy in small:
        copy.wait()

    columns, fills = [], []
    for shift in range(1, shards):
        owner = lax.rem(me + shift, shards)

        def fetch(slot, carry, owner=owner, shift=shift):
            block = owner * own_blocks + list_s[owner, slot]
            into = err_rows.at[pl.ds((shift - 1) * slots + slot, 1)]
            pltpu.make_async_copy(err.at[0, 0, pl.ds(block, 1)], into, sems.at[0]).start()
            return carry

        lax.fori_loop(0, slots, fetch, 0, unroll=slots)
        row = lists_v[me, pl.ds(owner, 1), :] + owner * own_blocks
        columns.append(as_column(row))
        slot_ids = lax.broadcasted_iota(I32, (slots, 1), 0)
        fills.append(slot_ids < count_s[me, owner])
    blocks = jnp.concatenate(columns, axis=0)
    filled = jnp.concatenate(fills, axis=0)
    out_row = divide(blocks, per_row)
    segment = blocks - out_row * per_row
    total = blocks.shape[0]
    chosen = onehot(lax.broadcasted_iota(I32, (total, cot_v.shape[1]), 1) == out_row)

    senders = [lists_v[lax.rem(me - shift + shards, shards), pl.ds(me, 1), :] for shift in range(shards)]
    gossiped = as_column(g_v[silo])
    sent = lax.broadcasted_iota(I32, (g_slots, 1), 0) < gc_s[silo]
    for shift, ids in enumerate(senders):
        same = onehot((gossiped == jnp.concatenate([ids, ids], axis=1)) & sent)
        if shift:
            match[:, 2 * (shift - 1) * slots : 2 * shift * slots] = same
        else:
            own_match[...] = same
    nblocks = shards * own_blocks
    step = TILE * per_row
    own_span = owner_tiles(shards, cot_v.shape[1]) * step
    start = first_tile(me, shards, cot_v.shape[1]) * step
    slot_ids = lax.broadcasted_iota(I32, (1, slots), 1)
    for owner in range(shards):
        place = lists_v[me, owner : owner + 1, :] + (owner * own_blocks - start)
        place = jnp.where(place < 0, place + nblocks, place)
        keep = slot_ids < count_s[me, owner]
        row_table[owner : owner + 1, :] = jnp.where(keep & (place < own_span), place, nblocks)
        row_table[shards + owner : shards + owner + 1, :] = jnp.where(
            keep & (place >= own_span), place - own_span, nblocks - own_span
        )
    place = lists_v[me, pl.ds(me, 1), :] + (me * own_blocks - start)
    row_table[2 * shards : 2 * shards + 1, :] = jnp.where(slot_ids < count_s[me, me], place, nblocks)
    out_rows = own_blocks // per_row
    chunks = per_row * width // 128
    row = divide(g_v[silo], per_row)
    place = (g_v[silo] - row * per_row) * (width // 128 * out_rows) + row
    sent = lax.broadcasted_iota(I32, (1, g_slots), 1) < gc_s[silo]
    g_table[...] = jnp.where(sent, place, chunks * out_rows)
    first, second = neighbours(silo, silos)
    for ids, into in (
        (jnp.concatenate(senders, axis=1), kept_hot),
        (g_v[silo], own_hot),
        (jnp.concatenate([g_v[first], g_v[second]], axis=1), spread),
    ):
        for part in range(per_row):
            here = lax.broadcasted_iota(I32, (out_rows, ids.shape[1]), 0) * per_row + part
            into[part * out_rows : (part + 1) * out_rows, :] = onehot(here == ids)

    cot_copy.wait()
    picked = dot(chosen, cot_v[...], ((1,), (1,))).astype(BF16)
    acc = jnp.zeros((total, act_v.shape[1]), F32)
    for part, copy in enumerate(act_copies):
        copy.wait()
        acc = acc + dot(picked[:, part * depth : (part + 1) * depth], act_v[part * depth : (part + 1) * depth, :])
    grad = jnp.zeros((total, width), F32)
    for part in range(per_row):
        grad = jnp.where(segment == part, acc[:, part * width : (part + 1) * width], grad)
    grad_rows[...] = jnp.where(filled, grad * scale, 0.0)
    pltpu.make_async_copy(err_rows, err_rows, sems.at[0]).wait()
    err_rows[...] = jnp.where(filled, err_rows[...], 0.0)


def moving_rows(shards, silos, own_blocks, per_row, scale, lists, counts, g_lists, g_counts, act, cot, err):
    slots = lists.shape[3]
    g_slots = g_lists.shape[2]
    width = err.shape[3]
    return pl.pallas_call(
        functools.partial(rows_kernel, shards, silos, own_blocks, per_row, scale),
        name="moving_rows",
        in_specs=[ANY] * 7,
        out_specs=[IN_VMEM] * 11,
        out_shape=[pltpu.VMEM(((shards - 1) * slots, width), F32)] * 2
        + [
            pltpu.VMEM(act.shape, BF16),
            pltpu.VMEM(cot.shape, BF16),
            pltpu.VMEM((g_slots, 2 * slots), BF16),
            pltpu.VMEM((g_slots, 2 * (shards - 1) * slots), BF16),
            pltpu.VMEM((own_blocks, shards * slots), BF16),
            pltpu.VMEM((own_blocks, g_slots), BF16),
            pltpu.VMEM((own_blocks, 2 * g_slots), BF16),
            pltpu.VMEM((2 * shards + 1, slots), I32),
            pltpu.VMEM((1, g_slots), I32),
        ],
        scratch_shapes=[
            pltpu.SMEM((shards, slots), I32),
            pltpu.SMEM((shards, shards), I32),
            pltpu.SMEM(g_counts.shape, I32),
            pltpu.VMEM(lists.shape[1:], I32),
            pltpu.VMEM(g_lists.shape, I32),
            pltpu.SemaphoreType.DMA((10,)),
        ],
        compiler_params=pltpu.CompilerParams(vmem_limit_bytes=16 * MIB),
    )(lists, counts, g_lists, g_counts, act, cot, err)


def sum_kernel(grad_rows, err_rows, *outs):
    slots = outs[0].shape[0]
    for place, out in enumerate(outs):
        rows = slice(place * slots, (place + 1) * slots)
        out[...] = err_rows[rows, :] + grad_rows[rows, :]


def outgoing_rows(shards, grad_rows, err_rows):
    shape = (grad_rows.shape[0] // (shards - 1), grad_rows.shape[1])
    return pl.pallas_call(
        sum_kernel,
        name="outgoing_rows",
        in_specs=[IN_VMEM] * 2,
        out_specs=[IN_VMEM] * (shards - 1),
        out_shape=[pltpu.VMEM(shape, F32)] * (shards - 1),
        compiler_params=pltpu.CompilerParams(vmem_limit_bytes=8 * MIB),
        cost_estimate=pl.CostEstimate(flops=10**10, bytes_accessed=3 * 10**7, transcendentals=0),
    )(grad_rows, err_rows)


def load_memory(err, err_v, tiles, step, into, sems):
    copies = [
        pltpu.make_async_copy(
            err.at[0, 0, pl.ds(pl.multiple_of(tile * step, 8), step), pl.ds(half * 128, 128)],
            err_v.at[half, pl.ds(place * step, step)],
            sems[half],
        )
        for place, tile in enumerate(tiles, into)
        for half in range(err_v.shape[0])
    ]
    for copy in copies:
        copy.start()
    return copies


def tile_gradient(cot_v, act_v, scale, tile):
    columns = pl.ds(pl.multiple_of(tile * TILE, TILE), TILE)
    return dot(cot_v[:, columns], act_v[...], ((0,), (0,))) * scale


def pieces(grad, place, per_row, halves):
    for seg in range(per_row):
        for half in range(halves):
            lane = (seg * halves + half) * 128
            where = pl.ds(place * TILE * per_row + seg, TILE, stride=per_row)
            yield (half, where, slice(None)), grad[:, lane : lane + 128]


def clear_rows(err_v, table_s, first, shards):
    for owner in range(first, first + shards):

        def clear(slot, carry, owner=owner):
            block = table_s[owner, slot]
            for half in range(err_v.shape[0]):
                err_v[half, pl.ds(block, 1), :] = jnp.zeros((1, 128), F32)
            return carry

        lax.fori_loop(0, table_s.shape[1], clear, 0, unroll=table_s.shape[1])


def gradient_kernel(
    shards, per_row, scale,
    err, p_v, e_v, own_match, act_v, cot_v, row_table, g_table,
    mine, base, err_v, table_s, g_s, rows_v, grad_v, drift_v, sems,
):
    me = lax.axis_index("shard")
    slots = mine.shape[0]
    g_slots = base.shape[0]
    halves = err_v.shape[0]
    out_rows = p_v.shape[1]
    chunks = p_v.shape[2] // 128
    step = TILE * per_row
    tiles = cot_v.shape[1] // TILE
    count = owner_tiles(shards, cot_v.shape[1])
    start = first_tile(me, shards, cot_v.shape[1])
    small = [
        pltpu.make_async_copy(row_table, table_s, sems.at[0]),
        pltpu.make_async_copy(g_table, g_s, sems.at[1]),
    ]
    for copy in small:
        copy.start()
    own_memory, other_memory = (
        load_memory(
            err, err_v, [lax.rem(start + place, tiles) for place in places], step, places[0],
            [sems.at[sem + half] for half in range(halves)],
        )
        for sem, places in ((2, range(count)), (2 + halves, range(count, tiles)))
    )

    def store(place, carry):
        for where, piece in pieces(tile_gradient(cot_v, act_v, scale, start + place), place, per_row, halves):
            grad_v[where] = piece
        return carry

    lax.fori_loop(0, count, store, 0)
    for chunk in range(chunks):
        lanes = slice(chunk * 128, (chunk + 1) * 128)
        drift_v[chunk * out_rows : (chunk + 1) * out_rows, :] = p_v[0, :, lanes] - e_v[0, :, lanes]
    for half in range(halves):
        nothing = (chunks + half) * out_rows
        drift_v[nothing : nothing + 8, :] = jnp.zeros((8, 128), F32)
        err_v[half, tiles * step :, :] = jnp.zeros((8, 128), F32)
    for copy in small:
        copy.wait()

    def gather(slot, carry):
        for half in range(halves):
            rows_v[half, pl.ds(slot, 1), :] = drift_v[pl.ds(g_s[0, slot] + half * out_rows, 1), :]
        return carry

    lax.fori_loop(0, g_slots, gather, 0, unroll=g_slots)
    base[...] = jnp.concatenate([rows_v[half, :g_slots] for half in range(halves)], axis=1)
    for copy in own_memory:
        copy.wait()
    for half in range(halves):
        err_v[half, : count * step, :] = err_v[half, : count * step, :] + grad_v[half]

    def take(slot, carry):
        for half in range(halves):
            rows_v[half, pl.ds(slot, 1), :] = err_v[half, pl.ds(table_s[2 * shards, slot], 1), :]
        return carry

    lax.fori_loop(0, slots, take, 0, unroll=slots)
    mine[...] = jnp.concatenate([rows_v[half, :slots] for half in range(halves)], axis=1)
    clear_rows(err_v, table_s, 0, shards)
    base[...] = base[...] - LEARN_RATE * dot(own_match[...], split(mine[...]))
    for copy in other_memory:
        copy.wait()


def gradient(shards, per_row, scale, err, params, estimate, own_match, act_v, cot_v, row_table, g_table):
    slots = row_table.shape[1]
    g_slots = g_table.shape[1]
    nblocks, width = err.shape[2:]
    halves = width // 128
    count = owner_tiles(shards, cot_v.shape[1])
    step = TILE * per_row
    chunks = params.shape[2] // 128
    return pl.pallas_call(
        functools.partial(gradient_kernel, shards, per_row, scale),
        name="gradient",
        in_specs=[ANY] + [IN_VMEM] * 7,
        out_specs=[IN_VMEM] * 3,
        out_shape=[
            pltpu.VMEM((slots, width), F32),
            pltpu.VMEM((g_slots, width), F32),
            pltpu.VMEM((halves, nblocks + 8, 128), F32),
        ],
        scratch_shapes=[
            pltpu.SMEM(row_table.shape, I32),
            pltpu.SMEM(g_table.shape, I32),
            pltpu.VMEM((halves, max(slots, g_slots), 128), F32),
            pltpu.VMEM((halves, count * step, 128), F32),
            pltpu.VMEM(((chunks + halves - 1) * params.shape[1] + 8, 128), F32),
            pltpu.SemaphoreType.DMA((2 + 2 * halves,)),
        ],
        compiler_params=pltpu.CompilerParams(vmem_limit_bytes=16 * MIB),
    )(err, params, estimate, own_match, act_v, cot_v, row_table, g_table)


def delta_kernel(base, match, *refs):
    *arrived, out, again = refs
    rows = jnp.concatenate([split(each[...]) for each in arrived], axis=0)
    total = base[...] - LEARN_RATE * dot(match[...], rows)
    out[: total.shape[0]] = total
    out[total.shape[0] :] = jnp.zeros((8, total.shape[1]), F32)
    again[...] = total


def delta_rows(base, match, arrived):
    return pl.pallas_call(
        delta_kernel,
        name="delta_rows",
        in_specs=[IN_VMEM] * (2 + len(arrived)),
        out_specs=[IN_VMEM] * 2,
        out_shape=[pltpu.VMEM((base.shape[0] + 8, base.shape[1]), F32), pltpu.VMEM(base.shape, F32)],
        compiler_params=pltpu.CompilerParams(vmem_limit_bytes=8 * MIB),
    )(base, match, *arrived)


def own_kernel(
    shards, per_row, scale,
    p_v, e_v, m_v, err_v, act_v, cot_v, row_table, kept_hot, own_hot, delta, *refs
):
    kept = refs[:shards]
    err_out, est_out, mixed_pre, params_pre, table_s, rest_v, est_v, sems = refs[shards:]
    me = lax.axis_index("shard")
    width = delta.shape[1]
    halves = err_v.shape[0]
    out_rows = p_v.shape[1]
    step = TILE * per_row
    tiles = cot_v.shape[1] // TILE
    count = owner_tiles(shards, cot_v.shape[1])
    start = first_tile(me, shards, cot_v.shape[1])
    small = pltpu.make_async_copy(row_table, table_s, sems.at[0])
    small.start()
    copies = []

    def store_memory(source, first, places):
        for place in places:
            tile = lax.rem(start + place, tiles)
            for half in range(halves):
                copy = pltpu.make_async_copy(
                    source.at[half, pl.ds((place - first) * step, step)],
                    err_out.at[0, 0, pl.ds(pl.multiple_of(tile * step, 8), step), pl.ds(half * 128, 128)],
                    sems.at[1 + half],
                )
                copy.start()
                copies.append(copy)

    store_memory(err_v, 0, range(count))

    def store(place, carry):
        grad = tile_gradient(cot_v, act_v, scale, lax.rem(start + count + place, tiles))
        for where, piece in pieces(grad, place, per_row, halves):
            rest_v[where] = piece
        return carry

    lax.fori_loop(0, tiles - count, store, 0)
    rest = (tiles - count) * step
    for half in range(halves):
        rest_v[half, :rest, :] = rest_v[half, :rest, :] + err_v[half, count * step : tiles * step, :]
    small.wait()
    clear_rows(rest_v, table_s, shards, shards)
    store_memory(rest_v, count, range(count, tiles))

    kept_parts = split(jnp.concatenate([rows[...] for rows in kept], axis=0))
    delta_parts = split(delta[...])
    for part in range(per_row):
        lanes = slice(part * width, (part + 1) * width)
        blocks = slice(part * out_rows, (part + 1) * out_rows)
        grad = pick(kept_hot[blocks, :], kept_parts)
        change = pick(own_hot[blocks, :], delta_parts)
        half_step = p_v[0, :, lanes] - LEARN_RATE * grad
        est = e_v[0, :, lanes] + change
        mix = m_v[0, :, lanes] + MIX_WEIGHT * change
        est_v[:, lanes] = est
        copy = pltpu.make_async_copy(est_v.at[:, lanes], est_out.at[0, :, lanes], sems.at[1 + halves + part])
        copy.start()
        copies.append(copy)
        mixed_pre[:, lanes] = mix
        params_pre[:, lanes] = half_step + CONSENSUS * (mix - est)
    for copy in copies:
        copy.wait()


def own_updates(
    shards, per_row, scale, err_shape, params, estimate, mixed, err_v, act_v, cot_v, row_table, kept_hot, own_hot, delta, kept
):
    owned = mixed.shape[1:]
    halves = err_v.shape[0]
    others = cot_v.shape[1] // TILE - owner_tiles(shards, cot_v.shape[1])
    return pl.pallas_call(
        functools.partial(own_kernel, shards, per_row, scale),
        name="own_updates",
        in_specs=[IN_VMEM] * (10 + shards),
        out_specs=[ANY, ANY, IN_VMEM, IN_VMEM],
        out_shape=[
            pltpu.HBM(err_shape, F32),
            pltpu.HBM(mixed.shape, F32),
            pltpu.VMEM(owned, F32),
            pltpu.VMEM(owned, F32),
        ],
        scratch_shapes=[
            pltpu.SMEM(row_table.shape, I32),
            pltpu.VMEM((halves, others * TILE * per_row + 8, 128), F32),
            pltpu.VMEM(owned, F32),
            pltpu.SemaphoreType.DMA((1 + halves + per_row,)),
        ],
        compiler_params=pltpu.CompilerParams(vmem_limit_bytes=16 * MIB),
    )(params, estimate, mixed, err_v, act_v, cot_v, row_table, kept_hot, own_hot, delta, *kept)


def final_kernel(per_row, mixed_pre, params_pre, spread, first, second, mixed_out, params_out, m_v, p_v, sems):
    out_rows = m_v.shape[0]
    width = m_v.shape[1] // per_row
    slots = second.shape[0]
    rows = split(jnp.concatenate([first[:slots, :], second[...]], axis=0))
    depth = spread.shape[1]
    copies = []
    for part in range(per_row):
        lanes = slice(part * width, (part + 1) * width)
        choice = spread[part * out_rows : (part + 1) * out_rows, :]
        change = dot(choice, rows[:depth]) + dot(choice, rows[depth:])
        m_v[:, lanes] = mixed_pre[:, lanes] + MIX_WEIGHT * change
        p_v[:, lanes] = params_pre[:, lanes] + (CONSENSUS * MIX_WEIGHT) * change
        pair = [
            pltpu.make_async_copy(m_v.at[:, lanes], mixed_out.at[0, :, lanes], sems.at[2 * part]),
            pltpu.make_async_copy(p_v.at[:, lanes], params_out.at[0, :, lanes], sems.at[2 * part + 1]),
        ]
        for copy in pair:
            copy.start()
        copies += pair
    for copy in copies:
        copy.wait()


def final(per_row, shape, mixed_pre, params_pre, spread, first, second):
    return pl.pallas_call(
        functools.partial(final_kernel, per_row),
        name="neighbours",
        in_specs=[IN_VMEM] * 5,
        out_specs=[ANY] * 2,
        out_shape=[pltpu.HBM(shape, F32)] * 2,
        scratch_shapes=[
            pltpu.VMEM(mixed_pre.shape, F32),
            pltpu.VMEM(mixed_pre.shape, F32),
            pltpu.SemaphoreType.DMA((2 * per_row,)),
        ],
        compiler_params=pltpu.CompilerParams(vmem_limit_bytes=20 * MIB),
    )(mixed_pre, params_pre, spread, first, second)


def neighbours(silo, silos):
    lower, upper = lax.rem(silo + silos - 1, silos), lax.rem(silo + 1, silos)
    if silos % 2:
        return lower, upper
    even = lax.rem(silo, 2) == 0
    return jnp.where(even, lower, upper), jnp.where(even, upper, lower)


def exchange(rows, again, silos):
    if silos % 2:
        routes = [[(a, (a + 1) % silos) for a in range(silos)], [(a, (a - 1) % silos) for a in range(silos)]]
    else:
        routes = [
            [(a, (a + 1 if a % 2 else a - 1) % silos) for a in range(silos)],
            [(a, a ^ 1) for a in range(silos)],
        ]
    far = lax.ppermute(rows, "silo", routes[0])
    near = lax.ppermute(again, "silo", routes[1])
    return far, near


def body(
    activ, cotangent, error_memory, params, estimate, mixed,
    kept_blocks, kept_counts, gossip_blocks, gossip_counts,
):
    shards = lax.axis_size("shard")
    silos = lax.axis_size("silo")
    nblocks, block_len = error_memory.shape[2:]
    own_blocks = nblocks // shards
    per_row = activ.shape[1] // block_len
    scale = activ.shape[1] ** (-0.5)
    activ, cotangent, error_memory, kept_blocks, kept_counts, gossip_blocks, gossip_counts = (
        pltpu.with_memory_space_constraint(array, pltpu.HBM)
        for array in (
            activ, cotangent, error_memory,
            kept_blocks, kept_counts, gossip_blocks, gossip_counts.reshape(silos),
        )
    )
    grad_rows, err_rows, act_v, cot_v, own_match, match, kept_hot, own_hot, spread, row_table, g_table = moving_rows(
        shards, silos, own_blocks, per_row, scale,
        kept_blocks, kept_counts, gossip_blocks, gossip_counts, activ, cotangent, error_memory,
    )
    outgoing = outgoing_rows(shards, grad_rows, err_rows)
    arrived = [
        lax.ppermute(rows, "shard", [(r, (r + shift) % shards) for r in range(shards)])
        for shift, rows in enumerate(outgoing, 1)
    ]
    params, estimate, mixed, row_table = lax.optimization_barrier((params, estimate, mixed, row_table))
    params, estimate, mixed = (
        pltpu.with_memory_space_constraint(array, pltpu.VMEM) for array in (params, estimate, mixed)
    )
    mine, base, err_v = gradient(
        shards, per_row, scale, error_memory, params, estimate, own_match, act_v, cot_v, row_table, g_table
    )
    delta, again = delta_rows(base, match, arrived)
    first, second = exchange(delta, again, silos)
    error_out, estimate_out, mixed_pre, params_pre = own_updates(
        shards, per_row, scale, error_memory.shape, params, estimate, mixed,
        err_v, act_v, cot_v, row_table, kept_hot, own_hot, again, [mine, *arrived],
    )
    mixed_out, params_out = final(per_row, mixed.shape, mixed_pre, params_pre, spread, first, second)
    return params_out, estimate_out, mixed_out, error_out


def solution(mesh):
    in_specs = (
        P(("silo", "shard"), None),
        P(("silo", "shard"), None),
        P("silo", "shard", None, None),
        P("silo", "shard", None),
        P("silo", "shard", None),
        P("silo", "shard", None),
        P("silo", None, None, None),
        P("silo", None, None),
        P(None, "shard", None),
        P(None, "shard"),
    )
    out_specs = (
        P("silo", "shard", None),
        P("silo", "shard", None),
        P("silo", "shard", None),
        P("silo", "shard", None, None),
    )
    return jax.shard_map(body, mesh=mesh, in_specs=in_specs, out_specs=out_specs, check_vma=False)
```

```python
import functools

import jax
import jax.numpy as jnp
from jax import lax
from jax.experimental import pallas as pl
from jax.experimental.pallas import tpu as pltpu
from jax.sharding import PartitionSpec as P

LEARN_RATE = 0.25
CONSENSUS = 0.5
MIX_WEIGHT = 1.0 / 3.0

F32, BF16, I32 = jnp.float32, jnp.bfloat16, jnp.int32
ANY = pl.BlockSpec(memory_space=pl.ANY)
IN_VMEM = pl.BlockSpec(memory_space=pltpu.VMEM)
MIB = 1 << 20


def dot(a, b, dims=((1,), (0,))):
    return lax.dot_general(a, b, (dims, ((), ())), preferred_element_type=F32)


def as_column(row):
    n = row.shape[1]
    eye = lax.broadcasted_iota(I32, (n, n), 0) == lax.broadcasted_iota(I32, (n, n), 1)
    spread = jnp.where(eye, jnp.broadcast_to(row.astype(F32), (n, n)), 0.0)
    return jnp.sum(spread, axis=1, keepdims=True).astype(I32)


def split(rows):
    high = rows.astype(BF16)
    return jnp.concatenate([high, (rows - high.astype(F32)).astype(BF16)], axis=0)


def pick(choice, rows):
    return dot(jnp.concatenate([choice, choice], axis=1), rows)


def onehot(mask):
    return jnp.where(mask, 1.0, 0.0).astype(BF16)


def divide(value, by):
    return (value * ((1 << 16) // by + 1)) >> 16


TILE = 128


def owner_tiles(shards, width_out):
    rows = width_out // shards
    return max(-(-(owner + 1) * rows // TILE) - owner * rows // TILE for owner in range(shards))


def first_tile(me, shards, width_out):
    last = width_out // TILE - owner_tiles(shards, width_out)
    return jnp.minimum(lax.div(me * (width_out // shards), TILE), last)


def rows_kernel(shards, silos, own_blocks, per_row, scale, lists, counts, g_lists, g_counts, act, cot, err, *refs):
    grad_rows, err_rows = refs[:2]
    (act_v, cot_v, own_match, match, kept_hot, own_hot, spread, row_table, g_table,
     list_s, count_s, gc_s, lists_v, g_v, sems) = refs[2:]
    me = lax.axis_index("shard")
    silo = lax.axis_index("silo")
    slots = lists_v.shape[2]
    g_slots = g_v.shape[2]
    width = err_rows.shape[1]
    parts = 4
    depth = act_v.shape[0] // parts
    small = [
        pltpu.make_async_copy(lists.at[0, me], list_s, sems.at[0]),
        pltpu.make_async_copy(lists.at[0], lists_v, sems.at[1]),
        pltpu.make_async_copy(counts.at[0], count_s, sems.at[2]),
        pltpu.make_async_copy(g_lists, g_v, sems.at[3]),
        pltpu.make_async_copy(g_counts, gc_s, sems.at[4]),
    ]
    cot_copy = pltpu.make_async_copy(cot, cot_v, sems.at[5])
    act_copies = [
        pltpu.make_async_copy(act.at[rows], act_v.at[rows], sems.at[6 + part])
        for part, rows in enumerate(pl.ds(part * depth, depth) for part in range(parts))
    ]
    for copy in [*small, cot_copy, *act_copies]:
        copy.start()
    for copy in small:
        copy.wait()

    columns, fills = [], []
    for shift in range(1, shards):
        owner = lax.rem(me + shift, shards)

        def fetch(slot, carry, owner=owner, shift=shift):
            block = owner * own_blocks + list_s[owner, slot]
            into = err_rows.at[pl.ds((shift - 1) * slots + slot, 1)]
            pltpu.make_async_copy(err.at[0, 0, pl.ds(block, 1)], into, sems.at[0]).start()
            return carry

        lax.fori_loop(0, slots, fetch, 0, unroll=slots)
        row = lists_v[me, pl.ds(owner, 1), :] + owner * own_blocks
        columns.append(as_column(row))
        slot_ids = lax.broadcasted_iota(I32, (slots, 1), 0)
        fills.append(slot_ids < count_s[me, owner])
    blocks = jnp.concatenate(columns, axis=0)
    filled = jnp.concatenate(fills, axis=0)
    out_row = divide(blocks, per_row)
    segment = blocks - out_row * per_row
    total = blocks.shape[0]
    chosen = onehot(lax.broadcasted_iota(I32, (total, cot_v.shape[1]), 1) == out_row)

    senders = [lists_v[lax.rem(me - shift + shards, shards), pl.ds(me, 1), :] for shift in range(shards)]
    gossiped = as_column(g_v[silo])
    sent = lax.broadcasted_iota(I32, (g_slots, 1), 0) < gc_s[silo]
    for shift, ids in enumerate(senders):
        same = onehot((gossiped == jnp.concatenate([ids, ids], axis=1)) & sent)
        if shift:
            match[:, 2 * (shift - 1) * slots : 2 * shift * slots] = same
        else:
            own_match[...] = same
    nblocks = shards * own_blocks
    step = TILE * per_row
    own_span = owner_tiles(shards, cot_v.shape[1]) * step
    start = first_tile(me, shards, cot_v.shape[1]) * step
    slot_ids = lax.broadcasted_iota(I32, (1, slots), 1)
    for owner in range(shards):
        place = lists_v[me, owner : owner + 1, :] + (owner * own_blocks - start)
        place = jnp.where(place < 0, place + nblocks, place)
        keep = slot_ids < count_s[me, owner]
        row_table[owner : owner + 1, :] = jnp.where(keep & (place < own_span), place, nblocks)
        row_table[shards + owner : shards + owner + 1, :] = jnp.where(
            keep & (place >= own_span), place - own_span, nblocks - own_span
        )
    place = lists_v[me, pl.ds(me, 1), :] + (me * own_blocks - start)
    row_table[2 * shards : 2 * shards + 1, :] = jnp.where(slot_ids < count_s[me, me], place, nblocks)
    out_rows = own_blocks // per_row
    chunks = per_row * width // 128
    row = divide(g_v[silo], per_row)
    place = (g_v[silo] - row * per_row) * (width // 128 * out_rows) + row
    sent = lax.broadcasted_iota(I32, (1, g_slots), 1) < gc_s[silo]
    g_table[...] = jnp.where(sent, place, chunks * out_rows)
    first, second = neighbours(silo, silos)
    for ids, into in (
        (jnp.concatenate(senders, axis=1), kept_hot),
        (g_v[silo], own_hot),
        (jnp.concatenate([g_v[first], g_v[second]], axis=1), spread),
    ):
        for part in range(per_row):
            here = lax.broadcasted_iota(I32, (out_rows, ids.shape[1]), 0) * per_row + part
            into[part * out_rows : (part + 1) * out_rows, :] = onehot(here == ids)

    cot_copy.wait()
    picked = dot(chosen, cot_v[...], ((1,), (1,))).astype(BF16)
    acc = jnp.zeros((total, act_v.shape[1]), F32)
    for part, copy in enumerate(act_copies):
        copy.wait()
        acc = acc + dot(picked[:, part * depth : (part + 1) * depth], act_v[part * depth : (part + 1) * depth, :])
    grad = jnp.zeros((total, width), F32)
    for part in range(per_row):
        grad = jnp.where(segment == part, acc[:, part * width : (part + 1) * width], grad)
    grad_rows[...] = jnp.where(filled, grad * scale, 0.0)
    pltpu.make_async_copy(err_rows, err_rows, sems.at[0]).wait()
    err_rows[...] = jnp.where(filled, err_rows[...], 0.0)


def moving_rows(shards, silos, own_blocks, per_row, scale, lists, counts, g_lists, g_counts, act, cot, err):
    slots = lists.shape[3]
    g_slots = g_lists.shape[2]
    width = err.shape[3]
    return pl.pallas_call(
        functools.partial(rows_kernel, shards, silos, own_blocks, per_row, scale),
        name="moving_rows",
        in_specs=[ANY] * 7,
        out_specs=[IN_VMEM] * 11,
        out_shape=[pltpu.VMEM(((shards - 1) * slots, width), F32)] * 2
        + [
            pltpu.VMEM(act.shape, BF16),
            pltpu.VMEM(cot.shape, BF16),
            pltpu.VMEM((g_slots, 2 * slots), BF16),
            pltpu.VMEM((g_slots, 2 * (shards - 1) * slots), BF16),
            pltpu.VMEM((own_blocks, shards * slots), BF16),
            pltpu.VMEM((own_blocks, g_slots), BF16),
            pltpu.VMEM((own_blocks, 2 * g_slots), BF16),
            pltpu.VMEM((2 * shards + 1, slots), I32),
            pltpu.VMEM((1, g_slots), I32),
        ],
        scratch_shapes=[
            pltpu.SMEM((shards, slots), I32),
            pltpu.SMEM((shards, shards), I32),
            pltpu.SMEM(g_counts.shape, I32),
            pltpu.VMEM(lists.shape[1:], I32),
            pltpu.VMEM(g_lists.shape, I32),
            pltpu.SemaphoreType.DMA((10,)),
        ],
        compiler_params=pltpu.CompilerParams(vmem_limit_bytes=16 * MIB),
    )(lists, counts, g_lists, g_counts, act, cot, err)


def early_tiles(me, silo):
    return jnp.where((me == 0) & (silo < 2), 2, 0)


def sum_kernel(shards, per_row, scale, grad_rows, err_rows, act_v, cot_v, *outs):
    *outs, grad_v = outs
    me = lax.axis_index("shard")
    start = first_tile(me, shards, cot_v.shape[1])

    def store(place, carry):
        grad = tile_gradient(cot_v, act_v, scale, start + place)
        for where, piece in pieces(grad, place, per_row, grad_v.shape[0]):
            grad_v[where] = piece
        return carry

    lax.fori_loop(0, early_tiles(me, lax.axis_index("silo")), store, 0)
    slots = outs[0].shape[0]
    for place, out in enumerate(outs):
        rows = slice(place * slots, (place + 1) * slots)
        out[...] = err_rows[rows, :] + grad_rows[rows, :]


def outgoing_rows(shards, per_row, scale, grad_rows, err_rows, act_v, cot_v):
    shape = (grad_rows.shape[0] // (shards - 1), grad_rows.shape[1])
    return pl.pallas_call(
        functools.partial(sum_kernel, shards, per_row, scale),
        name="outgoing_rows",
        in_specs=[IN_VMEM] * 4,
        out_specs=[IN_VMEM] * shards,
        out_shape=[pltpu.VMEM(shape, F32)] * (shards - 1)
        + [pltpu.VMEM((shape[1] // 128, owner_tiles(shards, cot_v.shape[1]) * TILE * per_row, 128), F32)],
        compiler_params=pltpu.CompilerParams(vmem_limit_bytes=8 * MIB),
        cost_estimate=pl.CostEstimate(flops=10**10, bytes_accessed=3 * 10**7, transcendentals=0),
    )(grad_rows, err_rows, act_v, cot_v)


def load_memory(err, err_v, tiles, step, into, sems):
    copies = [
        pltpu.make_async_copy(
            err.at[0, 0, pl.ds(pl.multiple_of(tile * step, 8), step), pl.ds(half * 128, 128)],
            err_v.at[half, pl.ds(place * step, step)],
            sems[half],
        )
        for place, tile in enumerate(tiles, into)
        for half in range(err_v.shape[0])
    ]
    for copy in copies:
        copy.start()
    return copies


def tile_gradient(cot_v, act_v, scale, tile):
    columns = pl.ds(pl.multiple_of(tile * TILE, TILE), TILE)
    return dot(cot_v[:, columns], act_v[...], ((0,), (0,))) * scale


def pieces(grad, place, per_row, halves):
    for seg in range(per_row):
        for half in range(halves):
            lane = (seg * halves + half) * 128
            where = pl.ds(place * TILE * per_row + seg, TILE, stride=per_row)
            yield (half, where, slice(None)), grad[:, lane : lane + 128]


def clear_rows(err_v, table_s, first, shards):
    for owner in range(first, first + shards):

        def clear(slot, carry, owner=owner):
            block = table_s[owner, slot]
            for half in range(err_v.shape[0]):
                err_v[half, pl.ds(block, 1), :] = jnp.zeros((1, 128), F32)
            return carry

        lax.fori_loop(0, table_s.shape[1], clear, 0, unroll=table_s.shape[1])


def gradient_kernel(
    shards, per_row, scale,
    err, params, e_v, own_match, act_v, cot_v, row_table, g_table, _,
    mine, base, err_v, p_v, grad_v, table_s, g_s, rows_v, drift_v, sems,
):
    me = lax.axis_index("shard")
    slots = mine.shape[0]
    g_slots = base.shape[0]
    halves = err_v.shape[0]
    out_rows = e_v.shape[1]
    chunks = e_v.shape[2] // 128
    step = TILE * per_row
    tiles = cot_v.shape[1] // TILE
    count = owner_tiles(shards, cot_v.shape[1])
    start = first_tile(me, shards, cot_v.shape[1])
    small = [
        pltpu.make_async_copy(row_table, table_s, sems.at[0]),
        pltpu.make_async_copy(g_table, g_s, sems.at[1]),
    ]
    for copy in small:
        copy.start()

    def load(places, sem):
        order = [lax.rem(start + place, tiles) for place in places]
        return load_memory(err, err_v, order, step, places[0], [sems.at[sem + half] for half in range(halves)])

    own_memory = load(range(count), 3)
    p_copy = pltpu.make_async_copy(params, p_v, sems.at[2])
    p_copy.start()
    other_memory = load(range(count, tiles), 3 + halves)

    def store(place, carry):
        for where, piece in pieces(tile_gradient(cot_v, act_v, scale, start + place), place, per_row, halves):
            grad_v[where] = piece
        return carry

    lax.fori_loop(early_tiles(me, lax.axis_index("silo")), count, store, 0)
    for copy in small + own_memory:
        copy.wait()
    for half in range(halves):
        err_v[half, : count * step, :] = err_v[half, : count * step, :] + grad_v[half]
        err_v[half, tiles * step :, :] = jnp.zeros((8, 128), F32)

    def take(slot, carry):
        for half in range(halves):
            rows_v[half, pl.ds(slot, 1), :] = err_v[half, pl.ds(table_s[2 * shards, slot], 1), :]
        return carry

    lax.fori_loop(0, slots, take, 0, unroll=slots)
    mine[...] = jnp.concatenate([rows_v[half, :slots] for half in range(halves)], axis=1)
    clear_rows(err_v, table_s, 0, shards)
    p_copy.wait()
    for chunk in range(chunks):
        lanes = slice(chunk * 128, (chunk + 1) * 128)
        drift_v[chunk * out_rows : (chunk + 1) * out_rows, :] = p_v[0, :, lanes] - e_v[0, :, lanes]
    for half in range(halves):
        nothing = (chunks + half) * out_rows
        drift_v[nothing : nothing + 8, :] = jnp.zeros((8, 128), F32)

    def gather(slot, carry):
        for half in range(halves):
            rows_v[half, pl.ds(slot, 1), :] = drift_v[pl.ds(g_s[0, slot] + half * out_rows, 1), :]
        return carry

    lax.fori_loop(0, g_slots, gather, 0, unroll=g_slots)
    rows = jnp.concatenate([rows_v[half, :g_slots] for half in range(halves)], axis=1)
    base[...] = rows - LEARN_RATE * dot(own_match[...], split(mine[...]))
    for copy in other_memory:
        copy.wait()


def gradient(shards, per_row, scale, err, params, estimate, own_match, act_v, cot_v, row_table, g_table, grad_v):
    slots = row_table.shape[1]
    g_slots = own_match.shape[0]
    nblocks, width = err.shape[2:]
    halves = width // 128
    chunks = params.shape[2] // 128
    return pl.pallas_call(
        functools.partial(gradient_kernel, shards, per_row, scale),
        name="gradient",
        in_specs=[ANY] * 2 + [IN_VMEM] * 7,
        out_specs=[IN_VMEM] * 5,
        out_shape=[
            pltpu.VMEM((slots, width), F32),
            pltpu.VMEM((g_slots, width), F32),
            pltpu.VMEM((halves, nblocks + 8, 128), F32),
            pltpu.VMEM(params.shape, F32),
            pltpu.VMEM(grad_v.shape, F32),
        ],
        input_output_aliases={8: 4},
        scratch_shapes=[
            pltpu.SMEM(row_table.shape, I32),
            pltpu.SMEM(g_table.shape, I32),
            pltpu.VMEM((halves, max(slots, g_slots), 128), F32),
            pltpu.VMEM(((chunks + halves - 1) * params.shape[1] + 8, 128), F32),
            pltpu.SemaphoreType.DMA((3 + 2 * halves,)),
        ],
        compiler_params=pltpu.CompilerParams(vmem_limit_bytes=16 * MIB),
    )(err, params, estimate, own_match, act_v, cot_v, row_table, g_table, grad_v)


def delta_kernel(base, match, *refs):
    *arrived, out, again = refs
    rows = jnp.concatenate([split(each[...]) for each in arrived], axis=0)
    total = base[...] - LEARN_RATE * dot(match[...], rows)
    out[: total.shape[0]] = total
    out[total.shape[0] :] = jnp.zeros((8, total.shape[1]), F32)
    again[...] = total


def delta_rows(base, match, arrived):
    return pl.pallas_call(
        delta_kernel,
        name="delta_rows",
        in_specs=[IN_VMEM] * (2 + len(arrived)),
        out_specs=[IN_VMEM] * 2,
        out_shape=[pltpu.VMEM((base.shape[0] + 8, base.shape[1]), F32), pltpu.VMEM(base.shape, F32)],
        compiler_params=pltpu.CompilerParams(vmem_limit_bytes=8 * MIB),
    )(base, match, *arrived)


def own_kernel(
    shards, per_row, scale,
    p_v, e_v, m_v, err_v, act_v, cot_v, row_table, kept_hot, own_hot, delta, *refs
):
    kept = refs[:shards]
    err_out, est_out, mixed_pre, params_pre, table_s, rest_v, est_v, sems = refs[shards:]
    me = lax.axis_index("shard")
    width = delta.shape[1]
    halves = err_v.shape[0]
    out_rows = p_v.shape[1]
    step = TILE * per_row
    tiles = cot_v.shape[1] // TILE
    count = owner_tiles(shards, cot_v.shape[1])
    start = first_tile(me, shards, cot_v.shape[1])
    small = pltpu.make_async_copy(row_table, table_s, sems.at[0])
    small.start()
    copies = []

    def store_memory(source, first, places):
        for place in places:
            tile = lax.rem(start + place, tiles)
            for half in range(halves):
                copy = pltpu.make_async_copy(
                    source.at[half, pl.ds((place - first) * step, step)],
                    err_out.at[0, 0, pl.ds(pl.multiple_of(tile * step, 8), step), pl.ds(half * 128, 128)],
                    sems.at[1 + half],
                )
                copy.start()
                copies.append(copy)

    store_memory(err_v, 0, range(count))

    def store(place, carry):
        grad = tile_gradient(cot_v, act_v, scale, lax.rem(start + count + place, tiles))
        held = pieces(grad, count + place, per_row, halves)
        for (where, piece), (there, _) in zip(pieces(grad, place, per_row, halves), held):
            rest_v[where] = err_v[there] + piece
        return carry

    lax.fori_loop(0, tiles - count, store, 0)
    small.wait()
    clear_rows(rest_v, table_s, shards, shards)
    store_memory(rest_v, count, range(count, tiles))

    kept_parts = split(jnp.concatenate([rows[...] for rows in kept], axis=0))
    delta_parts = split(delta[...])
    for part in range(per_row):
        lanes = slice(part * width, (part + 1) * width)
        blocks = slice(part * out_rows, (part + 1) * out_rows)
        grad = pick(kept_hot[blocks, :], kept_parts)
        change = pick(own_hot[blocks, :], delta_parts)
        half_step = p_v[0, :, lanes] - LEARN_RATE * grad
        est = e_v[0, :, lanes] + change
        mix = m_v[0, :, lanes] + MIX_WEIGHT * change
        est_v[:, lanes] = est
        copy = pltpu.make_async_copy(est_v.at[:, lanes], est_out.at[0, :, lanes], sems.at[1 + halves + part])
        copy.start()
        copies.append(copy)
        mixed_pre[:, lanes] = mix
        params_pre[:, lanes] = half_step + CONSENSUS * (mix - est)
    for copy in copies:
        copy.wait()


def own_updates(
    shards, per_row, scale, err_shape, params, estimate, mixed, err_v, act_v, cot_v, row_table, kept_hot, own_hot, delta, kept
):
    owned = mixed.shape[1:]
    halves = err_v.shape[0]
    others = cot_v.shape[1] // TILE - owner_tiles(shards, cot_v.shape[1])
    return pl.pallas_call(
        functools.partial(own_kernel, shards, per_row, scale),
        name="own_updates",
        in_specs=[IN_VMEM] * (10 + shards),
        out_specs=[ANY, ANY, IN_VMEM, IN_VMEM],
        out_shape=[
            pltpu.HBM(err_shape, F32),
            pltpu.HBM(mixed.shape, F32),
            pltpu.VMEM(owned, F32),
            pltpu.VMEM(owned, F32),
        ],
        scratch_shapes=[
            pltpu.SMEM(row_table.shape, I32),
            pltpu.VMEM((halves, others * TILE * per_row + 8, 128), F32),
            pltpu.VMEM(owned, F32),
            pltpu.SemaphoreType.DMA((1 + halves + per_row,)),
        ],
        compiler_params=pltpu.CompilerParams(vmem_limit_bytes=16 * MIB),
    )(params, estimate, mixed, err_v, act_v, cot_v, row_table, kept_hot, own_hot, delta, *kept)


def final_kernel(per_row, mixed_pre, params_pre, spread, first, second, mixed_out, params_out, m_v, p_v, sems):
    out_rows = m_v.shape[0]
    width = m_v.shape[1] // per_row
    slots = second.shape[0]
    rows = split(jnp.concatenate([first[:slots, :], second[...]], axis=0))
    depth = spread.shape[1]
    copies = []
    for part in range(per_row):
        lanes = slice(part * width, (part + 1) * width)
        choice = spread[part * out_rows : (part + 1) * out_rows, :]
        change = dot(choice, rows[:depth]) + dot(choice, rows[depth:])
        m_v[:, lanes] = mixed_pre[:, lanes] + MIX_WEIGHT * change
        p_v[:, lanes] = params_pre[:, lanes] + (CONSENSUS * MIX_WEIGHT) * change
        pair = [
            pltpu.make_async_copy(m_v.at[:, lanes], mixed_out.at[0, :, lanes], sems.at[2 * part]),
            pltpu.make_async_copy(p_v.at[:, lanes], params_out.at[0, :, lanes], sems.at[2 * part + 1]),
        ]
        for copy in pair:
            copy.start()
        copies += pair
    for copy in copies:
        copy.wait()


def final(per_row, shape, mixed_pre, params_pre, spread, first, second):
    return pl.pallas_call(
        functools.partial(final_kernel, per_row),
        name="neighbours",
        in_specs=[IN_VMEM] * 5,
        out_specs=[ANY] * 2,
        out_shape=[pltpu.HBM(shape, F32)] * 2,
        scratch_shapes=[
            pltpu.VMEM(mixed_pre.shape, F32),
            pltpu.VMEM(mixed_pre.shape, F32),
            pltpu.SemaphoreType.DMA((2 * per_row,)),
        ],
        compiler_params=pltpu.CompilerParams(vmem_limit_bytes=20 * MIB),
    )(mixed_pre, params_pre, spread, first, second)


def neighbours(silo, silos):
    lower, upper = lax.rem(silo + silos - 1, silos), lax.rem(silo + 1, silos)
    if silos % 2:
        return lower, upper
    even = lax.rem(silo, 2) == 0
    return jnp.where(even, lower, upper), jnp.where(even, upper, lower)


def exchange(rows, again, silos):
    if silos % 2:
        routes = [[(a, (a + 1) % silos) for a in range(silos)], [(a, (a - 1) % silos) for a in range(silos)]]
    else:
        routes = [
            [(a, (a + 1 if a % 2 else a - 1) % silos) for a in range(silos)],
            [(a, a ^ 1) for a in range(silos)],
        ]
    far = lax.ppermute(rows, "silo", routes[0])
    near = lax.ppermute(again, "silo", routes[1])
    return far, near


def body(
    activ, cotangent, error_memory, params, estimate, mixed,
    kept_blocks, kept_counts, gossip_blocks, gossip_counts,
):
    shards = lax.axis_size("shard")
    silos = lax.axis_size("silo")
    nblocks, block_len = error_memory.shape[2:]
    own_blocks = nblocks // shards
    per_row = activ.shape[1] // block_len
    scale = activ.shape[1] ** (-0.5)
    activ, cotangent, error_memory, params, kept_blocks, kept_counts, gossip_blocks, gossip_counts = (
        pltpu.with_memory_space_constraint(array, pltpu.HBM)
        for array in (
            activ, cotangent, error_memory, params,
            kept_blocks, kept_counts, gossip_blocks, gossip_counts.reshape(silos),
        )
    )
    grad_rows, err_rows, act_v, cot_v, own_match, match, kept_hot, own_hot, spread, row_table, g_table = moving_rows(
        shards, silos, own_blocks, per_row, scale,
        kept_blocks, kept_counts, gossip_blocks, gossip_counts, activ, cotangent, error_memory,
    )
    *outgoing, grad_v = outgoing_rows(shards, per_row, scale, grad_rows, err_rows, act_v, cot_v)
    arrived = [
        lax.ppermute(rows, "shard", [(r, (r + shift) % shards) for r in range(shards)])
        for shift, rows in enumerate(outgoing, 1)
    ]
    estimate, mixed = (pltpu.with_memory_space_constraint(array, pltpu.VMEM) for array in (estimate, mixed))
    mine, base, err_v, params, _ = gradient(
        shards, per_row, scale, error_memory, params, estimate, own_match, act_v, cot_v, row_table, g_table, grad_v
    )
    delta, again = delta_rows(base, match, arrived)
    first, second = exchange(delta, again, silos)
    error_out, estimate_out, mixed_pre, params_pre = own_updates(
        shards, per_row, scale, error_memory.shape, params, estimate, mixed,
        err_v, act_v, cot_v, row_table, kept_hot, own_hot, again, [mine, *arrived],
    )
    mixed_out, params_out = final(per_row, mixed.shape, mixed_pre, params_pre, spread, first, second)
    return params_out, estimate_out, mixed_out, error_out


def solution(mesh):
    in_specs = (
        P(("silo", "shard"), None),
        P(("silo", "shard"), None),
        P("silo", "shard", None, None),
        P("silo", "shard", None),
        P("silo", "shard", None),
        P("silo", "shard", None),
        P("silo", None, None, None),
        P("silo", None, None),
        P(None, "shard", None),
        P(None, "shard"),
    )
    out_specs = (
        P("silo", "shard", None),
        P("silo", "shard", None),
        P("silo", "shard", None),
        P("silo", "shard", None, None),
    )
    return jax.shard_map(body, mesh=mesh, in_specs=in_specs, out_specs=out_specs, check_vma=False)
```

```python
import functools

import jax
import jax.numpy as jnp
from jax import lax
from jax.experimental import pallas as pl
from jax.experimental.pallas import tpu as pltpu
from jax.sharding import PartitionSpec as P

LEARN_RATE = 0.25
CONSENSUS = 0.5
MIX_WEIGHT = 1.0 / 3.0

F32, BF16, I32 = jnp.float32, jnp.bfloat16, jnp.int32
ANY = pl.BlockSpec(memory_space=pl.ANY)
IN_VMEM = pl.BlockSpec(memory_space=pltpu.VMEM)
MIB = 1 << 20


def dot(a, b, dims=((1,), (0,))):
    return lax.dot_general(a, b, (dims, ((), ())), preferred_element_type=F32)


def as_column(row):
    n = row.shape[1]
    eye = lax.broadcasted_iota(I32, (n, n), 0) == lax.broadcasted_iota(I32, (n, n), 1)
    spread = jnp.where(eye, jnp.broadcast_to(row.astype(F32), (n, n)), 0.0)
    return jnp.sum(spread, axis=1, keepdims=True).astype(I32)


def split(rows):
    high = rows.astype(BF16)
    return jnp.concatenate([high, (rows - high.astype(F32)).astype(BF16)], axis=0)


def pick(choice, rows):
    return dot(jnp.concatenate([choice, choice], axis=1), rows)


def onehot(mask):
    return jnp.where(mask, 1.0, 0.0).astype(BF16)


def divide(value, by):
    return (value * ((1 << 16) // by + 1)) >> 16


TILE = 128


def owner_tiles(shards, width_out):
    rows = width_out // shards
    return max(-(-(owner + 1) * rows // TILE) - owner * rows // TILE for owner in range(shards))


def first_tile(me, shards, width_out):
    last = width_out // TILE - owner_tiles(shards, width_out)
    return jnp.minimum(lax.div(me * (width_out // shards), TILE), last)


def rows_kernel(shards, silos, own_blocks, per_row, scale, lists, counts, g_lists, g_counts, act, cot, err, *refs):
    grad_rows, err_rows = refs[:2]
    (act_v, cot_v, own_match, match, kept_hot, own_hot, spread, row_table, g_table,
     list_s, count_s, gc_s, lists_v, g_v, sems) = refs[2:]
    me = lax.axis_index("shard")
    silo = lax.axis_index("silo")
    slots = lists_v.shape[2]
    g_slots = g_v.shape[2]
    width = err_rows.shape[1]
    parts = 4
    depth = act_v.shape[0] // parts
    small = [
        pltpu.make_async_copy(lists.at[0, me], list_s, sems.at[0]),
        pltpu.make_async_copy(lists.at[0], lists_v, sems.at[1]),
        pltpu.make_async_copy(counts.at[0], count_s, sems.at[2]),
        pltpu.make_async_copy(g_lists, g_v, sems.at[3]),
        pltpu.make_async_copy(g_counts, gc_s, sems.at[4]),
    ]
    cot_copy = pltpu.make_async_copy(cot, cot_v, sems.at[5])
    act_copies = [
        pltpu.make_async_copy(act.at[rows], act_v.at[rows], sems.at[6 + part])
        for part, rows in enumerate(pl.ds(part * depth, depth) for part in range(parts))
    ]
    for copy in [*small, cot_copy, *act_copies]:
        copy.start()
    for copy in small:
        copy.wait()

    columns, fills = [], []
    for shift in range(1, shards):
        owner = lax.rem(me + shift, shards)

        def fetch(slot, carry, owner=owner, shift=shift):
            block = owner * own_blocks + list_s[owner, slot]
            into = err_rows.at[pl.ds((shift - 1) * slots + slot, 1)]
            pltpu.make_async_copy(err.at[0, 0, pl.ds(block, 1)], into, sems.at[0]).start()
            return carry

        lax.fori_loop(0, slots, fetch, 0, unroll=slots)
        row = lists_v[me, pl.ds(owner, 1), :] + owner * own_blocks
        columns.append(as_column(row))
        slot_ids = lax.broadcasted_iota(I32, (slots, 1), 0)
        fills.append(slot_ids < count_s[me, owner])
    blocks = jnp.concatenate(columns, axis=0)
    filled = jnp.concatenate(fills, axis=0)
    out_row = divide(blocks, per_row)
    segment = blocks - out_row * per_row
    total = blocks.shape[0]
    chosen = onehot(lax.broadcasted_iota(I32, (total, cot_v.shape[1]), 1) == out_row)

    senders = [lists_v[lax.rem(me - shift + shards, shards), pl.ds(me, 1), :] for shift in range(shards)]
    gossiped = as_column(g_v[silo])
    sent = lax.broadcasted_iota(I32, (g_slots, 1), 0) < gc_s[silo]
    for shift, ids in enumerate(senders):
        same = onehot((gossiped == jnp.concatenate([ids, ids], axis=1)) & sent)
        if shift:
            match[:, 2 * (shift - 1) * slots : 2 * shift * slots] = same
        else:
            own_match[...] = same
    nblocks = shards * own_blocks
    step = TILE * per_row
    own_span = owner_tiles(shards, cot_v.shape[1]) * step
    start = first_tile(me, shards, cot_v.shape[1]) * step
    slot_ids = lax.broadcasted_iota(I32, (1, slots), 1)
    for owner in range(shards):
        place = lists_v[me, owner : owner + 1, :] + (owner * own_blocks - start)
        place = jnp.where(place < 0, place + nblocks, place)
        keep = slot_ids < count_s[me, owner]
        row_table[owner : owner + 1, :] = jnp.where(keep & (place < own_span), place, nblocks)
        row_table[shards + owner : shards + owner + 1, :] = jnp.where(
            keep & (place >= own_span), place - own_span, nblocks - own_span
        )
    place = lists_v[me, pl.ds(me, 1), :] + (me * own_blocks - start)
    row_table[2 * shards : 2 * shards + 1, :] = jnp.where(slot_ids < count_s[me, me], place, nblocks)
    out_rows = own_blocks // per_row
    chunks = per_row * width // 128
    row = divide(g_v[silo], per_row)
    place = (g_v[silo] - row * per_row) * (width // 128 * out_rows) + row
    sent = lax.broadcasted_iota(I32, (1, g_slots), 1) < gc_s[silo]
    g_table[...] = jnp.where(sent, place, chunks * out_rows)
    first, second = neighbours(silo, silos)
    for ids, into in (
        (jnp.concatenate(senders, axis=1), kept_hot),
        (g_v[silo], own_hot),
        (jnp.concatenate([g_v[first], g_v[second]], axis=1), spread),
    ):
        for part in range(per_row):
            here = lax.broadcasted_iota(I32, (out_rows, ids.shape[1]), 0) * per_row + part
            into[part * out_rows : (part + 1) * out_rows, :] = onehot(here == ids)

    cot_copy.wait()
    picked = dot(chosen, cot_v[...], ((1,), (1,))).astype(BF16)
    acc = jnp.zeros((total, act_v.shape[1]), F32)
    for part, copy in enumerate(act_copies):
        copy.wait()
        acc = acc + dot(picked[:, part * depth : (part + 1) * depth], act_v[part * depth : (part + 1) * depth, :])
    grad = jnp.zeros((total, width), F32)
    for part in range(per_row):
        grad = jnp.where(segment == part, acc[:, part * width : (part + 1) * width], grad)
    grad_rows[...] = jnp.where(filled, grad * scale, 0.0)
    pltpu.make_async_copy(err_rows, err_rows, sems.at[0]).wait()
    err_rows[...] = jnp.where(filled, err_rows[...], 0.0)


def moving_rows(shards, silos, own_blocks, per_row, scale, lists, counts, g_lists, g_counts, act, cot, err):
    slots = lists.shape[3]
    g_slots = g_lists.shape[2]
    width = err.shape[3]
    return pl.pallas_call(
        functools.partial(rows_kernel, shards, silos, own_blocks, per_row, scale),
        name="moving_rows",
        in_specs=[ANY] * 7,
        out_specs=[IN_VMEM] * 11,
        out_shape=[pltpu.VMEM(((shards - 1) * slots, width), F32)] * 2
        + [
            pltpu.VMEM(act.shape, BF16),
            pltpu.VMEM(cot.shape, BF16),
            pltpu.VMEM((g_slots, 2 * slots), BF16),
            pltpu.VMEM((g_slots, 2 * (shards - 1) * slots), BF16),
            pltpu.VMEM((own_blocks, shards * slots), BF16),
            pltpu.VMEM((own_blocks, g_slots), BF16),
            pltpu.VMEM((own_blocks, 2 * g_slots), BF16),
            pltpu.VMEM((2 * shards + 1, slots), I32),
            pltpu.VMEM((1, g_slots), I32),
        ],
        scratch_shapes=[
            pltpu.SMEM((shards, slots), I32),
            pltpu.SMEM((shards, shards), I32),
            pltpu.SMEM(g_counts.shape, I32),
            pltpu.VMEM(lists.shape[1:], I32),
            pltpu.VMEM(g_lists.shape, I32),
            pltpu.SemaphoreType.DMA((10,)),
        ],
        compiler_params=pltpu.CompilerParams(vmem_limit_bytes=16 * MIB),
    )(lists, counts, g_lists, g_counts, act, cot, err)


def early_tiles(me, silo):
    return jnp.where((me == 0) & (silo < 2), 1, 0)


def tiles_by_then(silo, count, tiles):
    return jnp.where(silo == 1, tiles, count)


def sum_kernel(shards, per_row, scale, grad_rows, err_rows, act_v, cot_v, *outs):
    *outs, grad_v = outs
    me = lax.axis_index("shard")
    start = first_tile(me, shards, cot_v.shape[1])

    def store(place, carry):
        grad = tile_gradient(cot_v, act_v, scale, start + place)
        for where, piece in pieces(grad, place, per_row, grad_v.shape[0]):
            grad_v[where] = piece
        return carry

    lax.fori_loop(0, early_tiles(me, lax.axis_index("silo")), store, 0)
    slots = outs[0].shape[0]
    for place, out in enumerate(outs):
        rows = slice(place * slots, (place + 1) * slots)
        out[...] = err_rows[rows, :] + grad_rows[rows, :]


def outgoing_rows(shards, per_row, scale, grad_rows, err_rows, act_v, cot_v):
    shape = (grad_rows.shape[0] // (shards - 1), grad_rows.shape[1])
    return pl.pallas_call(
        functools.partial(sum_kernel, shards, per_row, scale),
        name="outgoing_rows",
        in_specs=[IN_VMEM] * 4,
        out_specs=[IN_VMEM] * shards,
        out_shape=[pltpu.VMEM(shape, F32)] * (shards - 1)
        + [pltpu.VMEM((shape[1] // 128, cot_v.shape[1] * per_row, 128), F32)],
        compiler_params=pltpu.CompilerParams(vmem_limit_bytes=8 * MIB),
        cost_estimate=pl.CostEstimate(flops=10**10, bytes_accessed=3 * 10**7, transcendentals=0),
    )(grad_rows, err_rows, act_v, cot_v)


def load_memory(err, err_v, tiles, step, into, sems):
    copies = [
        pltpu.make_async_copy(
            err.at[0, 0, pl.ds(pl.multiple_of(tile * step, 8), step), pl.ds(half * 128, 128)],
            err_v.at[half, pl.ds(place * step, step)],
            sems[half],
        )
        for place, tile in enumerate(tiles, into)
        for half in range(err_v.shape[0])
    ]
    for copy in copies:
        copy.start()
    return copies


def tile_gradient(cot_v, act_v, scale, tile):
    columns = pl.ds(pl.multiple_of(tile * TILE, TILE), TILE)
    return dot(cot_v[:, columns], act_v[...], ((0,), (0,))) * scale


def pieces(grad, place, per_row, halves):
    for seg in range(per_row):
        for half in range(halves):
            lane = (seg * halves + half) * 128
            where = pl.ds(place * TILE * per_row + seg, TILE, stride=per_row)
            yield (half, where, slice(None)), grad[:, lane : lane + 128]


def clear_rows(err_v, table_s, first, shards):
    for owner in range(first, first + shards):

        def clear(slot, carry, owner=owner):
            block = table_s[owner, slot]
            for half in range(err_v.shape[0]):
                err_v[half, pl.ds(block, 1), :] = jnp.zeros((1, 128), F32)
            return carry

        lax.fori_loop(0, table_s.shape[1], clear, 0, unroll=table_s.shape[1])


def gradient_kernel(
    shards, per_row, scale,
    err, params, e_v, own_match, act_v, cot_v, row_table, g_table, _,
    mine, base, err_v, p_v, grad_v, table_s, g_s, rows_v, drift_v, sems,
):
    me = lax.axis_index("shard")
    slots = mine.shape[0]
    g_slots = base.shape[0]
    halves = err_v.shape[0]
    out_rows = e_v.shape[1]
    chunks = e_v.shape[2] // 128
    step = TILE * per_row
    tiles = cot_v.shape[1] // TILE
    count = owner_tiles(shards, cot_v.shape[1])
    start = first_tile(me, shards, cot_v.shape[1])
    small = [
        pltpu.make_async_copy(row_table, table_s, sems.at[0]),
        pltpu.make_async_copy(g_table, g_s, sems.at[1]),
    ]
    for copy in small:
        copy.start()

    def load(places, sem):
        order = [lax.rem(start + place, tiles) for place in places]
        return load_memory(err, err_v, order, step, places[0], [sems.at[sem + half] for half in range(halves)])

    own_memory = load(range(count), 3)
    p_copy = pltpu.make_async_copy(params, p_v, sems.at[2])
    p_copy.start()
    other_memory = load(range(count, tiles), 3 + halves)

    def store(place, carry):
        grad = tile_gradient(cot_v, act_v, scale, lax.rem(start + place, tiles))
        for where, piece in pieces(grad, place, per_row, halves):
            grad_v[where] = piece
        return carry

    silo = lax.axis_index("silo")
    lax.fori_loop(early_tiles(me, silo), tiles_by_then(silo, count, tiles), store, 0)
    for copy in small + own_memory:
        copy.wait()
    done = count * step
    for half in range(halves):
        err_v[half, :done, :] = err_v[half, :done, :] + grad_v[half, :done, :]
        err_v[half, tiles * step :, :] = jnp.zeros((8, 128), F32)

    def take(slot, carry):
        for half in range(halves):
            rows_v[half, pl.ds(slot, 1), :] = err_v[half, pl.ds(table_s[2 * shards, slot], 1), :]
        return carry

    lax.fori_loop(0, slots, take, 0, unroll=slots)
    mine[...] = jnp.concatenate([rows_v[half, :slots] for half in range(halves)], axis=1)
    clear_rows(err_v, table_s, 0, shards)
    p_copy.wait()
    for chunk in range(chunks):
        lanes = slice(chunk * 128, (chunk + 1) * 128)
        drift_v[chunk * out_rows : (chunk + 1) * out_rows, :] = p_v[0, :, lanes] - e_v[0, :, lanes]
    for half in range(halves):
        nothing = (chunks + half) * out_rows
        drift_v[nothing : nothing + 8, :] = jnp.zeros((8, 128), F32)

    def gather(slot, carry):
        for half in range(halves):
            rows_v[half, pl.ds(slot, 1), :] = drift_v[pl.ds(g_s[0, slot] + half * out_rows, 1), :]
        return carry

    lax.fori_loop(0, g_slots, gather, 0, unroll=g_slots)
    rows = jnp.concatenate([rows_v[half, :g_slots] for half in range(halves)], axis=1)
    base[...] = rows - LEARN_RATE * dot(own_match[...], split(mine[...]))
    for copy in other_memory:
        copy.wait()


def gradient(shards, per_row, scale, err, params, estimate, own_match, act_v, cot_v, row_table, g_table, grad_v):
    slots = row_table.shape[1]
    g_slots = own_match.shape[0]
    nblocks, width = err.shape[2:]
    halves = width // 128
    chunks = params.shape[2] // 128
    return pl.pallas_call(
        functools.partial(gradient_kernel, shards, per_row, scale),
        name="gradient",
        in_specs=[ANY] * 2 + [IN_VMEM] * 7,
        out_specs=[IN_VMEM] * 5,
        out_shape=[
            pltpu.VMEM((slots, width), F32),
            pltpu.VMEM((g_slots, width), F32),
            pltpu.VMEM((halves, nblocks + 8, 128), F32),
            pltpu.VMEM(params.shape, F32),
            pltpu.VMEM(grad_v.shape, F32),
        ],
        input_output_aliases={8: 4},
        scratch_shapes=[
            pltpu.SMEM(row_table.shape, I32),
            pltpu.SMEM(g_table.shape, I32),
            pltpu.VMEM((halves, max(slots, g_slots), 128), F32),
            pltpu.VMEM(((chunks + halves - 1) * params.shape[1] + 8, 128), F32),
            pltpu.SemaphoreType.DMA((3 + 2 * halves,)),
        ],
        compiler_params=pltpu.CompilerParams(vmem_limit_bytes=16 * MIB),
    )(err, params, estimate, own_match, act_v, cot_v, row_table, g_table, grad_v)


def delta_kernel(base, match, *refs):
    *arrived, out, again = refs
    rows = jnp.concatenate([split(each[...]) for each in arrived], axis=0)
    total = base[...] - LEARN_RATE * dot(match[...], rows)
    out[: total.shape[0]] = total
    out[total.shape[0] :] = jnp.zeros((8, total.shape[1]), F32)
    again[...] = total


def delta_rows(base, match, arrived):
    return pl.pallas_call(
        delta_kernel,
        name="delta_rows",
        in_specs=[IN_VMEM] * (2 + len(arrived)),
        out_specs=[IN_VMEM] * 2,
        out_shape=[pltpu.VMEM((base.shape[0] + 8, base.shape[1]), F32), pltpu.VMEM(base.shape, F32)],
        cost_estimate=pl.CostEstimate(flops=10**10, bytes_accessed=3 * 10**7, transcendentals=0),
        compiler_params=pltpu.CompilerParams(vmem_limit_bytes=8 * MIB),
    )(base, match, *arrived)


def own_kernel(
    shards, per_row, scale,
    p_v, e_v, m_v, err_v, grad_v, act_v, cot_v, row_table, kept_hot, own_hot, delta, *refs
):
    kept = refs[:shards]
    err_out, est_out, mixed_pre, params_pre, table_s, rest_v, est_v, sems = refs[shards:]
    me = lax.axis_index("shard")
    width = delta.shape[1]
    halves = err_v.shape[0]
    out_rows = p_v.shape[1]
    step = TILE * per_row
    tiles = cot_v.shape[1] // TILE
    count = owner_tiles(shards, cot_v.shape[1])
    start = first_tile(me, shards, cot_v.shape[1])
    small = pltpu.make_async_copy(row_table, table_s, sems.at[0])
    small.start()
    copies = []

    def store_memory(source, first, places):
        for place in places:
            tile = lax.rem(start + place, tiles)
            for half in range(halves):
                copy = pltpu.make_async_copy(
                    source.at[half, pl.ds((place - first) * step, step)],
                    err_out.at[0, 0, pl.ds(pl.multiple_of(tile * step, 8), step), pl.ds(half * 128, 128)],
                    sems.at[1 + half],
                )
                copy.start()
                copies.append(copy)

    store_memory(err_v, 0, range(count))

    def store(place, carry):
        grad = tile_gradient(cot_v, act_v, scale, lax.rem(start + count + place, tiles))
        held = pieces(grad, count + place, per_row, halves)
        for (where, piece), (there, _) in zip(pieces(grad, place, per_row, halves), held):
            rest_v[where] = err_v[there] + piece
        return carry

    by_then = tiles_by_then(lax.axis_index("silo"), count, tiles)

    @pl.when(by_then == tiles)
    def _():
        for half in range(halves):
            rows = slice(count * step, tiles * step)
            rest_v[half, : (tiles - count) * step, :] = err_v[half, rows, :] + grad_v[half, rows, :]

    lax.fori_loop(0, tiles - by_then, store, 0)
    small.wait()
    clear_rows(rest_v, table_s, shards, shards)
    store_memory(rest_v, count, range(count, tiles))

    kept_parts = split(jnp.concatenate([rows[...] for rows in kept], axis=0))
    delta_parts = split(delta[...])
    for part in range(per_row):
        lanes = slice(part * width, (part + 1) * width)
        blocks = slice(part * out_rows, (part + 1) * out_rows)
        grad = pick(kept_hot[blocks, :], kept_parts)
        change = pick(own_hot[blocks, :], delta_parts)
        half_step = p_v[0, :, lanes] - LEARN_RATE * grad
        est = e_v[0, :, lanes] + change
        mix = m_v[0, :, lanes] + MIX_WEIGHT * change
        est_v[:, lanes] = est
        copy = pltpu.make_async_copy(est_v.at[:, lanes], est_out.at[0, :, lanes], sems.at[1 + halves + part])
        copy.start()
        copies.append(copy)
        mixed_pre[:, lanes] = mix
        params_pre[:, lanes] = half_step + CONSENSUS * (mix - est)
    for copy in copies:
        copy.wait()


def own_updates(
    shards, per_row, scale, err_shape, params, estimate, mixed, err_v, grad_v, act_v, cot_v, row_table, kept_hot, own_hot, delta, kept
):
    owned = mixed.shape[1:]
    halves = err_v.shape[0]
    others = cot_v.shape[1] // TILE - owner_tiles(shards, cot_v.shape[1])
    return pl.pallas_call(
        functools.partial(own_kernel, shards, per_row, scale),
        name="own_updates",
        in_specs=[IN_VMEM] * (11 + shards),
        out_specs=[ANY, ANY, IN_VMEM, IN_VMEM],
        out_shape=[
            pltpu.HBM(err_shape, F32),
            pltpu.HBM(mixed.shape, F32),
            pltpu.VMEM(owned, F32),
            pltpu.VMEM(owned, F32),
        ],
        scratch_shapes=[
            pltpu.SMEM(row_table.shape, I32),
            pltpu.VMEM((halves, others * TILE * per_row + 8, 128), F32),
            pltpu.VMEM(owned, F32),
            pltpu.SemaphoreType.DMA((1 + halves + per_row,)),
        ],
        compiler_params=pltpu.CompilerParams(vmem_limit_bytes=16 * MIB),
    )(params, estimate, mixed, err_v, grad_v, act_v, cot_v, row_table, kept_hot, own_hot, delta, *kept)


def final_kernel(per_row, mixed_pre, params_pre, spread, first, second, mixed_out, params_out, m_v, p_v, sems):
    out_rows = m_v.shape[0]
    width = m_v.shape[1] // per_row
    slots = second.shape[0]
    rows = split(jnp.concatenate([first[:slots, :], second[...]], axis=0))
    depth = spread.shape[1]
    copies = []
    for part in range(per_row):
        lanes = slice(part * width, (part + 1) * width)
        choice = spread[part * out_rows : (part + 1) * out_rows, :]
        change = dot(choice, rows[:depth]) + dot(choice, rows[depth:])
        m_v[:, lanes] = mixed_pre[:, lanes] + MIX_WEIGHT * change
        p_v[:, lanes] = params_pre[:, lanes] + (CONSENSUS * MIX_WEIGHT) * change
        pair = [
            pltpu.make_async_copy(m_v.at[:, lanes], mixed_out.at[0, :, lanes], sems.at[2 * part]),
            pltpu.make_async_copy(p_v.at[:, lanes], params_out.at[0, :, lanes], sems.at[2 * part + 1]),
        ]
        for copy in pair:
            copy.start()
        copies += pair
    for copy in copies:
        copy.wait()


def final(per_row, shape, mixed_pre, params_pre, spread, first, second):
    return pl.pallas_call(
        functools.partial(final_kernel, per_row),
        name="neighbours",
        in_specs=[IN_VMEM] * 5,
        out_specs=[ANY] * 2,
        out_shape=[pltpu.HBM(shape, F32)] * 2,
        scratch_shapes=[
            pltpu.VMEM(mixed_pre.shape, F32),
            pltpu.VMEM(mixed_pre.shape, F32),
            pltpu.SemaphoreType.DMA((2 * per_row,)),
        ],
        compiler_params=pltpu.CompilerParams(vmem_limit_bytes=20 * MIB),
    )(mixed_pre, params_pre, spread, first, second)


def neighbours(silo, silos):
    lower, upper = lax.rem(silo + silos - 1, silos), lax.rem(silo + 1, silos)
    if silos % 2:
        return lower, upper
    even = lax.rem(silo, 2) == 0
    return jnp.where(even, lower, upper), jnp.where(even, upper, lower)


def exchange(rows, again, silos):
    if silos % 2:
        routes = [[(a, (a + 1) % silos) for a in range(silos)], [(a, (a - 1) % silos) for a in range(silos)]]
    else:
        routes = [
            [(a, (a + 1 if a % 2 else a - 1) % silos) for a in range(silos)],
            [(a, a ^ 1) for a in range(silos)],
        ]
    far = lax.ppermute(rows, "silo", routes[0])
    near = lax.ppermute(again, "silo", routes[1])
    return far, near


def body(
    activ, cotangent, error_memory, params, estimate, mixed,
    kept_blocks, kept_counts, gossip_blocks, gossip_counts,
):
    shards = lax.axis_size("shard")
    silos = lax.axis_size("silo")
    nblocks, block_len = error_memory.shape[2:]
    own_blocks = nblocks // shards
    per_row = activ.shape[1] // block_len
    scale = activ.shape[1] ** (-0.5)
    activ, cotangent, error_memory, params, kept_blocks, kept_counts, gossip_blocks, gossip_counts = (
        pltpu.with_memory_space_constraint(array, pltpu.HBM)
        for array in (
            activ, cotangent, error_memory, params,
            kept_blocks, kept_counts, gossip_blocks, gossip_counts.reshape(silos),
        )
    )
    grad_rows, err_rows, act_v, cot_v, own_match, match, kept_hot, own_hot, spread, row_table, g_table = moving_rows(
        shards, silos, own_blocks, per_row, scale,
        kept_blocks, kept_counts, gossip_blocks, gossip_counts, activ, cotangent, error_memory,
    )
    *outgoing, grad_v = outgoing_rows(shards, per_row, scale, grad_rows, err_rows, act_v, cot_v)
    arrived = [
        lax.ppermute(rows, "shard", [(r, (r + shift) % shards) for r in range(shards)])
        for shift, rows in enumerate(outgoing, 1)
    ]
    estimate, mixed = (pltpu.with_memory_space_constraint(array, pltpu.VMEM) for array in (estimate, mixed))
    mine, base, err_v, params, grad_v = gradient(
        shards, per_row, scale, error_memory, params, estimate, own_match, act_v, cot_v, row_table, g_table, grad_v
    )
    delta, again = delta_rows(base, match, arrived)
    first, second = exchange(delta, again, silos)
    error_out, estimate_out, mixed_pre, params_pre = own_updates(
        shards, per_row, scale, error_memory.shape, params, estimate, mixed,
        err_v, grad_v, act_v, cot_v, row_table, kept_hot, own_hot, again, [mine, *arrived],
    )
    mixed_out, params_out = final(per_row, mixed.shape, mixed_pre, params_pre, spread, first, second)
    return params_out, estimate_out, mixed_out, error_out


def solution(mesh):
    in_specs = (
        P(("silo", "shard"), None),
        P(("silo", "shard"), None),
        P("silo", "shard", None, None),
        P("silo", "shard", None),
        P("silo", "shard", None),
        P("silo", "shard", None),
        P("silo", None, None, None),
        P("silo", None, None),
        P(None, "shard", None),
        P(None, "shard"),
    )
    out_specs = (
        P("silo", "shard", None),
        P("silo", "shard", None),
        P("silo", "shard", None),
        P("silo", "shard", None, None),
    )
    return jax.shard_map(body, mesh=mesh, in_specs=in_specs, out_specs=out_specs, check_vma=False)
```

```python
import functools

import jax
import jax.numpy as jnp
from jax import lax
from jax.experimental import pallas as pl
from jax.experimental.pallas import tpu as pltpu
from jax.sharding import PartitionSpec as P

LEARN_RATE = 0.25
CONSENSUS = 0.5
MIX_WEIGHT = 1.0 / 3.0

F32, BF16, I32 = jnp.float32, jnp.bfloat16, jnp.int32
ANY = pl.BlockSpec(memory_space=pl.ANY)
IN_VMEM = pl.BlockSpec(memory_space=pltpu.VMEM)
MIB = 1 << 20


def dot(a, b, dims=((1,), (0,))):
    return lax.dot_general(a, b, (dims, ((), ())), preferred_element_type=F32)


def as_column(row):
    n = row.shape[1]
    eye = lax.broadcasted_iota(I32, (n, n), 0) == lax.broadcasted_iota(I32, (n, n), 1)
    spread = jnp.where(eye, jnp.broadcast_to(row.astype(F32), (n, n)), 0.0)
    return jnp.sum(spread, axis=1, keepdims=True).astype(I32)


def split(rows):
    high = rows.astype(BF16)
    return jnp.concatenate([high, (rows - high.astype(F32)).astype(BF16)], axis=0)


def exact_pick(choice, rows):
    high = rows.astype(BF16)
    rest = rows - high.astype(F32)
    return dot(choice, high) + pick(choice, split(rest))


def pick(choice, rows):
    return dot(jnp.concatenate([choice, choice], axis=1), rows)


def onehot(mask):
    return jnp.where(mask, 1.0, 0.0).astype(BF16)


def divide(value, by):
    return (value * ((1 << 16) // by + 1)) >> 16


TILE = 128


def owner_tiles(shards, width_out):
    rows = width_out // shards
    return max(-(-(owner + 1) * rows // TILE) - owner * rows // TILE for owner in range(shards))


def first_tile(me, shards, width_out):
    last = width_out // TILE - owner_tiles(shards, width_out)
    return jnp.minimum(lax.div(me * (width_out // shards), TILE), last)


def rows_kernel(shards, silos, own_blocks, per_row, scale, lists, counts, g_lists, g_counts, act, cot, err, *refs):
    grad_rows, err_rows = refs[:2]
    (act_v, cot_v, own_match, match, kept_hot, own_hot, spread, row_table, g_table,
     list_s, count_s, gc_s, lists_v, g_v, sems) = refs[2:]
    me = lax.axis_index("shard")
    silo = lax.axis_index("silo")
    slots = lists_v.shape[2]
    g_slots = g_v.shape[2]
    width = err_rows.shape[1]
    parts = 4
    depth = act_v.shape[0] // parts
    small = [
        pltpu.make_async_copy(lists.at[0, me], list_s, sems.at[0]),
        pltpu.make_async_copy(lists.at[0], lists_v, sems.at[1]),
        pltpu.make_async_copy(counts.at[0], count_s, sems.at[2]),
        pltpu.make_async_copy(g_lists, g_v, sems.at[3]),
        pltpu.make_async_copy(g_counts, gc_s, sems.at[4]),
    ]
    cot_copy = pltpu.make_async_copy(cot, cot_v, sems.at[5])
    act_copies = [
        pltpu.make_async_copy(act.at[rows], act_v.at[rows], sems.at[6 + part])
        for part, rows in enumerate(pl.ds(part * depth, depth) for part in range(parts))
    ]
    for copy in [*small, cot_copy, *act_copies]:
        copy.start()
    for copy in small:
        copy.wait()

    columns, fills = [], []
    for shift in range(1, shards):
        owner = lax.rem(me + shift, shards)

        def fetch(slot, carry, owner=owner, shift=shift):
            block = owner * own_blocks + list_s[owner, slot]
            into = err_rows.at[pl.ds((shift - 1) * slots + slot, 1)]
            pltpu.make_async_copy(err.at[0, 0, pl.ds(block, 1)], into, sems.at[0]).start()
            return carry

        lax.fori_loop(0, slots, fetch, 0, unroll=slots)
        row = lists_v[me, pl.ds(owner, 1), :] + owner * own_blocks
        columns.append(as_column(row))
        slot_ids = lax.broadcasted_iota(I32, (slots, 1), 0)
        fills.append(slot_ids < count_s[me, owner])
    blocks = jnp.concatenate(columns, axis=0)
    filled = jnp.concatenate(fills, axis=0)
    out_row = divide(blocks, per_row)
    segment = blocks - out_row * per_row
    total = blocks.shape[0]
    chosen = onehot(lax.broadcasted_iota(I32, (total, cot_v.shape[1]), 1) == out_row)

    senders = [lists_v[lax.rem(me - shift + shards, shards), pl.ds(me, 1), :] for shift in range(shards)]
    gossiped = as_column(g_v[silo])
    sent = lax.broadcasted_iota(I32, (g_slots, 1), 0) < gc_s[silo]
    for shift, ids in enumerate(senders):
        same = onehot((gossiped == jnp.concatenate([ids, ids], axis=1)) & sent)
        if shift:
            match[:, 2 * (shift - 1) * slots : 2 * shift * slots] = same
        else:
            own_match[...] = same
    nblocks = shards * own_blocks
    step = TILE * per_row
    own_span = owner_tiles(shards, cot_v.shape[1]) * step
    start = first_tile(me, shards, cot_v.shape[1]) * step
    slot_ids = lax.broadcasted_iota(I32, (1, slots), 1)
    for owner in range(shards):
        place = lists_v[me, owner : owner + 1, :] + (owner * own_blocks - start)
        place = jnp.where(place < 0, place + nblocks, place)
        keep = slot_ids < count_s[me, owner]
        row_table[owner : owner + 1, :] = jnp.where(keep & (place < own_span), place, nblocks)
        row_table[shards + owner : shards + owner + 1, :] = jnp.where(
            keep & (place >= own_span), place - own_span, nblocks - own_span
        )
    place = lists_v[me, pl.ds(me, 1), :] + (me * own_blocks - start)
    row_table[2 * shards : 2 * shards + 1, :] = jnp.where(slot_ids < count_s[me, me], place, nblocks)
    out_rows = own_blocks // per_row
    chunks = per_row * width // 128
    row = divide(g_v[silo], per_row)
    place = (g_v[silo] - row * per_row) * (width // 128 * out_rows) + row
    sent = lax.broadcasted_iota(I32, (1, g_slots), 1) < gc_s[silo]
    g_table[...] = jnp.where(sent, place, chunks * out_rows)
    first, second = neighbours(silo, silos)
    for ids, into in (
        (jnp.concatenate(senders, axis=1), kept_hot),
        (g_v[silo], own_hot),
        (jnp.concatenate([g_v[first], g_v[second]], axis=1), spread),
    ):
        for part in range(per_row):
            here = lax.broadcasted_iota(I32, (out_rows, ids.shape[1]), 0) * per_row + part
            into[part * out_rows : (part + 1) * out_rows, :] = onehot(here == ids)

    cot_copy.wait()
    picked = dot(chosen, cot_v[...], ((1,), (1,))).astype(BF16)
    acc = jnp.zeros((total, act_v.shape[1]), F32)
    for part, copy in enumerate(act_copies):
        copy.wait()
        acc = acc + dot(picked[:, part * depth : (part + 1) * depth], act_v[part * depth : (part + 1) * depth, :])
    grad = jnp.zeros((total, width), F32)
    for part in range(per_row):
        grad = jnp.where(segment == part, acc[:, part * width : (part + 1) * width], grad)
    grad_rows[...] = jnp.where(filled, grad * scale, 0.0)
    pltpu.make_async_copy(err_rows, err_rows, sems.at[0]).wait()
    err_rows[...] = jnp.where(filled, err_rows[...], 0.0)


def moving_rows(shards, silos, own_blocks, per_row, scale, lists, counts, g_lists, g_counts, act, cot, err):
    slots = lists.shape[3]
    g_slots = g_lists.shape[2]
    width = err.shape[3]
    return pl.pallas_call(
        functools.partial(rows_kernel, shards, silos, own_blocks, per_row, scale),
        name="moving_rows",
        in_specs=[ANY] * 7,
        out_specs=[IN_VMEM] * 11,
        out_shape=[pltpu.VMEM(((shards - 1) * slots, width), F32)] * 2
        + [
            pltpu.VMEM(act.shape, BF16),
            pltpu.VMEM(cot.shape, BF16),
            pltpu.VMEM((g_slots, 2 * slots), BF16),
            pltpu.VMEM((g_slots, 2 * (shards - 1) * slots), BF16),
            pltpu.VMEM((own_blocks, shards * slots), BF16),
            pltpu.VMEM((own_blocks, g_slots), BF16),
            pltpu.VMEM((own_blocks, 2 * g_slots), BF16),
            pltpu.VMEM((2 * shards + 1, slots), I32),
            pltpu.VMEM((1, g_slots), I32),
        ],
        scratch_shapes=[
            pltpu.SMEM((shards, slots), I32),
            pltpu.SMEM((shards, shards), I32),
            pltpu.SMEM(g_counts.shape, I32),
            pltpu.VMEM(lists.shape[1:], I32),
            pltpu.VMEM(g_lists.shape, I32),
            pltpu.SemaphoreType.DMA((10,)),
        ],
        compiler_params=pltpu.CompilerParams(vmem_limit_bytes=16 * MIB),
    )(lists, counts, g_lists, g_counts, act, cot, err)


def early_tiles(me, silo):
    return jnp.where((me == 0) & (silo < 2), 1, 0)


def tiles_by_then(silo, count, tiles):
    return jnp.where(silo == 1, tiles, count)


def sum_kernel(shards, per_row, scale, grad_rows, err_rows, act_v, cot_v, *outs):
    *outs, grad_v = outs
    me = lax.axis_index("shard")
    start = first_tile(me, shards, cot_v.shape[1])

    def store(place, carry):
        grad = tile_gradient(cot_v, act_v, scale, start + place)
        for where, piece in pieces(grad, place, per_row, grad_v.shape[0]):
            grad_v[where] = piece
        return carry

    lax.fori_loop(0, early_tiles(me, lax.axis_index("silo")), store, 0)
    slots = outs[0].shape[0]
    for place, out in enumerate(outs):
        rows = slice(place * slots, (place + 1) * slots)
        out[...] = err_rows[rows, :] + grad_rows[rows, :]


def outgoing_rows(shards, per_row, scale, grad_rows, err_rows, act_v, cot_v):
    shape = (grad_rows.shape[0] // (shards - 1), grad_rows.shape[1])
    return pl.pallas_call(
        functools.partial(sum_kernel, shards, per_row, scale),
        name="outgoing_rows",
        in_specs=[IN_VMEM] * 4,
        out_specs=[IN_VMEM] * shards,
        out_shape=[pltpu.VMEM(shape, F32)] * (shards - 1)
        + [pltpu.VMEM((shape[1] // 128, cot_v.shape[1] * per_row + 8, 128), F32)],
        compiler_params=pltpu.CompilerParams(vmem_limit_bytes=8 * MIB),
        cost_estimate=pl.CostEstimate(flops=10**10, bytes_accessed=3 * 10**7, transcendentals=0),
    )(grad_rows, err_rows, act_v, cot_v)


def load_memory(err, err_v, tiles, step, into, sems):
    copies = [
        pltpu.make_async_copy(
            err.at[0, 0, pl.ds(pl.multiple_of(tile * step, 8), step), pl.ds(half * 128, 128)],
            err_v.at[half, pl.ds(place * step, step)],
            sems[half],
        )
        for place, tile in enumerate(tiles, into)
        for half in range(err_v.shape[0])
    ]
    for copy in copies:
        copy.start()
    return copies


def tile_gradient(cot_v, act_v, scale, tile):
    columns = pl.ds(pl.multiple_of(tile * TILE, TILE), TILE)
    return dot(cot_v[:, columns], act_v[...], ((0,), (0,))) * scale


def pieces(grad, place, per_row, halves):
    for seg in range(per_row):
        for half in range(halves):
            lane = (seg * halves + half) * 128
            where = pl.ds(place * TILE * per_row + seg, TILE, stride=per_row)
            yield (half, where, slice(None)), grad[:, lane : lane + 128]


def clear_rows(err_v, table_s, first, shards):
    for owner in range(first, first + shards):

        def clear(slot, carry, owner=owner):
            block = table_s[owner, slot]
            for half in range(err_v.shape[0]):
                err_v[half, pl.ds(block, 1), :] = jnp.zeros((1, 128), F32)
            return carry

        lax.fori_loop(0, table_s.shape[1], clear, 0, unroll=table_s.shape[1])


def gradient_kernel(
    shards, per_row, scale,
    err, params, e_v, own_match, act_v, cot_v, row_table, g_table, _,
    mine, base, err_v, p_v, grad_v, table_s, g_s, rows_v, drift_v, sems,
):
    me = lax.axis_index("shard")
    slots = mine.shape[0]
    g_slots = base.shape[0]
    halves = err_v.shape[0]
    out_rows = e_v.shape[1]
    chunks = e_v.shape[2] // 128
    step = TILE * per_row
    tiles = cot_v.shape[1] // TILE
    count = owner_tiles(shards, cot_v.shape[1])
    start = first_tile(me, shards, cot_v.shape[1])
    small = [
        pltpu.make_async_copy(row_table, table_s, sems.at[0]),
        pltpu.make_async_copy(g_table, g_s, sems.at[1]),
    ]
    for copy in small:
        copy.start()

    def load(places, sem):
        order = [lax.rem(start + place, tiles) for place in places]
        return load_memory(err, err_v, order, step, places[0], [sems.at[sem + half] for half in range(halves)])

    own_memory = load(range(count), 3)
    p_copy = pltpu.make_async_copy(params, p_v, sems.at[2])
    p_copy.start()
    other_memory = load(range(count, tiles), 3 + halves)

    def store(place, carry):
        grad = tile_gradient(cot_v, act_v, scale, lax.rem(start + place, tiles))
        for where, piece in pieces(grad, place, per_row, halves):
            grad_v[where] = piece
        return carry

    silo = lax.axis_index("silo")
    lax.fori_loop(early_tiles(me, silo), tiles_by_then(silo, count, tiles), store, 0)
    for copy in small + own_memory:
        copy.wait()
    done = count * step
    for half in range(halves):
        err_v[half, :done, :] = err_v[half, :done, :] + grad_v[half, :done, :]
        err_v[half, tiles * step :, :] = jnp.zeros((8, 128), F32)

    def take(slot, carry):
        for half in range(halves):
            rows_v[half, pl.ds(slot, 1), :] = err_v[half, pl.ds(table_s[2 * shards, slot], 1), :]
        return carry

    lax.fori_loop(0, slots, take, 0, unroll=slots)
    mine[...] = jnp.concatenate([rows_v[half, :slots] for half in range(halves)], axis=1)
    clear_rows(err_v, table_s, 0, shards)
    p_copy.wait()
    for chunk in range(chunks):
        lanes = slice(chunk * 128, (chunk + 1) * 128)
        drift_v[chunk * out_rows : (chunk + 1) * out_rows, :] = p_v[0, :, lanes] - e_v[0, :, lanes]
    for half in range(halves):
        nothing = (chunks + half) * out_rows
        drift_v[nothing : nothing + 8, :] = jnp.zeros((8, 128), F32)

    def gather(slot, carry):
        for half in range(halves):
            rows_v[half, pl.ds(slot, 1), :] = drift_v[pl.ds(g_s[0, slot] + half * out_rows, 1), :]
        return carry

    lax.fori_loop(0, g_slots, gather, 0, unroll=g_slots)
    rows = jnp.concatenate([rows_v[half, :g_slots] for half in range(halves)], axis=1)
    base[...] = rows - LEARN_RATE * dot(own_match[...], split(mine[...]))
    for copy in other_memory:
        copy.wait()


def gradient(shards, per_row, scale, err, params, estimate, own_match, act_v, cot_v, row_table, g_table, grad_v):
    slots = row_table.shape[1]
    g_slots = own_match.shape[0]
    nblocks, width = err.shape[2:]
    halves = width // 128
    chunks = params.shape[2] // 128
    return pl.pallas_call(
        functools.partial(gradient_kernel, shards, per_row, scale),
        name="gradient",
        in_specs=[ANY] * 2 + [IN_VMEM] * 7,
        out_specs=[IN_VMEM] * 5,
        out_shape=[
            pltpu.VMEM((slots, width), F32),
            pltpu.VMEM((g_slots, width), F32),
            pltpu.VMEM((halves, nblocks + 8, 128), F32),
            pltpu.VMEM(params.shape, F32),
            pltpu.VMEM(grad_v.shape, F32),
        ],
        input_output_aliases={8: 4},
        scratch_shapes=[
            pltpu.SMEM(row_table.shape, I32),
            pltpu.SMEM(g_table.shape, I32),
            pltpu.VMEM((halves, max(slots, g_slots), 128), F32),
            pltpu.VMEM(((chunks + halves - 1) * params.shape[1] + 8, 128), F32),
            pltpu.SemaphoreType.DMA((3 + 2 * halves,)),
        ],
        compiler_params=pltpu.CompilerParams(vmem_limit_bytes=16 * MIB),
    )(err, params, estimate, own_match, act_v, cot_v, row_table, g_table, grad_v)


def delta_kernel(base, match, *refs):
    *arrived, out, again = refs
    rows = jnp.concatenate([split(each[...]) for each in arrived], axis=0)
    total = base[...] - LEARN_RATE * dot(match[...], rows)
    out[: total.shape[0]] = total
    out[total.shape[0] :] = jnp.zeros((8, total.shape[1]), F32)
    again[...] = total


def delta_rows(base, match, arrived):
    return pl.pallas_call(
        delta_kernel,
        name="delta_rows",
        in_specs=[IN_VMEM] * (2 + len(arrived)),
        out_specs=[IN_VMEM] * 2,
        out_shape=[pltpu.VMEM((base.shape[0] + 8, base.shape[1]), F32), pltpu.VMEM(base.shape, F32)],
        cost_estimate=pl.CostEstimate(flops=10**10, bytes_accessed=3 * 10**7, transcendentals=0),
        compiler_params=pltpu.CompilerParams(vmem_limit_bytes=8 * MIB),
    )(base, match, *arrived)


def own_kernel(
    shards, per_row, scale,
    p_v, e_v, m_v, err_v, grad_v, act_v, cot_v, row_table, kept_hot, own_hot, delta, *refs
):
    kept = refs[:shards]
    err_out, est_out, mixed_pre, params_pre, table_s, rest_v, est_v, sems = refs[shards:]
    me = lax.axis_index("shard")
    width = delta.shape[1]
    halves = err_v.shape[0]
    out_rows = p_v.shape[1]
    step = TILE * per_row
    tiles = cot_v.shape[1] // TILE
    count = owner_tiles(shards, cot_v.shape[1])
    start = first_tile(me, shards, cot_v.shape[1])
    small = pltpu.make_async_copy(row_table, table_s, sems.at[0])
    small.start()
    copies = []

    def store_memory(source, first, places):
        for place in places:
            tile = lax.rem(start + place, tiles)
            for half in range(halves):
                copy = pltpu.make_async_copy(
                    source.at[half, pl.ds((place - first) * step, step)],
                    err_out.at[0, 0, pl.ds(pl.multiple_of(tile * step, 8), step), pl.ds(half * 128, 128)],
                    sems.at[1 + half],
                )
                copy.start()
                copies.append(copy)

    store_memory(err_v, 0, range(count))

    def store(place, carry):
        grad = tile_gradient(cot_v, act_v, scale, lax.rem(start + count + place, tiles))
        held = pieces(grad, count + place, per_row, halves)
        for (where, piece), (there, _) in zip(pieces(grad, place, per_row, halves), held):
            rest_v[where] = err_v[there] + piece
        return carry

    by_then = tiles_by_then(lax.axis_index("silo"), count, tiles)

    @pl.when(by_then == tiles)
    def _():
        for half in range(halves):
            rows = slice(count * step, tiles * step)
            rest_v[half, : (tiles - count) * step, :] = err_v[half, rows, :] + grad_v[half, rows, :]

    lax.fori_loop(0, tiles - by_then, store, 0)
    small.wait()
    clear_rows(rest_v, table_s, shards, shards)
    store_memory(rest_v, count, range(count, tiles))

    kept_parts = split(jnp.concatenate([rows[...] for rows in kept], axis=0))
    for part in range(per_row):
        lanes = slice(part * width, (part + 1) * width)
        blocks = slice(part * out_rows, (part + 1) * out_rows)
        grad = pick(kept_hot[blocks, :], kept_parts)
        change = exact_pick(own_hot[blocks, :], delta[...])
        half_step = p_v[0, :, lanes] - LEARN_RATE * grad
        est = e_v[0, :, lanes] + change
        mix = m_v[0, :, lanes] + MIX_WEIGHT * change
        est_v[:, lanes] = est
        copy = pltpu.make_async_copy(est_v.at[:, lanes], est_out.at[0, :, lanes], sems.at[1 + halves + part])
        copy.start()
        copies.append(copy)
        mixed_pre[:, lanes] = mix
        params_pre[:, lanes] = half_step + CONSENSUS * (mix - est)
    for copy in copies:
        copy.wait()


def own_updates(
    shards, per_row, scale, err_shape, params, estimate, mixed, err_v, grad_v, act_v, cot_v, row_table, kept_hot, own_hot, delta, kept
):
    owned = mixed.shape[1:]
    halves = err_v.shape[0]
    others = cot_v.shape[1] // TILE - owner_tiles(shards, cot_v.shape[1])
    return pl.pallas_call(
        functools.partial(own_kernel, shards, per_row, scale),
        name="own_updates",
        in_specs=[IN_VMEM] * (11 + shards),
        out_specs=[ANY, ANY, IN_VMEM, IN_VMEM],
        out_shape=[
            pltpu.HBM(err_shape, F32),
            pltpu.HBM(mixed.shape, F32),
            pltpu.VMEM(owned, F32),
            pltpu.VMEM(owned, F32),
        ],
        scratch_shapes=[
            pltpu.SMEM(row_table.shape, I32),
            pltpu.VMEM((halves, others * TILE * per_row + 8, 128), F32),
            pltpu.VMEM(owned, F32),
            pltpu.SemaphoreType.DMA((1 + halves + per_row,)),
        ],
        compiler_params=pltpu.CompilerParams(vmem_limit_bytes=16 * MIB),
    )(params, estimate, mixed, err_v, grad_v, act_v, cot_v, row_table, kept_hot, own_hot, delta, *kept)


def final_kernel(per_row, mixed_pre, params_pre, spread, first, second, mixed_out, params_out, m_v, p_v, sems):
    out_rows = m_v.shape[0]
    width = m_v.shape[1] // per_row
    slots = second.shape[0]
    rows = split(jnp.concatenate([first[:slots, :], second[...]], axis=0))
    depth = spread.shape[1]
    copies = []
    for part in range(per_row):
        lanes = slice(part * width, (part + 1) * width)
        choice = spread[part * out_rows : (part + 1) * out_rows, :]
        change = dot(choice, rows[:depth]) + dot(choice, rows[depth:])
        m_v[:, lanes] = mixed_pre[:, lanes] + MIX_WEIGHT * change
        p_v[:, lanes] = params_pre[:, lanes] + (CONSENSUS * MIX_WEIGHT) * change
        pair = [
            pltpu.make_async_copy(m_v.at[:, lanes], mixed_out.at[0, :, lanes], sems.at[2 * part]),
            pltpu.make_async_copy(p_v.at[:, lanes], params_out.at[0, :, lanes], sems.at[2 * part + 1]),
        ]
        for copy in pair:
            copy.start()
        copies += pair
    for copy in copies:
        copy.wait()


def final(per_row, shape, mixed_pre, params_pre, spread, first, second):
    return pl.pallas_call(
        functools.partial(final_kernel, per_row),
        name="neighbours",
        in_specs=[IN_VMEM] * 5,
        out_specs=[ANY] * 2,
        out_shape=[pltpu.HBM(shape, F32)] * 2,
        scratch_shapes=[
            pltpu.VMEM(mixed_pre.shape, F32),
            pltpu.VMEM(mixed_pre.shape, F32),
            pltpu.SemaphoreType.DMA((2 * per_row,)),
        ],
        compiler_params=pltpu.CompilerParams(vmem_limit_bytes=20 * MIB),
    )(mixed_pre, params_pre, spread, first, second)


def neighbours(silo, silos):
    lower, upper = lax.rem(silo + silos - 1, silos), lax.rem(silo + 1, silos)
    if silos % 2:
        return lower, upper
    even = lax.rem(silo, 2) == 0
    return jnp.where(even, lower, upper), jnp.where(even, upper, lower)


def exchange(rows, again, silos):
    if silos % 2:
        routes = [[(a, (a + 1) % silos) for a in range(silos)], [(a, (a - 1) % silos) for a in range(silos)]]
    else:
        routes = [
            [(a, (a + 1 if a % 2 else a - 1) % silos) for a in range(silos)],
            [(a, a ^ 1) for a in range(silos)],
        ]
    far = lax.ppermute(rows, "silo", routes[0])
    near = lax.ppermute(again, "silo", routes[1])
    return far, near


def body(
    activ, cotangent, error_memory, params, estimate, mixed,
    kept_blocks, kept_counts, gossip_blocks, gossip_counts,
):
    shards = lax.axis_size("shard")
    silos = lax.axis_size("silo")
    nblocks, block_len = error_memory.shape[2:]
    own_blocks = nblocks // shards
    per_row = activ.shape[1] // block_len
    scale = activ.shape[1] ** (-0.5)
    activ, cotangent, error_memory, params, kept_blocks, kept_counts, gossip_blocks, gossip_counts = (
        pltpu.with_memory_space_constraint(array, pltpu.HBM)
        for array in (
            activ, cotangent, error_memory, params,
            kept_blocks, kept_counts, gossip_blocks, gossip_counts.reshape(silos),
        )
    )
    grad_rows, err_rows, act_v, cot_v, own_match, match, kept_hot, own_hot, spread, row_table, g_table = moving_rows(
        shards, silos, own_blocks, per_row, scale,
        kept_blocks, kept_counts, gossip_blocks, gossip_counts, activ, cotangent, error_memory,
    )
    *outgoing, grad_v = outgoing_rows(shards, per_row, scale, grad_rows, err_rows, act_v, cot_v)
    arrived = [
        lax.ppermute(rows, "shard", [(r, (r + shift) % shards) for r in range(shards)])
        for shift, rows in enumerate(outgoing, 1)
    ]
    estimate, mixed = (pltpu.with_memory_space_constraint(array, pltpu.VMEM) for array in (estimate, mixed))
    mine, base, err_v, params, grad_v = gradient(
        shards, per_row, scale, error_memory, params, estimate, own_match, act_v, cot_v, row_table, g_table, grad_v
    )
    delta, again = delta_rows(base, match, arrived)
    first, second = exchange(delta, again, silos)
    error_out, estimate_out, mixed_pre, params_pre = own_updates(
        shards, per_row, scale, error_memory.shape, params, estimate, mixed,
        err_v, grad_v, act_v, cot_v, row_table, kept_hot, own_hot, again, [mine, *arrived],
    )
    mixed_out, params_out = final(per_row, mixed.shape, mixed_pre, params_pre, spread, first, second)
    return params_out, estimate_out, mixed_out, error_out


def solution(mesh):
    in_specs = (
        P(("silo", "shard"), None),
        P(("silo", "shard"), None),
        P("silo", "shard", None, None),
        P("silo", "shard", None),
        P("silo", "shard", None),
        P("silo", "shard", None),
        P("silo", None, None, None),
        P("silo", None, None),
        P(None, "shard", None),
        P(None, "shard"),
    )
    out_specs = (
        P("silo", "shard", None),
        P("silo", "shard", None),
        P("silo", "shard", None),
        P("silo", "shard", None, None),
    )
    return jax.shard_map(body, mesh=mesh, in_specs=in_specs, out_specs=out_specs, check_vma=False)
```

```python
import functools

import jax
import jax.numpy as jnp
from jax import lax
from jax.experimental import pallas as pl
from jax.experimental.pallas import tpu as pltpu
from jax.sharding import PartitionSpec as P

LEARN_RATE = 0.25
CONSENSUS = 0.5
MIX_WEIGHT = 1.0 / 3.0

F32, BF16, I32 = jnp.float32, jnp.bfloat16, jnp.int32
ANY = pl.BlockSpec(memory_space=pl.ANY)
IN_VMEM = pl.BlockSpec(memory_space=pltpu.VMEM)
MIB = 1 << 20


def dot(a, b, dims=((1,), (0,))):
    return lax.dot_general(a, b, (dims, ((), ())), preferred_element_type=F32)


def as_column(row):
    n = row.shape[1]
    eye = lax.broadcasted_iota(I32, (n, n), 0) == lax.broadcasted_iota(I32, (n, n), 1)
    spread = jnp.where(eye, jnp.broadcast_to(row.astype(F32), (n, n)), 0.0)
    return jnp.sum(spread, axis=1, keepdims=True).astype(I32)


def split(rows):
    high = rows.astype(BF16)
    return jnp.concatenate([high, (rows - high.astype(F32)).astype(BF16)], axis=0)


def pick(choice, rows):
    return dot(jnp.concatenate([choice, choice], axis=1), rows)


def onehot(mask):
    return jnp.where(mask, 1.0, 0.0).astype(BF16)


def divide(value, by):
    return (value * ((1 << 16) // by + 1)) >> 16


TILE = 128


def owner_tiles(shards, width_out):
    rows = width_out // shards
    return max(-(-(owner + 1) * rows // TILE) - owner * rows // TILE for owner in range(shards))


def first_tile(me, shards, width_out):
    last = width_out // TILE - owner_tiles(shards, width_out)
    return jnp.minimum(lax.div(me * (width_out // shards), TILE), last)


def rows_kernel(shards, silos, own_blocks, per_row, scale, lists, counts, g_lists, g_counts, act, cot, err, *refs):
    grad_rows, err_rows = refs[:2]
    (act_v, cot_v, own_match, match, kept_hot, own_hot, spread, row_table, g_table,
     list_s, count_s, gc_s, lists_v, g_v, sems) = refs[2:]
    me = lax.axis_index("shard")
    silo = lax.axis_index("silo")
    slots = lists_v.shape[2]
    g_slots = g_v.shape[2]
    width = err_rows.shape[1]
    parts = 4
    depth = act_v.shape[0] // parts
    small = [
        pltpu.make_async_copy(lists.at[0, me], list_s, sems.at[0]),
        pltpu.make_async_copy(lists.at[0], lists_v, sems.at[1]),
        pltpu.make_async_copy(counts.at[0], count_s, sems.at[2]),
        pltpu.make_async_copy(g_lists, g_v, sems.at[3]),
        pltpu.make_async_copy(g_counts, gc_s, sems.at[4]),
    ]
    cot_copy = pltpu.make_async_copy(cot, cot_v, sems.at[5])
    act_copies = [
        pltpu.make_async_copy(act.at[rows], act_v.at[rows], sems.at[6 + part])
        for part, rows in enumerate(pl.ds(part * depth, depth) for part in range(parts))
    ]
    for copy in [*small, cot_copy, *act_copies]:
        copy.start()
    for copy in small:
        copy.wait()

    columns, fills = [], []
    for shift in range(1, shards):
        owner = lax.rem(me + shift, shards)

        def fetch(slot, carry, owner=owner, shift=shift):
            block = owner * own_blocks + list_s[owner, slot]
            into = err_rows.at[pl.ds((shift - 1) * slots + slot, 1)]
            pltpu.make_async_copy(err.at[0, 0, pl.ds(block, 1)], into, sems.at[0]).start()
            return carry

        lax.fori_loop(0, slots, fetch, 0, unroll=slots)
        row = lists_v[me, pl.ds(owner, 1), :] + owner * own_blocks
        columns.append(as_column(row))
        slot_ids = lax.broadcasted_iota(I32, (slots, 1), 0)
        fills.append(slot_ids < count_s[me, owner])
    blocks = jnp.concatenate(columns, axis=0)
    filled = jnp.concatenate(fills, axis=0)
    out_row = divide(blocks, per_row)
    segment = blocks - out_row * per_row
    total = blocks.shape[0]
    chosen = onehot(lax.broadcasted_iota(I32, (total, cot_v.shape[1]), 1) == out_row)

    senders = [lists_v[lax.rem(me - shift + shards, shards), pl.ds(me, 1), :] for shift in range(shards)]
    gossiped = as_column(g_v[silo])
    sent = lax.broadcasted_iota(I32, (g_slots, 1), 0) < gc_s[silo]
    for shift, ids in enumerate(senders):
        same = onehot((gossiped == jnp.concatenate([ids, ids], axis=1)) & sent)
        if shift:
            match[:, 2 * (shift - 1) * slots : 2 * shift * slots] = same
        else:
            own_match[...] = same
    nblocks = shards * own_blocks
    step = TILE * per_row
    own_span = owner_tiles(shards, cot_v.shape[1]) * step
    start = first_tile(me, shards, cot_v.shape[1]) * step
    slot_ids = lax.broadcasted_iota(I32, (1, slots), 1)
    for owner in range(shards):
        place = lists_v[me, owner : owner + 1, :] + (owner * own_blocks - start)
        place = jnp.where(place < 0, place + nblocks, place)
        keep = slot_ids < count_s[me, owner]
        row_table[owner : owner + 1, :] = jnp.where(keep & (place < own_span), place, nblocks)
        row_table[shards + owner : shards + owner + 1, :] = jnp.where(
            keep & (place >= own_span), place - own_span, nblocks - own_span
        )
    place = lists_v[me, pl.ds(me, 1), :] + (me * own_blocks - start)
    row_table[2 * shards : 2 * shards + 1, :] = jnp.where(slot_ids < count_s[me, me], place, nblocks)
    out_rows = own_blocks // per_row
    chunks = per_row * width // 128
    row = divide(g_v[silo], per_row)
    place = (g_v[silo] - row * per_row) * (width // 128 * out_rows) + row
    sent_row = lax.broadcasted_iota(I32, (1, g_slots), 1) < gc_s[silo]
    g_table[...] = jnp.where(sent_row, place, chunks * out_rows)
    first, second = neighbours(silo, silos)
    for ids, into in (
        (jnp.concatenate(senders, axis=1), kept_hot),
        (jnp.where(sent_row, g_v[silo], -1), own_hot),
        (jnp.concatenate([g_v[first], g_v[second]], axis=1), spread),
    ):
        for part in range(per_row):
            here = lax.broadcasted_iota(I32, (out_rows, ids.shape[1]), 0) * per_row + part
            into[part * out_rows : (part + 1) * out_rows, :] = onehot(here == ids)

    cot_copy.wait()
    picked = dot(chosen, cot_v[...], ((1,), (1,))).astype(BF16)
    acc = jnp.zeros((total, act_v.shape[1]), F32)
    for part, copy in enumerate(act_copies):
        copy.wait()
        acc = acc + dot(picked[:, part * depth : (part + 1) * depth], act_v[part * depth : (part + 1) * depth, :])
    grad = jnp.zeros((total, width), F32)
    for part in range(per_row):
        grad = jnp.where(segment == part, acc[:, part * width : (part + 1) * width], grad)
    grad_rows[...] = jnp.where(filled, grad * scale, 0.0)
    pltpu.make_async_copy(err_rows, err_rows, sems.at[0]).wait()
    err_rows[...] = jnp.where(filled, err_rows[...], 0.0)


def moving_rows(shards, silos, own_blocks, per_row, scale, lists, counts, g_lists, g_counts, act, cot, err):
    slots = lists.shape[3]
    g_slots = g_lists.shape[2]
    width = err.shape[3]
    return pl.pallas_call(
        functools.partial(rows_kernel, shards, silos, own_blocks, per_row, scale),
        name="moving_rows",
        in_specs=[ANY] * 7,
        out_specs=[IN_VMEM] * 11,
        out_shape=[pltpu.VMEM(((shards - 1) * slots, width), F32)] * 2
        + [
            pltpu.VMEM(act.shape, BF16),
            pltpu.VMEM(cot.shape, BF16),
            pltpu.VMEM((g_slots, 2 * slots), BF16),
            pltpu.VMEM((g_slots, 2 * (shards - 1) * slots), BF16),
            pltpu.VMEM((own_blocks, shards * slots), BF16),
            pltpu.VMEM((own_blocks, g_slots), BF16),
            pltpu.VMEM((own_blocks, 2 * g_slots), BF16),
            pltpu.VMEM((2 * shards + 1, slots), I32),
            pltpu.VMEM((1, g_slots), I32),
        ],
        scratch_shapes=[
            pltpu.SMEM((shards, slots), I32),
            pltpu.SMEM((shards, shards), I32),
            pltpu.SMEM(g_counts.shape, I32),
            pltpu.VMEM(lists.shape[1:], I32),
            pltpu.VMEM(g_lists.shape, I32),
            pltpu.SemaphoreType.DMA((10,)),
        ],
        compiler_params=pltpu.CompilerParams(vmem_limit_bytes=16 * MIB),
    )(lists, counts, g_lists, g_counts, act, cot, err)


def early_tiles(me, silo):
    return jnp.where((me == 0) & (silo < 2), 1, 0)


def tiles_by_then(silo, count, tiles):
    return jnp.where(silo == 1, tiles, count)


def sum_kernel(shards, per_row, scale, grad_rows, err_rows, act_v, cot_v, *outs):
    *outs, grad_v = outs
    me = lax.axis_index("shard")
    start = first_tile(me, shards, cot_v.shape[1])

    def store(place, carry):
        grad = tile_gradient(cot_v, act_v, scale, start + place)
        for where, piece in pieces(grad, place, per_row, grad_v.shape[0]):
            grad_v[where] = piece
        return carry

    lax.fori_loop(0, early_tiles(me, lax.axis_index("silo")), store, 0)
    slots = outs[0].shape[0]
    for place, out in enumerate(outs):
        rows = slice(place * slots, (place + 1) * slots)
        out[...] = err_rows[rows, :] + grad_rows[rows, :]


def outgoing_rows(shards, per_row, scale, grad_rows, err_rows, act_v, cot_v):
    shape = (grad_rows.shape[0] // (shards - 1), grad_rows.shape[1])
    return pl.pallas_call(
        functools.partial(sum_kernel, shards, per_row, scale),
        name="outgoing_rows",
        in_specs=[IN_VMEM] * 4,
        out_specs=[IN_VMEM] * shards,
        out_shape=[pltpu.VMEM(shape, F32)] * (shards - 1)
        + [pltpu.VMEM((shape[1] // 128, cot_v.shape[1] * per_row + 8, 128), F32)],
        compiler_params=pltpu.CompilerParams(vmem_limit_bytes=8 * MIB),
        cost_estimate=pl.CostEstimate(flops=10**10, bytes_accessed=3 * 10**7, transcendentals=0),
    )(grad_rows, err_rows, act_v, cot_v)


def load_memory(err, err_v, tiles, step, into, sems):
    copies = [
        pltpu.make_async_copy(
            err.at[0, 0, pl.ds(pl.multiple_of(tile * step, 8), step), pl.ds(half * 128, 128)],
            err_v.at[half, pl.ds(place * step, step)],
            sems[half],
        )
        for place, tile in enumerate(tiles, into)
        for half in range(err_v.shape[0])
    ]
    for copy in copies:
        copy.start()
    return copies


def tile_gradient(cot_v, act_v, scale, tile):
    columns = pl.ds(pl.multiple_of(tile * TILE, TILE), TILE)
    return dot(cot_v[:, columns], act_v[...], ((0,), (0,))) * scale


def pieces(grad, place, per_row, halves):
    for seg in range(per_row):
        for half in range(halves):
            lane = (seg * halves + half) * 128
            where = pl.ds(place * TILE * per_row + seg, TILE, stride=per_row)
            yield (half, where, slice(None)), grad[:, lane : lane + 128]


def clear_rows(err_v, table_s, first, shards):
    for owner in range(first, first + shards):

        def clear(slot, carry, owner=owner):
            block = table_s[owner, slot]
            for half in range(err_v.shape[0]):
                err_v[half, pl.ds(block, 1), :] = jnp.zeros((1, 128), F32)
            return carry

        lax.fori_loop(0, table_s.shape[1], clear, 0, unroll=table_s.shape[1])


def gradient_kernel(
    shards, per_row, scale,
    err, params, e_v, own_match, act_v, cot_v, row_table, g_table, _,
    mine, base, err_v, p_v, grad_v, table_s, g_s, rows_v, drift_v, sems,
):
    me = lax.axis_index("shard")
    slots = mine.shape[0]
    g_slots = base.shape[0]
    halves = err_v.shape[0]
    out_rows = e_v.shape[1]
    chunks = e_v.shape[2] // 128
    step = TILE * per_row
    tiles = cot_v.shape[1] // TILE
    count = owner_tiles(shards, cot_v.shape[1])
    start = first_tile(me, shards, cot_v.shape[1])
    small = [
        pltpu.make_async_copy(row_table, table_s, sems.at[0]),
        pltpu.make_async_copy(g_table, g_s, sems.at[1]),
    ]
    for copy in small:
        copy.start()

    def load(places, sem):
        order = [lax.rem(start + place, tiles) for place in places]
        return load_memory(err, err_v, order, step, places[0], [sems.at[sem + half] for half in range(halves)])

    own_memory = load(range(count), 3)
    p_copy = pltpu.make_async_copy(params, p_v, sems.at[2])
    p_copy.start()
    other_memory = load(range(count, tiles), 3 + halves)

    def store(place, carry):
        grad = tile_gradient(cot_v, act_v, scale, lax.rem(start + place, tiles))
        for where, piece in pieces(grad, place, per_row, halves):
            grad_v[where] = piece
        return carry

    silo = lax.axis_index("silo")
    lax.fori_loop(early_tiles(me, silo), tiles_by_then(silo, count, tiles), store, 0)
    for copy in small + own_memory:
        copy.wait()
    done = count * step
    for half in range(halves):
        err_v[half, :done, :] = err_v[half, :done, :] + grad_v[half, :done, :]
        err_v[half, tiles * step :, :] = jnp.zeros((8, 128), F32)

    def take(slot, carry):
        for half in range(halves):
            rows_v[half, pl.ds(slot, 1), :] = err_v[half, pl.ds(table_s[2 * shards, slot], 1), :]
        return carry

    lax.fori_loop(0, slots, take, 0, unroll=slots)
    mine[...] = jnp.concatenate([rows_v[half, :slots] for half in range(halves)], axis=1)
    clear_rows(err_v, table_s, 0, shards)
    p_copy.wait()
    for chunk in range(chunks):
        lanes = slice(chunk * 128, (chunk + 1) * 128)
        drift_v[chunk * out_rows : (chunk + 1) * out_rows, :] = p_v[0, :, lanes] - e_v[0, :, lanes]
    for half in range(halves):
        nothing = (chunks + half) * out_rows
        drift_v[nothing : nothing + 8, :] = jnp.zeros((8, 128), F32)

    def gather(slot, carry):
        for half in range(halves):
            rows_v[half, pl.ds(slot, 1), :] = drift_v[pl.ds(g_s[0, slot] + half * out_rows, 1), :]
        return carry

    lax.fori_loop(0, g_slots, gather, 0, unroll=g_slots)
    rows = jnp.concatenate([rows_v[half, :g_slots] for half in range(halves)], axis=1)
    base[...] = rows - LEARN_RATE * dot(own_match[...], split(mine[...]))
    for copy in other_memory:
        copy.wait()


def gradient(shards, per_row, scale, err, params, estimate, own_match, act_v, cot_v, row_table, g_table, grad_v):
    slots = row_table.shape[1]
    g_slots = own_match.shape[0]
    nblocks, width = err.shape[2:]
    halves = width // 128
    chunks = params.shape[2] // 128
    return pl.pallas_call(
        functools.partial(gradient_kernel, shards, per_row, scale),
        name="gradient",
        in_specs=[ANY] * 2 + [IN_VMEM] * 7,
        out_specs=[IN_VMEM] * 5,
        out_shape=[
            pltpu.VMEM((slots, width), F32),
            pltpu.VMEM((g_slots, width), F32),
            pltpu.VMEM((halves, nblocks + 8, 128), F32),
            pltpu.VMEM(params.shape, F32),
            pltpu.VMEM(grad_v.shape, F32),
        ],
        input_output_aliases={8: 4},
        scratch_shapes=[
            pltpu.SMEM(row_table.shape, I32),
            pltpu.SMEM(g_table.shape, I32),
            pltpu.VMEM((halves, max(slots, g_slots), 128), F32),
            pltpu.VMEM(((chunks + halves - 1) * params.shape[1] + 8, 128), F32),
            pltpu.SemaphoreType.DMA((3 + 2 * halves,)),
        ],
        compiler_params=pltpu.CompilerParams(vmem_limit_bytes=16 * MIB),
    )(err, params, estimate, own_match, act_v, cot_v, row_table, g_table, grad_v)


def delta_kernel(base, match, *refs):
    *arrived, out, again = refs
    rows = jnp.concatenate([split(each[...]) for each in arrived], axis=0)
    total = base[...] - LEARN_RATE * dot(match[...], rows)
    out[: total.shape[0]] = total
    out[total.shape[0] :] = jnp.zeros((8, total.shape[1]), F32)
    again[...] = total


def delta_rows(base, match, arrived):
    return pl.pallas_call(
        delta_kernel,
        name="delta_rows",
        in_specs=[IN_VMEM] * (2 + len(arrived)),
        out_specs=[IN_VMEM] * 2,
        out_shape=[pltpu.VMEM((base.shape[0] + 8, base.shape[1]), F32), pltpu.VMEM(base.shape, F32)],
        cost_estimate=pl.CostEstimate(flops=10**10, bytes_accessed=3 * 10**7, transcendentals=0),
        compiler_params=pltpu.CompilerParams(vmem_limit_bytes=8 * MIB),
    )(base, match, *arrived)


def own_kernel(
    shards, per_row, scale,
    p_v, e_v, m_v, err_v, grad_v, act_v, cot_v, row_table, kept_hot, own_hot, _, *refs
):
    kept = refs[:shards]
    err_out, est_out, mixed_pre, params_pre, table_s, rest_v, est_v, sems = refs[shards:]
    me = lax.axis_index("shard")
    width = kept[0].shape[1]
    halves = err_v.shape[0]
    out_rows = p_v.shape[1]
    step = TILE * per_row
    tiles = cot_v.shape[1] // TILE
    count = owner_tiles(shards, cot_v.shape[1])
    start = first_tile(me, shards, cot_v.shape[1])
    small = pltpu.make_async_copy(row_table, table_s, sems.at[0])
    small.start()
    copies = []

    def store_memory(source, first, places):
        for place in places:
            tile = lax.rem(start + place, tiles)
            for half in range(halves):
                copy = pltpu.make_async_copy(
                    source.at[half, pl.ds((place - first) * step, step)],
                    err_out.at[0, 0, pl.ds(pl.multiple_of(tile * step, 8), step), pl.ds(half * 128, 128)],
                    sems.at[1 + half],
                )
                copy.start()
                copies.append(copy)

    store_memory(err_v, 0, range(count))

    def store(place, carry):
        grad = tile_gradient(cot_v, act_v, scale, lax.rem(start + count + place, tiles))
        held = pieces(grad, count + place, per_row, halves)
        for (where, piece), (there, _) in zip(pieces(grad, place, per_row, halves), held):
            rest_v[where] = err_v[there] + piece
        return carry

    by_then = tiles_by_then(lax.axis_index("silo"), count, tiles)

    @pl.when(by_then == tiles)
    def _():
        for half in range(halves):
            rows = slice(count * step, tiles * step)
            rest_v[half, : (tiles - count) * step, :] = err_v[half, rows, :] + grad_v[half, rows, :]

    lax.fori_loop(0, tiles - by_then, store, 0)
    small.wait()
    clear_rows(rest_v, table_s, shards, shards)
    store_memory(rest_v, count, range(count, tiles))

    kept_parts = split(jnp.concatenate([rows[...] for rows in kept], axis=0))
    ones = jnp.ones((own_hot.shape[1], width), BF16)
    for part in range(per_row):
        lanes = slice(part * width, (part + 1) * width)
        blocks = slice(part * out_rows, (part + 1) * out_rows)
        grad = pick(kept_hot[blocks, :], kept_parts)
        half_step = p_v[0, :, lanes] - LEARN_RATE * grad
        gossiped = dot(own_hot[blocks, :], ones) > 0.0
        change = jnp.where(gossiped, half_step - e_v[0, :, lanes], 0.0)
        est = e_v[0, :, lanes] + change
        mix = m_v[0, :, lanes] + MIX_WEIGHT * change
        est_v[:, lanes] = est
        copy = pltpu.make_async_copy(est_v.at[:, lanes], est_out.at[0, :, lanes], sems.at[1 + halves + part])
        copy.start()
        copies.append(copy)
        mixed_pre[:, lanes] = mix
        params_pre[:, lanes] = half_step + CONSENSUS * (mix - est)
    for copy in copies:
        copy.wait()


def own_updates(
    shards, per_row, scale, err_shape, params, estimate, mixed, err_v, grad_v, act_v, cot_v, row_table, kept_hot, own_hot, delta, kept
):
    owned = mixed.shape[1:]
    halves = err_v.shape[0]
    others = cot_v.shape[1] // TILE - owner_tiles(shards, cot_v.shape[1])
    return pl.pallas_call(
        functools.partial(own_kernel, shards, per_row, scale),
        name="own_updates",
        in_specs=[IN_VMEM] * (11 + shards),
        out_specs=[ANY, ANY, IN_VMEM, IN_VMEM],
        out_shape=[
            pltpu.HBM(err_shape, F32),
            pltpu.HBM(mixed.shape, F32),
            pltpu.VMEM(owned, F32),
            pltpu.VMEM(owned, F32),
        ],
        scratch_shapes=[
            pltpu.SMEM(row_table.shape, I32),
            pltpu.VMEM((halves, others * TILE * per_row + 8, 128), F32),
            pltpu.VMEM(owned, F32),
            pltpu.SemaphoreType.DMA((1 + halves + per_row,)),
        ],
        compiler_params=pltpu.CompilerParams(vmem_limit_bytes=16 * MIB),
    )(params, estimate, mixed, err_v, grad_v, act_v, cot_v, row_table, kept_hot, own_hot, delta, *kept)


def final_kernel(per_row, mixed_pre, params_pre, spread, first, second, mixed_out, params_out, m_v, p_v, sems):
    out_rows = m_v.shape[0]
    width = m_v.shape[1] // per_row
    slots = second.shape[0]
    rows = split(jnp.concatenate([first[:slots, :], second[...]], axis=0))
    depth = spread.shape[1]
    copies = []
    for part in range(per_row):
        lanes = slice(part * width, (part + 1) * width)
        choice = spread[part * out_rows : (part + 1) * out_rows, :]
        change = dot(choice, rows[:depth]) + dot(choice, rows[depth:])
        m_v[:, lanes] = mixed_pre[:, lanes] + MIX_WEIGHT * change
        p_v[:, lanes] = params_pre[:, lanes] + (CONSENSUS * MIX_WEIGHT) * change
        pair = [
            pltpu.make_async_copy(m_v.at[:, lanes], mixed_out.at[0, :, lanes], sems.at[2 * part]),
            pltpu.make_async_copy(p_v.at[:, lanes], params_out.at[0, :, lanes], sems.at[2 * part + 1]),
        ]
        for copy in pair:
            copy.start()
        copies += pair
    for copy in copies:
        copy.wait()


def final(per_row, shape, mixed_pre, params_pre, spread, first, second):
    return pl.pallas_call(
        functools.partial(final_kernel, per_row),
        name="neighbours",
        in_specs=[IN_VMEM] * 5,
        out_specs=[ANY] * 2,
        out_shape=[pltpu.HBM(shape, F32)] * 2,
        scratch_shapes=[
            pltpu.VMEM(mixed_pre.shape, F32),
            pltpu.VMEM(mixed_pre.shape, F32),
            pltpu.SemaphoreType.DMA((2 * per_row,)),
        ],
        compiler_params=pltpu.CompilerParams(vmem_limit_bytes=20 * MIB),
    )(mixed_pre, params_pre, spread, first, second)


def neighbours(silo, silos):
    lower, upper = lax.rem(silo + silos - 1, silos), lax.rem(silo + 1, silos)
    if silos % 2:
        return lower, upper
    even = lax.rem(silo, 2) == 0
    return jnp.where(even, lower, upper), jnp.where(even, upper, lower)


def exchange(rows, again, silos):
    if silos % 2:
        routes = [[(a, (a + 1) % silos) for a in range(silos)], [(a, (a - 1) % silos) for a in range(silos)]]
    else:
        routes = [
            [(a, (a + 1 if a % 2 else a - 1) % silos) for a in range(silos)],
            [(a, a ^ 1) for a in range(silos)],
        ]
    far = lax.ppermute(rows, "silo", routes[0])
    near = lax.ppermute(again, "silo", routes[1])
    return far, near


def body(
    activ, cotangent, error_memory, params, estimate, mixed,
    kept_blocks, kept_counts, gossip_blocks, gossip_counts,
):
    shards = lax.axis_size("shard")
    silos = lax.axis_size("silo")
    nblocks, block_len = error_memory.shape[2:]
    own_blocks = nblocks // shards
    per_row = activ.shape[1] // block_len
    scale = activ.shape[1] ** (-0.5)
    activ, cotangent, error_memory, params, kept_blocks, kept_counts, gossip_blocks, gossip_counts = (
        pltpu.with_memory_space_constraint(array, pltpu.HBM)
        for array in (
            activ, cotangent, error_memory, params,
            kept_blocks, kept_counts, gossip_blocks, gossip_counts.reshape(silos),
        )
    )
    grad_rows, err_rows, act_v, cot_v, own_match, match, kept_hot, own_hot, spread, row_table, g_table = moving_rows(
        shards, silos, own_blocks, per_row, scale,
        kept_blocks, kept_counts, gossip_blocks, gossip_counts, activ, cotangent, error_memory,
    )
    *outgoing, grad_v = outgoing_rows(shards, per_row, scale, grad_rows, err_rows, act_v, cot_v)
    arrived = [
        lax.ppermute(rows, "shard", [(r, (r + shift) % shards) for r in range(shards)])
        for shift, rows in enumerate(outgoing, 1)
    ]
    estimate, mixed = (pltpu.with_memory_space_constraint(array, pltpu.VMEM) for array in (estimate, mixed))
    mine, base, err_v, params, grad_v = gradient(
        shards, per_row, scale, error_memory, params, estimate, own_match, act_v, cot_v, row_table, g_table, grad_v
    )
    delta, again = delta_rows(base, match, arrived)
    first, second = exchange(delta, again, silos)
    error_out, estimate_out, mixed_pre, params_pre = own_updates(
        shards, per_row, scale, error_memory.shape, params, estimate, mixed,
        err_v, grad_v, act_v, cot_v, row_table, kept_hot, own_hot, again, [mine, *arrived],
    )
    mixed_out, params_out = final(per_row, mixed.shape, mixed_pre, params_pre, spread, first, second)
    return params_out, estimate_out, mixed_out, error_out


def solution(mesh):
    in_specs = (
        P(("silo", "shard"), None),
        P(("silo", "shard"), None),
        P("silo", "shard", None, None),
        P("silo", "shard", None),
        P("silo", "shard", None),
        P("silo", "shard", None),
        P("silo", None, None, None),
        P("silo", None, None),
        P(None, "shard", None),
        P(None, "shard"),
    )
    out_specs = (
        P("silo", "shard", None),
        P("silo", "shard", None),
        P("silo", "shard", None),
        P("silo", "shard", None, None),
    )
    return jax.shard_map(body, mesh=mesh, in_specs=in_specs, out_specs=out_specs, check_vma=False)
```

```python
import functools

import jax
import jax.numpy as jnp
from jax import lax
from jax.experimental import pallas as pl
from jax.experimental.pallas import tpu as pltpu
from jax.sharding import PartitionSpec as P

LEARN_RATE = 0.25
CONSENSUS = 0.5
MIX_WEIGHT = 1.0 / 3.0

F32, BF16, I32 = jnp.float32, jnp.bfloat16, jnp.int32
ANY = pl.BlockSpec(memory_space=pl.ANY)
IN_VMEM = pl.BlockSpec(memory_space=pltpu.VMEM)
MIB = 1 << 20


def dot(a, b, dims=((1,), (0,))):
    return lax.dot_general(a, b, (dims, ((), ())), preferred_element_type=F32)


def as_column(row):
    n = row.shape[1]
    eye = lax.broadcasted_iota(I32, (n, n), 0) == lax.broadcasted_iota(I32, (n, n), 1)
    spread = jnp.where(eye, jnp.broadcast_to(row.astype(F32), (n, n)), 0.0)
    return jnp.sum(spread, axis=1, keepdims=True).astype(I32)


def split(rows):
    high = rows.astype(BF16)
    return jnp.concatenate([high, (rows - high.astype(F32)).astype(BF16)], axis=0)


def pick(choice, rows):
    return dot(jnp.concatenate([choice, choice], axis=1), rows)


def onehot(mask):
    return jnp.where(mask, 1.0, 0.0).astype(BF16)


def divide(value, by):
    return (value * ((1 << 16) // by + 1)) >> 16


TILE = 128


def owner_tiles(shards, width_out):
    rows = width_out // shards
    return max(-(-(owner + 1) * rows // TILE) - owner * rows // TILE for owner in range(shards))


def first_tile(me, shards, width_out):
    last = width_out // TILE - owner_tiles(shards, width_out)
    return jnp.minimum(lax.div(me * (width_out // shards), TILE), last)


def rows_kernel(shards, silos, own_blocks, per_row, scale, lists, counts, g_lists, g_counts, act, cot, err, *refs):
    grad_rows, err_rows = refs[:2]
    (act_v, cot_v, own_match, match, kept_hot, own_hot, spread, row_table, g_table,
     list_s, count_s, gc_s, lists_v, g_v, sems) = refs[2:]
    me = lax.axis_index("shard")
    silo = lax.axis_index("silo")
    slots = lists_v.shape[2]
    g_slots = g_v.shape[2]
    width = err_rows.shape[1]
    parts = 4
    depth = act_v.shape[0] // parts
    small = [
        pltpu.make_async_copy(lists.at[0, me], list_s, sems.at[0]),
        pltpu.make_async_copy(lists.at[0], lists_v, sems.at[1]),
        pltpu.make_async_copy(counts.at[0], count_s, sems.at[2]),
        pltpu.make_async_copy(g_lists, g_v, sems.at[3]),
        pltpu.make_async_copy(g_counts, gc_s, sems.at[4]),
    ]
    cot_copy = pltpu.make_async_copy(cot, cot_v, sems.at[5])
    act_copies = [
        pltpu.make_async_copy(act.at[rows], act_v.at[rows], sems.at[6 + part])
        for part, rows in enumerate(pl.ds(part * depth, depth) for part in range(parts))
    ]
    for copy in [*small, cot_copy, *act_copies]:
        copy.start()
    for copy in small:
        copy.wait()

    columns, fills = [], []
    for shift in range(1, shards):
        owner = lax.rem(me + shift, shards)

        def fetch(slot, carry, owner=owner, shift=shift):
            block = owner * own_blocks + list_s[owner, slot]
            into = err_rows.at[pl.ds((shift - 1) * slots + slot, 1)]
            pltpu.make_async_copy(err.at[0, 0, pl.ds(block, 1)], into, sems.at[0]).start()
            return carry

        lax.fori_loop(0, slots, fetch, 0, unroll=slots)
        row = lists_v[me, pl.ds(owner, 1), :] + owner * own_blocks
        columns.append(as_column(row))
        slot_ids = lax.broadcasted_iota(I32, (slots, 1), 0)
        fills.append(slot_ids < count_s[me, owner])
    blocks = jnp.concatenate(columns, axis=0)
    filled = jnp.concatenate(fills, axis=0)
    out_row = divide(blocks, per_row)
    segment = blocks - out_row * per_row
    total = blocks.shape[0]
    chosen = onehot(lax.broadcasted_iota(I32, (total, cot_v.shape[1]), 1) == out_row)

    senders = [lists_v[lax.rem(me - shift + shards, shards), pl.ds(me, 1), :] for shift in range(shards)]
    gossiped = as_column(g_v[silo])
    sent = lax.broadcasted_iota(I32, (g_slots, 1), 0) < gc_s[silo]
    for shift, ids in enumerate(senders):
        same = onehot((gossiped == jnp.concatenate([ids, ids], axis=1)) & sent)
        if shift:
            match[:, 2 * (shift - 1) * slots : 2 * shift * slots] = same
        else:
            own_match[...] = same
    nblocks = shards * own_blocks
    step = TILE * per_row
    own_span = owner_tiles(shards, cot_v.shape[1]) * step
    start = first_tile(me, shards, cot_v.shape[1]) * step
    slot_ids = lax.broadcasted_iota(I32, (1, slots), 1)
    for owner in range(shards):
        place = lists_v[me, owner : owner + 1, :] + (owner * own_blocks - start)
        place = jnp.where(place < 0, place + nblocks, place)
        keep = slot_ids < count_s[me, owner]
        row_table[owner : owner + 1, :] = jnp.where(keep & (place < own_span), place, nblocks)
        row_table[shards + owner : shards + owner + 1, :] = jnp.where(
            keep & (place >= own_span), place - own_span, nblocks - own_span
        )
    place = lists_v[me, pl.ds(me, 1), :] + (me * own_blocks - start)
    row_table[2 * shards : 2 * shards + 1, :] = jnp.where(slot_ids < count_s[me, me], place, nblocks)
    out_rows = own_blocks // per_row
    chunks = per_row * width // 128
    row = divide(g_v[silo], per_row)
    place = (g_v[silo] - row * per_row) * (width // 128 * out_rows) + row
    sent_row = lax.broadcasted_iota(I32, (1, g_slots), 1) < gc_s[silo]
    g_table[...] = jnp.where(sent_row, place, chunks * out_rows)
    first, second = neighbours(silo, silos)
    for ids, into in (
        (jnp.concatenate(senders, axis=1), kept_hot),
        (jnp.where(sent_row, g_v[silo], -1), own_hot),
        (jnp.concatenate([g_v[first], g_v[second]], axis=1), spread),
    ):
        for part in range(per_row):
            here = lax.broadcasted_iota(I32, (out_rows, ids.shape[1]), 0) * per_row + part
            into[part * out_rows : (part + 1) * out_rows, :] = onehot(here == ids)

    cot_copy.wait()
    picked = dot(chosen, cot_v[...], ((1,), (1,))).astype(BF16)
    acc = jnp.zeros((total, act_v.shape[1]), F32)
    for part, copy in enumerate(act_copies):
        copy.wait()
        acc = acc + dot(picked[:, part * depth : (part + 1) * depth], act_v[part * depth : (part + 1) * depth, :])
    grad = jnp.zeros((total, width), F32)
    for part in range(per_row):
        grad = jnp.where(segment == part, acc[:, part * width : (part + 1) * width], grad)
    grad_rows[...] = jnp.where(filled, grad * scale, 0.0)
    pltpu.make_async_copy(err_rows, err_rows, sems.at[0]).wait()
    err_rows[...] = jnp.where(filled, err_rows[...], 0.0)


def moving_rows(shards, silos, own_blocks, per_row, scale, lists, counts, g_lists, g_counts, act, cot, err):
    slots = lists.shape[3]
    g_slots = g_lists.shape[2]
    width = err.shape[3]
    return pl.pallas_call(
        functools.partial(rows_kernel, shards, silos, own_blocks, per_row, scale),
        name="moving_rows",
        in_specs=[ANY] * 7,
        out_specs=[IN_VMEM] * 11,
        out_shape=[pltpu.VMEM(((shards - 1) * slots, width), F32)] * 2
        + [
            pltpu.VMEM(act.shape, BF16),
            pltpu.VMEM(cot.shape, BF16),
            pltpu.VMEM((g_slots, 2 * slots), BF16),
            pltpu.VMEM((g_slots, 2 * (shards - 1) * slots), BF16),
            pltpu.VMEM((own_blocks, shards * slots), BF16),
            pltpu.VMEM((own_blocks, g_slots), BF16),
            pltpu.VMEM((own_blocks, 2 * g_slots), BF16),
            pltpu.VMEM((2 * shards + 1, slots), I32),
            pltpu.VMEM((1, g_slots), I32),
        ],
        scratch_shapes=[
            pltpu.SMEM((shards, slots), I32),
            pltpu.SMEM((shards, shards), I32),
            pltpu.SMEM(g_counts.shape, I32),
            pltpu.VMEM(lists.shape[1:], I32),
            pltpu.VMEM(g_lists.shape, I32),
            pltpu.SemaphoreType.DMA((10,)),
        ],
        compiler_params=pltpu.CompilerParams(vmem_limit_bytes=16 * MIB),
    )(lists, counts, g_lists, g_counts, act, cot, err)


def early_tiles(me, silo):
    return jnp.where((me == 0) & (silo < 2), 1, 0)


def tiles_by_then(silo, count, tiles):
    return jnp.where(silo == 1, tiles, count)


def sum_kernel(shards, per_row, scale, grad_rows, err_rows, act_v, cot_v, *outs):
    *outs, grad_v = outs
    me = lax.axis_index("shard")
    start = first_tile(me, shards, cot_v.shape[1])

    def store(place, carry):
        grad = tile_gradient(cot_v, act_v, scale, start + place)
        for where, piece in pieces(grad, place, per_row, grad_v.shape[0]):
            grad_v[where] = piece
        return carry

    lax.fori_loop(0, early_tiles(me, lax.axis_index("silo")), store, 0)
    slots = outs[0].shape[0]
    for place, out in enumerate(outs):
        rows = slice(place * slots, (place + 1) * slots)
        out[...] = err_rows[rows, :] + grad_rows[rows, :]


def outgoing_rows(shards, per_row, scale, grad_rows, err_rows, act_v, cot_v):
    shape = (grad_rows.shape[0] // (shards - 1), grad_rows.shape[1])
    return pl.pallas_call(
        functools.partial(sum_kernel, shards, per_row, scale),
        name="outgoing_rows",
        in_specs=[IN_VMEM] * 4,
        out_specs=[IN_VMEM] * shards,
        out_shape=[pltpu.VMEM(shape, F32)] * (shards - 1)
        + [pltpu.VMEM((shape[1] // 128, TILE * per_row + 8, 128), F32)],
        compiler_params=pltpu.CompilerParams(vmem_limit_bytes=8 * MIB),
        cost_estimate=pl.CostEstimate(flops=10**10, bytes_accessed=3 * 10**7, transcendentals=0),
    )(grad_rows, err_rows, act_v, cot_v)


def load_memory(err, err_v, tiles, step, into, sems):
    copies = [
        pltpu.make_async_copy(
            err.at[0, 0, pl.ds(pl.multiple_of(tile * step, 8), step), pl.ds(half * 128, 128)],
            err_v.at[half, pl.ds(place * step, step)],
            sems[half],
        )
        for place, tile in enumerate(tiles, into)
        for half in range(err_v.shape[0])
    ]
    for copy in copies:
        copy.start()
    return copies


def tile_gradient(cot_v, act_v, scale, tile):
    columns = pl.ds(pl.multiple_of(tile * TILE, TILE), TILE)
    return dot(cot_v[:, columns], act_v[...], ((0,), (0,))) * scale


def pieces(grad, place, per_row, halves):
    for seg in range(per_row):
        for half in range(halves):
            lane = (seg * halves + half) * 128
            where = pl.ds(place * TILE * per_row + seg, TILE, stride=per_row)
            yield (half, where, slice(None)), grad[:, lane : lane + 128]


def clear_rows(err_v, table_s, first, shards):
    for owner in range(first, first + shards):

        def clear(slot, carry, owner=owner):
            block = table_s[owner, slot]
            for half in range(err_v.shape[0]):
                err_v[half, pl.ds(block, 1), :] = jnp.zeros((1, 128), F32)
            return carry

        lax.fori_loop(0, table_s.shape[1], clear, 0, unroll=table_s.shape[1])


def gradient_kernel(
    shards, per_row, scale,
    err, params, e_v, own_match, act_v, cot_v, row_table, g_table, early_v,
    mine, base, err_v, p_v, grad_v, table_s, g_s, rows_v, drift_v, sems,
):
    me = lax.axis_index("shard")
    slots = mine.shape[0]
    g_slots = base.shape[0]
    halves = err_v.shape[0]
    out_rows = e_v.shape[1]
    chunks = e_v.shape[2] // 128
    step = TILE * per_row
    tiles = cot_v.shape[1] // TILE
    count = owner_tiles(shards, cot_v.shape[1])
    start = first_tile(me, shards, cot_v.shape[1])
    small = [
        pltpu.make_async_copy(row_table, table_s, sems.at[0]),
        pltpu.make_async_copy(g_table, g_s, sems.at[1]),
    ]
    for copy in small:
        copy.start()

    def load(places, sem):
        order = [lax.rem(start + place, tiles) for place in places]
        return load_memory(err, err_v, order, step, places[0], [sems.at[sem + half] for half in range(halves)])

    own_memory = load(range(count), 3)
    p_copy = pltpu.make_async_copy(params, p_v, sems.at[2])
    p_copy.start()
    other_memory = load(range(count, tiles), 3 + halves)

    def store(place, carry):
        grad = tile_gradient(cot_v, act_v, scale, lax.rem(start + place, tiles))
        for where, piece in pieces(grad, place, per_row, halves):
            grad_v[where] = piece
        return carry

    silo = lax.axis_index("silo")
    lax.fori_loop(early_tiles(me, silo), tiles_by_then(silo, count, tiles), store, 0)
    for copy in small + own_memory:
        copy.wait()
    done = count * step

    @pl.when(early_tiles(me, silo) > 0)
    def _():
        for half in range(halves):
            err_v[half, :step, :] = err_v[half, :step, :] + early_v[half, :step, :]

    @pl.when(early_tiles(me, silo) == 0)
    def _():
        for half in range(halves):
            err_v[half, :step, :] = err_v[half, :step, :] + grad_v[half, :step, :]

    for half in range(halves):
        err_v[half, step:done, :] = err_v[half, step:done, :] + grad_v[half, step:done, :]
        err_v[half, tiles * step :, :] = jnp.zeros((8, 128), F32)

    def take(slot, carry):
        for half in range(halves):
            rows_v[half, pl.ds(slot, 1), :] = err_v[half, pl.ds(table_s[2 * shards, slot], 1), :]
        return carry

    lax.fori_loop(0, slots, take, 0, unroll=slots)
    mine[...] = jnp.concatenate([rows_v[half, :slots] for half in range(halves)], axis=1)
    clear_rows(err_v, table_s, 0, shards)
    p_copy.wait()
    for chunk in range(chunks):
        lanes = slice(chunk * 128, (chunk + 1) * 128)
        drift_v[chunk * out_rows : (chunk + 1) * out_rows, :] = p_v[0, :, lanes] - e_v[0, :, lanes]
    for half in range(halves):
        nothing = (chunks + half) * out_rows
        drift_v[nothing : nothing + 8, :] = jnp.zeros((8, 128), F32)

    def gather(slot, carry):
        for half in range(halves):
            rows_v[half, pl.ds(slot, 1), :] = drift_v[pl.ds(g_s[0, slot] + half * out_rows, 1), :]
        return carry

    lax.fori_loop(0, g_slots, gather, 0, unroll=g_slots)
    rows = jnp.concatenate([rows_v[half, :g_slots] for half in range(halves)], axis=1)
    base[...] = rows - LEARN_RATE * dot(own_match[...], split(mine[...]))
    for copy in other_memory:
        copy.wait()


def gradient(shards, per_row, scale, err, params, estimate, own_match, act_v, cot_v, row_table, g_table, early_v):
    slots = row_table.shape[1]
    g_slots = own_match.shape[0]
    nblocks, width = err.shape[2:]
    halves = width // 128
    chunks = params.shape[2] // 128
    return pl.pallas_call(
        functools.partial(gradient_kernel, shards, per_row, scale),
        name="gradient",
        in_specs=[ANY] * 2 + [IN_VMEM] * 7,
        out_specs=[IN_VMEM] * 5,
        out_shape=[
            pltpu.VMEM((slots, width), F32),
            pltpu.VMEM((g_slots, width), F32),
            pltpu.VMEM((halves, nblocks + 8, 128), F32),
            pltpu.VMEM(params.shape, F32),
            pltpu.VMEM((halves, nblocks + 8, 128), F32),
        ],
        scratch_shapes=[
            pltpu.SMEM(row_table.shape, I32),
            pltpu.SMEM(g_table.shape, I32),
            pltpu.VMEM((halves, max(slots, g_slots), 128), F32),
            pltpu.VMEM(((chunks + halves - 1) * params.shape[1] + 8, 128), F32),
            pltpu.SemaphoreType.DMA((3 + 2 * halves,)),
        ],
        compiler_params=pltpu.CompilerParams(vmem_limit_bytes=16 * MIB),
    )(err, params, estimate, own_match, act_v, cot_v, row_table, g_table, early_v)


def delta_kernel(base, match, *refs):
    *arrived, out, again = refs
    rows = jnp.concatenate([split(each[...]) for each in arrived], axis=0)
    total = base[...] - LEARN_RATE * dot(match[...], rows)
    out[: total.shape[0]] = total
    out[total.shape[0] :] = jnp.zeros((8, total.shape[1]), F32)
    again[...] = total


def delta_rows(base, match, arrived):
    return pl.pallas_call(
        delta_kernel,
        name="delta_rows",
        in_specs=[IN_VMEM] * (2 + len(arrived)),
        out_specs=[IN_VMEM] * 2,
        out_shape=[pltpu.VMEM((base.shape[0] + 8, base.shape[1]), F32), pltpu.VMEM(base.shape, F32)],
        cost_estimate=pl.CostEstimate(flops=10**10, bytes_accessed=3 * 10**7, transcendentals=0),
        compiler_params=pltpu.CompilerParams(vmem_limit_bytes=8 * MIB),
    )(base, match, *arrived)


def own_kernel(
    shards, per_row, scale,
    p_v, e_v, m_v, err_v, grad_v, act_v, cot_v, row_table, kept_hot, own_hot, _, *refs
):
    kept = refs[:shards]
    err_out, est_out, mixed_pre, params_pre, table_s, rest_v, est_v, sems = refs[shards:]
    me = lax.axis_index("shard")
    width = kept[0].shape[1]
    halves = err_v.shape[0]
    out_rows = p_v.shape[1]
    step = TILE * per_row
    tiles = cot_v.shape[1] // TILE
    count = owner_tiles(shards, cot_v.shape[1])
    start = first_tile(me, shards, cot_v.shape[1])
    small = pltpu.make_async_copy(row_table, table_s, sems.at[0])
    small.start()
    copies = []

    def store_memory(source, first, places):
        for place in places:
            tile = lax.rem(start + place, tiles)
            for half in range(halves):
                copy = pltpu.make_async_copy(
                    source.at[half, pl.ds((place - first) * step, step)],
                    err_out.at[0, 0, pl.ds(pl.multiple_of(tile * step, 8), step), pl.ds(half * 128, 128)],
                    sems.at[1 + half],
                )
                copy.start()
                copies.append(copy)

    store_memory(err_v, 0, range(count))

    def store(place, carry):
        grad = tile_gradient(cot_v, act_v, scale, lax.rem(start + count + place, tiles))
        held = pieces(grad, count + place, per_row, halves)
        for (where, piece), (there, _) in zip(pieces(grad, place, per_row, halves), held):
            rest_v[where] = err_v[there] + piece
        return carry

    by_then = tiles_by_then(lax.axis_index("silo"), count, tiles)

    @pl.when(by_then == tiles)
    def _():
        for half in range(halves):
            rows = slice(count * step, tiles * step)
            rest_v[half, : (tiles - count) * step, :] = err_v[half, rows, :] + grad_v[half, rows, :]

    lax.fori_loop(0, tiles - by_then, store, 0)
    small.wait()
    clear_rows(rest_v, table_s, shards, shards)
    store_memory(rest_v, count, range(count, tiles))

    kept_parts = split(jnp.concatenate([rows[...] for rows in kept], axis=0))
    ones = jnp.ones((own_hot.shape[1], width), BF16)
    for part in range(per_row):
        lanes = slice(part * width, (part + 1) * width)
        blocks = slice(part * out_rows, (part + 1) * out_rows)
        grad = pick(kept_hot[blocks, :], kept_parts)
        half_step = p_v[0, :, lanes] - LEARN_RATE * grad
        gossiped = dot(own_hot[blocks, :], ones) > 0.0
        change = jnp.where(gossiped, half_step - e_v[0, :, lanes], 0.0)
        est = e_v[0, :, lanes] + change
        mix = m_v[0, :, lanes] + MIX_WEIGHT * change
        est_v[:, lanes] = est
        copy = pltpu.make_async_copy(est_v.at[:, lanes], est_out.at[0, :, lanes], sems.at[1 + halves + part])
        copy.start()
        copies.append(copy)
        mixed_pre[:, lanes] = mix
        params_pre[:, lanes] = half_step + CONSENSUS * (mix - est)
    for copy in copies:
        copy.wait()


def own_updates(
    shards, per_row, scale, err_shape, params, estimate, mixed, err_v, grad_v, act_v, cot_v, row_table, kept_hot, own_hot, delta, kept
):
    owned = mixed.shape[1:]
    halves = err_v.shape[0]
    others = cot_v.shape[1] // TILE - owner_tiles(shards, cot_v.shape[1])
    return pl.pallas_call(
        functools.partial(own_kernel, shards, per_row, scale),
        name="own_updates",
        in_specs=[IN_VMEM] * (11 + shards),
        out_specs=[ANY, ANY, IN_VMEM, IN_VMEM],
        out_shape=[
            pltpu.HBM(err_shape, F32),
            pltpu.HBM(mixed.shape, F32),
            pltpu.VMEM(owned, F32),
            pltpu.VMEM(owned, F32),
        ],
        scratch_shapes=[
            pltpu.SMEM(row_table.shape, I32),
            pltpu.VMEM((halves, others * TILE * per_row + 8, 128), F32),
            pltpu.VMEM(owned, F32),
            pltpu.SemaphoreType.DMA((1 + halves + per_row,)),
        ],
        compiler_params=pltpu.CompilerParams(vmem_limit_bytes=16 * MIB),
    )(params, estimate, mixed, err_v, grad_v, act_v, cot_v, row_table, kept_hot, own_hot, delta, *kept)


def final_kernel(per_row, mixed_pre, params_pre, spread, first, second, mixed_out, params_out, m_v, p_v, sems):
    out_rows = m_v.shape[0]
    width = m_v.shape[1] // per_row
    slots = second.shape[0]
    rows = split(jnp.concatenate([first[:slots, :], second[...]], axis=0))
    depth = spread.shape[1]
    copies = []
    for part in range(per_row):
        lanes = slice(part * width, (part + 1) * width)
        choice = spread[part * out_rows : (part + 1) * out_rows, :]
        change = dot(choice, rows[:depth]) + dot(choice, rows[depth:])
        m_v[:, lanes] = mixed_pre[:, lanes] + MIX_WEIGHT * change
        p_v[:, lanes] = params_pre[:, lanes] + (CONSENSUS * MIX_WEIGHT) * change
        pair = [
            pltpu.make_async_copy(m_v.at[:, lanes], mixed_out.at[0, :, lanes], sems.at[2 * part]),
            pltpu.make_async_copy(p_v.at[:, lanes], params_out.at[0, :, lanes], sems.at[2 * part + 1]),
        ]
        for copy in pair:
            copy.start()
        copies += pair
    for copy in copies:
        copy.wait()


def final(per_row, shape, mixed_pre, params_pre, spread, first, second):
    return pl.pallas_call(
        functools.partial(final_kernel, per_row),
        name="neighbours",
        in_specs=[IN_VMEM] * 5,
        out_specs=[ANY] * 2,
        out_shape=[pltpu.HBM(shape, F32)] * 2,
        scratch_shapes=[
            pltpu.VMEM(mixed_pre.shape, F32),
            pltpu.VMEM(mixed_pre.shape, F32),
            pltpu.SemaphoreType.DMA((2 * per_row,)),
        ],
        compiler_params=pltpu.CompilerParams(vmem_limit_bytes=20 * MIB),
    )(mixed_pre, params_pre, spread, first, second)


def neighbours(silo, silos):
    lower, upper = lax.rem(silo + silos - 1, silos), lax.rem(silo + 1, silos)
    if silos % 2:
        return lower, upper
    even = lax.rem(silo, 2) == 0
    return jnp.where(even, lower, upper), jnp.where(even, upper, lower)


def exchange(rows, again, silos):
    if silos % 2:
        routes = [[(a, (a + 1) % silos) for a in range(silos)], [(a, (a - 1) % silos) for a in range(silos)]]
    else:
        routes = [
            [(a, (a + 1 if a % 2 else a - 1) % silos) for a in range(silos)],
            [(a, a ^ 1) for a in range(silos)],
        ]
    far = lax.ppermute(rows, "silo", routes[0])
    near = lax.ppermute(again, "silo", routes[1])
    return far, near


def body(
    activ, cotangent, error_memory, params, estimate, mixed,
    kept_blocks, kept_counts, gossip_blocks, gossip_counts,
):
    shards = lax.axis_size("shard")
    silos = lax.axis_size("silo")
    nblocks, block_len = error_memory.shape[2:]
    own_blocks = nblocks // shards
    per_row = activ.shape[1] // block_len
    scale = activ.shape[1] ** (-0.5)
    activ, cotangent, error_memory, params, kept_blocks, kept_counts, gossip_blocks, gossip_counts = (
        pltpu.with_memory_space_constraint(array, pltpu.HBM)
        for array in (
            activ, cotangent, error_memory, params,
            kept_blocks, kept_counts, gossip_blocks, gossip_counts.reshape(silos),
        )
    )
    grad_rows, err_rows, act_v, cot_v, own_match, match, kept_hot, own_hot, spread, row_table, g_table = moving_rows(
        shards, silos, own_blocks, per_row, scale,
        kept_blocks, kept_counts, gossip_blocks, gossip_counts, activ, cotangent, error_memory,
    )
    *outgoing, early_v = outgoing_rows(shards, per_row, scale, grad_rows, err_rows, act_v, cot_v)
    arrived = [
        lax.ppermute(rows, "shard", [(r, (r + shift) % shards) for r in range(shards)])
        for shift, rows in enumerate(outgoing, 1)
    ]
    estimate, mixed = (pltpu.with_memory_space_constraint(array, pltpu.VMEM) for array in (estimate, mixed))
    mine, base, err_v, params, grad_v = gradient(
        shards, per_row, scale, error_memory, params, estimate, own_match, act_v, cot_v, row_table, g_table, early_v
    )
    delta, again = delta_rows(base, match, arrived)
    first, second = exchange(delta, again, silos)
    error_out, estimate_out, mixed_pre, params_pre = own_updates(
        shards, per_row, scale, error_memory.shape, params, estimate, mixed,
        err_v, grad_v, act_v, cot_v, row_table, kept_hot, own_hot, again, [mine, *arrived],
    )
    mixed_out, params_out = final(per_row, mixed.shape, mixed_pre, params_pre, spread, first, second)
    return params_out, estimate_out, mixed_out, error_out


def solution(mesh):
    in_specs = (
        P(("silo", "shard"), None),
        P(("silo", "shard"), None),
        P("silo", "shard", None, None),
        P("silo", "shard", None),
        P("silo", "shard", None),
        P("silo", "shard", None),
        P("silo", None, None, None),
        P("silo", None, None),
        P(None, "shard", None),
        P(None, "shard"),
    )
    out_specs = (
        P("silo", "shard", None),
        P("silo", "shard", None),
        P("silo", "shard", None),
        P("silo", "shard", None, None),
    )
    return jax.shard_map(body, mesh=mesh, in_specs=in_specs, out_specs=out_specs, check_vma=False)
```

```python
import functools

import jax
import jax.numpy as jnp
from jax import lax
from jax.experimental import pallas as pl
from jax.experimental.pallas import tpu as pltpu
from jax.sharding import PartitionSpec as P

LEARN_RATE = 0.25
CONSENSUS = 0.5
MIX_WEIGHT = 1.0 / 3.0

F32, BF16, I32 = jnp.float32, jnp.bfloat16, jnp.int32
ANY = pl.BlockSpec(memory_space=pl.ANY)
IN_VMEM = pl.BlockSpec(memory_space=pltpu.VMEM)
MIB = 1 << 20


def dot(a, b, dims=((1,), (0,))):
    return lax.dot_general(a, b, (dims, ((), ())), preferred_element_type=F32)


def as_column(row):
    n = row.shape[1]
    eye = lax.broadcasted_iota(I32, (n, n), 0) == lax.broadcasted_iota(I32, (n, n), 1)
    spread = jnp.where(eye, jnp.broadcast_to(row.astype(F32), (n, n)), 0.0)
    return jnp.sum(spread, axis=1, keepdims=True).astype(I32)


def split(rows):
    high = rows.astype(BF16)
    return jnp.concatenate([high, (rows - high.astype(F32)).astype(BF16)], axis=0)


def pick(choice, rows):
    return dot(jnp.concatenate([choice, choice], axis=1), rows)


def onehot(mask):
    return jnp.where(mask, 1.0, 0.0).astype(BF16)


def divide(value, by):
    return (value * ((1 << 16) // by + 1)) >> 16


TILE = 128


def owner_tiles(shards, width_out):
    rows = width_out // shards
    return max(-(-(owner + 1) * rows // TILE) - owner * rows // TILE for owner in range(shards))


def first_tile(me, shards, width_out):
    last = width_out // TILE - owner_tiles(shards, width_out)
    return jnp.minimum(lax.div(me * (width_out // shards), TILE), last)


def rows_kernel(shards, silos, own_blocks, per_row, scale, lists, counts, g_lists, g_counts, act, cot, err, *refs):
    grad_rows, err_rows = refs[:2]
    (act_v, cot_v, own_match, match, kept_hot, own_hot, spread, row_table, g_table,
     list_s, count_s, gc_s, lists_v, g_v, sems) = refs[2:]
    me = lax.axis_index("shard")
    silo = lax.axis_index("silo")
    slots = lists_v.shape[2]
    g_slots = g_v.shape[2]
    width = err_rows.shape[1]
    parts = 4
    depth = act_v.shape[0] // parts
    small = [
        pltpu.make_async_copy(lists.at[0, me], list_s, sems.at[0]),
        pltpu.make_async_copy(lists.at[0], lists_v, sems.at[1]),
        pltpu.make_async_copy(counts.at[0], count_s, sems.at[2]),
        pltpu.make_async_copy(g_lists, g_v, sems.at[3]),
        pltpu.make_async_copy(g_counts, gc_s, sems.at[4]),
    ]
    cot_copy = pltpu.make_async_copy(cot, cot_v, sems.at[5])
    act_copies = [
        pltpu.make_async_copy(act.at[rows], act_v.at[rows], sems.at[6 + part])
        for part, rows in enumerate(pl.ds(part * depth, depth) for part in range(parts))
    ]
    for copy in [*small, cot_copy, *act_copies]:
        copy.start()
    small[0].wait()
    columns, fills = [], []
    for shift in range(1, shards):
        owner = lax.rem(me + shift, shards)

        def fetch(slot, carry, owner=owner, shift=shift):
            block = owner * own_blocks + list_s[owner, slot]
            into = err_rows.at[pl.ds((shift - 1) * slots + slot, 1)]
            pltpu.make_async_copy(err.at[0, 0, pl.ds(block, 1)], into, sems.at[0]).start()
            return carry

        lax.fori_loop(0, slots, fetch, 0, unroll=slots)
    for copy in small[1:]:
        copy.wait()
    for shift in range(1, shards):
        owner = lax.rem(me + shift, shards)
        row = lists_v[me, pl.ds(owner, 1), :] + owner * own_blocks
        columns.append(as_column(row))
        slot_ids = lax.broadcasted_iota(I32, (slots, 1), 0)
        fills.append(slot_ids < count_s[me, owner])
    blocks = jnp.concatenate(columns, axis=0)
    filled = jnp.concatenate(fills, axis=0)
    out_row = divide(blocks, per_row)
    segment = blocks - out_row * per_row
    total = blocks.shape[0]
    chosen = onehot(lax.broadcasted_iota(I32, (total, cot_v.shape[1]), 1) == out_row)

    senders = [lists_v[lax.rem(me - shift + shards, shards), pl.ds(me, 1), :] for shift in range(shards)]
    gossiped = as_column(g_v[silo])
    sent = lax.broadcasted_iota(I32, (g_slots, 1), 0) < gc_s[silo]
    for shift, ids in enumerate(senders):
        same = onehot((gossiped == jnp.concatenate([ids, ids], axis=1)) & sent)
        if shift:
            match[:, 2 * (shift - 1) * slots : 2 * shift * slots] = same
        else:
            own_match[...] = same
    nblocks = shards * own_blocks
    step = TILE * per_row
    own_span = owner_tiles(shards, cot_v.shape[1]) * step
    start = first_tile(me, shards, cot_v.shape[1]) * step
    slot_ids = lax.broadcasted_iota(I32, (1, slots), 1)
    for owner in range(shards):
        place = lists_v[me, owner : owner + 1, :] + (owner * own_blocks - start)
        place = jnp.where(place < 0, place + nblocks, place)
        keep = slot_ids < count_s[me, owner]
        row_table[owner : owner + 1, :] = jnp.where(keep & (place < own_span), place, nblocks)
        row_table[shards + owner : shards + owner + 1, :] = jnp.where(
            keep & (place >= own_span), place - own_span, nblocks - own_span
        )
    place = lists_v[me, pl.ds(me, 1), :] + (me * own_blocks - start)
    row_table[2 * shards : 2 * shards + 1, :] = jnp.where(slot_ids < count_s[me, me], place, nblocks)
    out_rows = own_blocks // per_row
    chunks = per_row * width // 128
    row = divide(g_v[silo], per_row)
    place = (g_v[silo] - row * per_row) * (width // 128 * out_rows) + row
    sent_row = lax.broadcasted_iota(I32, (1, g_slots), 1) < gc_s[silo]
    g_table[...] = jnp.where(sent_row, place, chunks * out_rows)
    first, second = neighbours(silo, silos)
    for ids, into in (
        (jnp.concatenate(senders, axis=1), kept_hot),
        (jnp.where(sent_row, g_v[silo], -1), own_hot),
        (jnp.concatenate([g_v[first], g_v[second]], axis=1), spread),
    ):
        for part in range(per_row):
            here = lax.broadcasted_iota(I32, (out_rows, ids.shape[1]), 0) * per_row + part
            into[part * out_rows : (part + 1) * out_rows, :] = onehot(here == ids)

    cot_copy.wait()
    picked = dot(chosen, cot_v[...], ((1,), (1,))).astype(BF16)
    acc = jnp.zeros((total, act_v.shape[1]), F32)
    for part, copy in enumerate(act_copies):
        copy.wait()
        acc = acc + dot(picked[:, part * depth : (part + 1) * depth], act_v[part * depth : (part + 1) * depth, :])
    grad = jnp.zeros((total, width), F32)
    for part in range(per_row):
        grad = jnp.where(segment == part, acc[:, part * width : (part + 1) * width], grad)
    grad_rows[...] = jnp.where(filled, grad * scale, 0.0)
    pltpu.make_async_copy(err_rows, err_rows, sems.at[0]).wait()
    err_rows[...] = jnp.where(filled, err_rows[...], 0.0)


def moving_rows(shards, silos, own_blocks, per_row, scale, lists, counts, g_lists, g_counts, act, cot, err):
    slots = lists.shape[3]
    g_slots = g_lists.shape[2]
    width = err.shape[3]
    return pl.pallas_call(
        functools.partial(rows_kernel, shards, silos, own_blocks, per_row, scale),
        name="moving_rows",
        in_specs=[ANY] * 7,
        out_specs=[IN_VMEM] * 11,
        out_shape=[pltpu.VMEM(((shards - 1) * slots, width), F32)] * 2
        + [
            pltpu.VMEM(act.shape, BF16),
            pltpu.VMEM(cot.shape, BF16),
            pltpu.VMEM((g_slots, 2 * slots), BF16),
            pltpu.VMEM((g_slots, 2 * (shards - 1) * slots), BF16),
            pltpu.VMEM((own_blocks, shards * slots), BF16),
            pltpu.VMEM((own_blocks, g_slots), BF16),
            pltpu.VMEM((own_blocks, 2 * g_slots), BF16),
            pltpu.VMEM((2 * shards + 1, slots), I32),
            pltpu.VMEM((1, g_slots), I32),
        ],
        scratch_shapes=[
            pltpu.SMEM((shards, slots), I32),
            pltpu.SMEM((shards, shards), I32),
            pltpu.SMEM(g_counts.shape, I32),
            pltpu.VMEM(lists.shape[1:], I32),
            pltpu.VMEM(g_lists.shape, I32),
            pltpu.SemaphoreType.DMA((10,)),
        ],
        compiler_params=pltpu.CompilerParams(vmem_limit_bytes=16 * MIB),
    )(lists, counts, g_lists, g_counts, act, cot, err)


def early_tiles(me, silo):
    return jnp.where((me == 0) & (silo < 2), 1, 0)


def tiles_by_then(silo, count, tiles):
    return jnp.where(silo == 1, tiles, count)


def sum_kernel(shards, per_row, scale, grad_rows, err_rows, act_v, cot_v, *outs):
    *outs, grad_v = outs
    me = lax.axis_index("shard")
    start = first_tile(me, shards, cot_v.shape[1])

    def store(place, carry):
        grad = tile_gradient(cot_v, act_v, scale, start + place)
        for where, piece in pieces(grad, place, per_row, grad_v.shape[0]):
            grad_v[where] = piece
        return carry

    lax.fori_loop(0, early_tiles(me, lax.axis_index("silo")), store, 0)
    slots = outs[0].shape[0]
    for place, out in enumerate(outs):
        rows = slice(place * slots, (place + 1) * slots)
        out[...] = err_rows[rows, :] + grad_rows[rows, :]


def outgoing_rows(shards, per_row, scale, grad_rows, err_rows, act_v, cot_v):
    shape = (grad_rows.shape[0] // (shards - 1), grad_rows.shape[1])
    return pl.pallas_call(
        functools.partial(sum_kernel, shards, per_row, scale),
        name="outgoing_rows",
        in_specs=[IN_VMEM] * 4,
        out_specs=[IN_VMEM] * shards,
        out_shape=[pltpu.VMEM(shape, F32)] * (shards - 1)
        + [pltpu.VMEM((shape[1] // 128, TILE * per_row + 8, 128), F32)],
        compiler_params=pltpu.CompilerParams(vmem_limit_bytes=8 * MIB),
        cost_estimate=pl.CostEstimate(flops=10**10, bytes_accessed=3 * 10**7, transcendentals=0),
    )(grad_rows, err_rows, act_v, cot_v)


def load_memory(err, err_v, tiles, step, into, sems):
    copies = [
        pltpu.make_async_copy(
            err.at[0, 0, pl.ds(pl.multiple_of(tile * step, 8), step), pl.ds(half * 128, 128)],
            err_v.at[half, pl.ds(place * step, step)],
            sems[half],
        )
        for place, tile in enumerate(tiles, into)
        for half in range(err_v.shape[0])
    ]
    for copy in copies:
        copy.start()
    return copies


def tile_gradient(cot_v, act_v, scale, tile):
    columns = pl.ds(pl.multiple_of(tile * TILE, TILE), TILE)
    return dot(cot_v[:, columns], act_v[...], ((0,), (0,))) * scale


def pieces(grad, place, per_row, halves):
    for seg in range(per_row):
        for half in range(halves):
            lane = (seg * halves + half) * 128
            where = pl.ds(place * TILE * per_row + seg, TILE, stride=per_row)
            yield (half, where, slice(None)), grad[:, lane : lane + 128]


def clear_rows(err_v, table_s, first, shards):
    for owner in range(first, first + shards):

        def clear(slot, carry, owner=owner):
            block = table_s[owner, slot]
            for half in range(err_v.shape[0]):
                err_v[half, pl.ds(block, 1), :] = jnp.zeros((1, 128), F32)
            return carry

        lax.fori_loop(0, table_s.shape[1], clear, 0, unroll=table_s.shape[1])


def gradient_kernel(
    shards, per_row, scale,
    err, params, e_v, own_match, act_v, cot_v, row_table, g_table, early_v,
    mine, base, err_v, p_v, grad_v, table_s, g_s, rows_v, drift_v, sems,
):
    me = lax.axis_index("shard")
    slots = mine.shape[0]
    g_slots = base.shape[0]
    halves = err_v.shape[0]
    out_rows = e_v.shape[1]
    chunks = e_v.shape[2] // 128
    step = TILE * per_row
    tiles = cot_v.shape[1] // TILE
    count = owner_tiles(shards, cot_v.shape[1])
    start = first_tile(me, shards, cot_v.shape[1])
    small = [
        pltpu.make_async_copy(row_table, table_s, sems.at[0]),
        pltpu.make_async_copy(g_table, g_s, sems.at[1]),
    ]
    for copy in small:
        copy.start()

    def load(places, sem):
        order = [lax.rem(start + place, tiles) for place in places]
        return load_memory(err, err_v, order, step, places[0], [sems.at[sem + half] for half in range(halves)])

    own_memory = load(range(count), 3)
    p_copy = pltpu.make_async_copy(params, p_v, sems.at[2])
    p_copy.start()
    other_memory = load(range(count, tiles), 3 + halves)

    def store(place, carry):
        grad = tile_gradient(cot_v, act_v, scale, lax.rem(start + place, tiles))
        for where, piece in pieces(grad, place, per_row, halves):
            grad_v[where] = piece
        return carry

    silo = lax.axis_index("silo")
    lax.fori_loop(early_tiles(me, silo), tiles_by_then(silo, count, tiles), store, 0)
    for copy in small + own_memory:
        copy.wait()
    done = count * step

    @pl.when(early_tiles(me, silo) > 0)
    def _():
        for half in range(halves):
            err_v[half, :step, :] = err_v[half, :step, :] + early_v[half, :step, :]

    @pl.when(early_tiles(me, silo) == 0)
    def _():
        for half in range(halves):
            err_v[half, :step, :] = err_v[half, :step, :] + grad_v[half, :step, :]

    for half in range(halves):
        err_v[half, step:done, :] = err_v[half, step:done, :] + grad_v[half, step:done, :]
        err_v[half, tiles * step :, :] = jnp.zeros((8, 128), F32)

    def take(slot, carry):
        for half in range(halves):
            rows_v[half, pl.ds(slot, 1), :] = err_v[half, pl.ds(table_s[2 * shards, slot], 1), :]
        return carry

    lax.fori_loop(0, slots, take, 0, unroll=slots)
    mine[...] = jnp.concatenate([rows_v[half, :slots] for half in range(halves)], axis=1)
    clear_rows(err_v, table_s, 0, shards)
    p_copy.wait()
    for chunk in range(chunks):
        lanes = slice(chunk * 128, (chunk + 1) * 128)
        drift_v[chunk * out_rows : (chunk + 1) * out_rows, :] = p_v[0, :, lanes] - e_v[0, :, lanes]
    for half in range(halves):
        nothing = (chunks + half) * out_rows
        drift_v[nothing : nothing + 8, :] = jnp.zeros((8, 128), F32)

    def gather(slot, carry):
        for half in range(halves):
            rows_v[half, pl.ds(slot, 1), :] = drift_v[pl.ds(g_s[0, slot] + half * out_rows, 1), :]
        return carry

    lax.fori_loop(0, g_slots, gather, 0, unroll=g_slots)
    rows = jnp.concatenate([rows_v[half, :g_slots] for half in range(halves)], axis=1)
    base[...] = rows - LEARN_RATE * dot(own_match[...], split(mine[...]))
    for copy in other_memory:
        copy.wait()


def gradient(shards, per_row, scale, err, params, estimate, own_match, act_v, cot_v, row_table, g_table, early_v):
    slots = row_table.shape[1]
    g_slots = own_match.shape[0]
    nblocks, width = err.shape[2:]
    halves = width // 128
    chunks = params.shape[2] // 128
    return pl.pallas_call(
        functools.partial(gradient_kernel, shards, per_row, scale),
        name="gradient",
        in_specs=[ANY] * 2 + [IN_VMEM] * 7,
        out_specs=[IN_VMEM] * 5,
        out_shape=[
            pltpu.VMEM((slots, width), F32),
            pltpu.VMEM((g_slots, width), F32),
            pltpu.VMEM((halves, nblocks + 8, 128), F32),
            pltpu.VMEM(params.shape, F32),
            pltpu.VMEM((halves, nblocks + 8, 128), F32),
        ],
        scratch_shapes=[
            pltpu.SMEM(row_table.shape, I32),
            pltpu.SMEM(g_table.shape, I32),
            pltpu.VMEM((halves, max(slots, g_slots), 128), F32),
            pltpu.VMEM(((chunks + halves - 1) * params.shape[1] + 8, 128), F32),
            pltpu.SemaphoreType.DMA((3 + 2 * halves,)),
        ],
        compiler_params=pltpu.CompilerParams(vmem_limit_bytes=16 * MIB),
    )(err, params, estimate, own_match, act_v, cot_v, row_table, g_table, early_v)


def delta_kernel(base, match, *refs):
    *arrived, out, again = refs
    rows = jnp.concatenate([split(each[...]) for each in arrived], axis=0)
    total = base[...] - LEARN_RATE * dot(match[...], rows)
    out[: total.shape[0]] = total
    out[total.shape[0] :] = jnp.zeros((8, total.shape[1]), F32)
    again[...] = total


def delta_rows(base, match, arrived):
    return pl.pallas_call(
        delta_kernel,
        name="delta_rows",
        in_specs=[IN_VMEM] * (2 + len(arrived)),
        out_specs=[IN_VMEM] * 2,
        out_shape=[pltpu.VMEM((base.shape[0] + 8, base.shape[1]), F32), pltpu.VMEM(base.shape, F32)],
        cost_estimate=pl.CostEstimate(flops=10**10, bytes_accessed=3 * 10**7, transcendentals=0),
        compiler_params=pltpu.CompilerParams(vmem_limit_bytes=8 * MIB),
    )(base, match, *arrived)


def own_kernel(
    shards, per_row, scale,
    p_v, e_v, m_v, err_v, grad_v, act_v, cot_v, row_table, kept_hot, own_hot, _, *refs
):
    kept = refs[:shards]
    err_out, est_out, mixed_pre, params_pre, table_s, rest_v, est_v, sems = refs[shards:]
    me = lax.axis_index("shard")
    width = kept[0].shape[1]
    halves = err_v.shape[0]
    out_rows = p_v.shape[1]
    step = TILE * per_row
    tiles = cot_v.shape[1] // TILE
    count = owner_tiles(shards, cot_v.shape[1])
    start = first_tile(me, shards, cot_v.shape[1])
    small = pltpu.make_async_copy(row_table, table_s, sems.at[0])
    small.start()
    copies = []

    def store_memory(source, first, places):
        for place in places:
            tile = lax.rem(start + place, tiles)
            for half in range(halves):
                copy = pltpu.make_async_copy(
                    source.at[half, pl.ds((place - first) * step, step)],
                    err_out.at[0, 0, pl.ds(pl.multiple_of(tile * step, 8), step), pl.ds(half * 128, 128)],
                    sems.at[1 + half],
                )
                copy.start()
                copies.append(copy)

    store_memory(err_v, 0, range(count))

    def store(place, carry):
        grad = tile_gradient(cot_v, act_v, scale, lax.rem(start + count + place, tiles))
        held = pieces(grad, count + place, per_row, halves)
        for (where, piece), (there, _) in zip(pieces(grad, place, per_row, halves), held):
            rest_v[where] = err_v[there] + piece
        return carry

    by_then = tiles_by_then(lax.axis_index("silo"), count, tiles)

    @pl.when(by_then == tiles)
    def _():
        for half in range(halves):
            rows = slice(count * step, tiles * step)
            rest_v[half, : (tiles - count) * step, :] = err_v[half, rows, :] + grad_v[half, rows, :]

    lax.fori_loop(0, tiles - by_then, store, 0)
    small.wait()
    clear_rows(rest_v, table_s, shards, shards)
    store_memory(rest_v, count, range(count, tiles))

    kept_parts = split(jnp.concatenate([rows[...] for rows in kept], axis=0))
    ones = jnp.ones((own_hot.shape[1], width), BF16)
    for part in range(per_row):
        lanes = slice(part * width, (part + 1) * width)
        blocks = slice(part * out_rows, (part + 1) * out_rows)
        grad = pick(kept_hot[blocks, :], kept_parts)
        half_step = p_v[0, :, lanes] - LEARN_RATE * grad
        gossiped = dot(own_hot[blocks, :], ones) > 0.0
        change = jnp.where(gossiped, half_step - e_v[0, :, lanes], 0.0)
        est = e_v[0, :, lanes] + change
        mix = m_v[0, :, lanes] + MIX_WEIGHT * change
        est_v[:, lanes] = est
        copy = pltpu.make_async_copy(est_v.at[:, lanes], est_out.at[0, :, lanes], sems.at[1 + halves + part])
        copy.start()
        copies.append(copy)
        mixed_pre[:, lanes] = mix
        params_pre[:, lanes] = half_step + CONSENSUS * (mix - est)
    for copy in copies:
        copy.wait()


def own_updates(
    shards, per_row, scale, err_shape, params, estimate, mixed, err_v, grad_v, act_v, cot_v, row_table, kept_hot, own_hot, delta, kept
):
    owned = mixed.shape[1:]
    halves = err_v.shape[0]
    others = cot_v.shape[1] // TILE - owner_tiles(shards, cot_v.shape[1])
    return pl.pallas_call(
        functools.partial(own_kernel, shards, per_row, scale),
        name="own_updates",
        in_specs=[IN_VMEM] * (11 + shards),
        out_specs=[ANY, ANY, IN_VMEM, IN_VMEM],
        out_shape=[
            pltpu.HBM(err_shape, F32),
            pltpu.HBM(mixed.shape, F32),
            pltpu.VMEM(owned, F32),
            pltpu.VMEM(owned, F32),
        ],
        scratch_shapes=[
            pltpu.SMEM(row_table.shape, I32),
            pltpu.VMEM((halves, others * TILE * per_row + 8, 128), F32),
            pltpu.VMEM(owned, F32),
            pltpu.SemaphoreType.DMA((1 + halves + per_row,)),
        ],
        compiler_params=pltpu.CompilerParams(vmem_limit_bytes=16 * MIB),
    )(params, estimate, mixed, err_v, grad_v, act_v, cot_v, row_table, kept_hot, own_hot, delta, *kept)


def final_kernel(per_row, mixed_pre, params_pre, spread, first, second, mixed_out, params_out, m_v, p_v, sems):
    out_rows = m_v.shape[0]
    width = m_v.shape[1] // per_row
    slots = second.shape[0]
    rows = split(jnp.concatenate([first[:slots, :], second[...]], axis=0))
    depth = spread.shape[1]
    copies = []
    for part in range(per_row):
        lanes = slice(part * width, (part + 1) * width)
        choice = spread[part * out_rows : (part + 1) * out_rows, :]
        change = dot(choice, rows[:depth]) + dot(choice, rows[depth:])
        m_v[:, lanes] = mixed_pre[:, lanes] + MIX_WEIGHT * change
        p_v[:, lanes] = params_pre[:, lanes] + (CONSENSUS * MIX_WEIGHT) * change
        pair = [
            pltpu.make_async_copy(m_v.at[:, lanes], mixed_out.at[0, :, lanes], sems.at[2 * part]),
            pltpu.make_async_copy(p_v.at[:, lanes], params_out.at[0, :, lanes], sems.at[2 * part + 1]),
        ]
        for copy in pair:
            copy.start()
        copies += pair
    for copy in copies:
        copy.wait()


def final(per_row, shape, mixed_pre, params_pre, spread, first, second):
    return pl.pallas_call(
        functools.partial(final_kernel, per_row),
        name="neighbours",
        in_specs=[IN_VMEM] * 5,
        out_specs=[ANY] * 2,
        out_shape=[pltpu.HBM(shape, F32)] * 2,
        scratch_shapes=[
            pltpu.VMEM(mixed_pre.shape, F32),
            pltpu.VMEM(mixed_pre.shape, F32),
            pltpu.SemaphoreType.DMA((2 * per_row,)),
        ],
        compiler_params=pltpu.CompilerParams(vmem_limit_bytes=20 * MIB),
    )(mixed_pre, params_pre, spread, first, second)


def neighbours(silo, silos):
    lower, upper = lax.rem(silo + silos - 1, silos), lax.rem(silo + 1, silos)
    if silos % 2:
        return lower, upper
    even = lax.rem(silo, 2) == 0
    return jnp.where(even, lower, upper), jnp.where(even, upper, lower)


def exchange(rows, again, silos):
    if silos % 2:
        routes = [[(a, (a + 1) % silos) for a in range(silos)], [(a, (a - 1) % silos) for a in range(silos)]]
    else:
        routes = [
            [(a, (a + 1 if a % 2 else a - 1) % silos) for a in range(silos)],
            [(a, a ^ 1) for a in range(silos)],
        ]
    far = lax.ppermute(rows, "silo", routes[0])
    near = lax.ppermute(again, "silo", routes[1])
    return far, near


def body(
    activ, cotangent, error_memory, params, estimate, mixed,
    kept_blocks, kept_counts, gossip_blocks, gossip_counts,
):
    shards = lax.axis_size("shard")
    silos = lax.axis_size("silo")
    nblocks, block_len = error_memory.shape[2:]
    own_blocks = nblocks // shards
    per_row = activ.shape[1] // block_len
    scale = activ.shape[1] ** (-0.5)
    activ, cotangent, error_memory, params, kept_blocks, kept_counts, gossip_blocks, gossip_counts = (
        pltpu.with_memory_space_constraint(array, pltpu.HBM)
        for array in (
            activ, cotangent, error_memory, params,
            kept_blocks, kept_counts, gossip_blocks, gossip_counts.reshape(silos),
        )
    )
    grad_rows, err_rows, act_v, cot_v, own_match, match, kept_hot, own_hot, spread, row_table, g_table = moving_rows(
        shards, silos, own_blocks, per_row, scale,
        kept_blocks, kept_counts, gossip_blocks, gossip_counts, activ, cotangent, error_memory,
    )
    *outgoing, early_v = outgoing_rows(shards, per_row, scale, grad_rows, err_rows, act_v, cot_v)
    arrived = [
        lax.ppermute(rows, "shard", [(r, (r + shift) % shards) for r in range(shards)])
        for shift, rows in enumerate(outgoing, 1)
    ]
    estimate, mixed = (pltpu.with_memory_space_constraint(array, pltpu.VMEM) for array in (estimate, mixed))
    mine, base, err_v, params, grad_v = gradient(
        shards, per_row, scale, error_memory, params, estimate, own_match, act_v, cot_v, row_table, g_table, early_v
    )
    delta, again = delta_rows(base, match, arrived)
    first, second = exchange(delta, again, silos)
    error_out, estimate_out, mixed_pre, params_pre = own_updates(
        shards, per_row, scale, error_memory.shape, params, estimate, mixed,
        err_v, grad_v, act_v, cot_v, row_table, kept_hot, own_hot, again, [mine, *arrived],
    )
    mixed_out, params_out = final(per_row, mixed.shape, mixed_pre, params_pre, spread, first, second)
    return params_out, estimate_out, mixed_out, error_out


def solution(mesh):
    in_specs = (
        P(("silo", "shard"), None),
        P(("silo", "shard"), None),
        P("silo", "shard", None, None),
        P("silo", "shard", None),
        P("silo", "shard", None),
        P("silo", "shard", None),
        P("silo", None, None, None),
        P("silo", None, None),
        P(None, "shard", None),
        P(None, "shard"),
    )
    out_specs = (
        P("silo", "shard", None),
        P("silo", "shard", None),
        P("silo", "shard", None),
        P("silo", "shard", None, None),
    )
    return jax.shard_map(body, mesh=mesh, in_specs=in_specs, out_specs=out_specs, check_vma=False)
```
